32 devices in a mesh: fsdp: 16 (over z, y, core), dp: 2 (over x).
Axes of the slice: x: 2, y: 2, z: 4, core: 2. Of those that a mesh axis runs over, the one named last changes fastest.
Arguments:
- tokens: bfloat16 [12288, 768], P(('fsdp', 'dp')), may hold values from -6 to 6
- memory: bfloat16 [24576, 768], P(('fsdp', 'dp')), may hold values from -6 to 6
- out_grad: bfloat16 [12288, 768], P(('fsdp', 'dp')), may hold values from -6 to 6
- target_len: int32 [32, 6], P(('fsdp', 'dp')), may hold values from 1 to 128, 384 in all within a row
- source_len: int32 [32, 6], P(('fsdp', 'dp')), may hold values from 1 to 512, 768 in all within a row
- task_ids: int32 [32, 6], P(('fsdp', 'dp')), may hold values from 0 to 7
- norm_gains: bfloat16 [3, 768], P(None, 'fsdp'), may hold values from 0.25 to 1.75
- self_qkv: bfloat16 [768, 2304], P('fsdp'), may hold values from -0.21875 to 0.21875
- self_out: bfloat16 [768, 768], P('fsdp'), may hold values from -0.625 to 0.625
- cross_query: bfloat16 [768, 768], P('fsdp'), may hold values from -0.21875 to 0.21875
- cross_keyval: bfloat16 [768, 1536], P('fsdp'), may hold values from -0.21875 to 0.21875
- cross_out: bfloat16 [768, 768], P('fsdp'), may hold values from -0.875 to 0.875
- feed_in: bfloat16 [768, 3072], P('fsdp'), may hold values from -0.21875 to 0.21875
- feed_out: bfloat16 [3072, 768], P('fsdp'), may hold values from -0.109375 to 0.109375
- task_table: bfloat16 [8, 64], P(None, 'fsdp'), may hold values from -5 to 5
- hyper_in: bfloat16 [64, 128], P(None, 'fsdp'), may hold values from -0.75 to 0.75
- maker_down: bfloat16 [128, 55296], P(None, 'fsdp'), may hold values from -0.03125 to 0.03125
- maker_up: bfloat16 [128, 55296], P(None, 'fsdp'), may hold values from -0.15625 to 0.15625
- maker_norm: bfloat16 [128, 2304], P(None, 'fsdp'), may hold values from -0.1875 to 0.1875
Outputs:
- block_out: bfloat16 [12288, 768], P(('fsdp', 'dp'))
- grad_tokens: float32 [12288, 768], P(('fsdp', 'dp'))
- grad_memory: float32 [24576, 768], P(('fsdp', 'dp'))
- grad_norm_gains: float32 [3, 768], P(None, 'fsdp')
- grad_self_qkv: float32 [768, 2304], P('fsdp')
- grad_self_out: float32 [768, 768], P('fsdp')
- grad_cross_query: float32 [768, 768], P('fsdp')
- grad_cross_keyval: float32 [768, 1536], P('fsdp')
- grad_cross_out: float32 [768, 768], P('fsdp')
- grad_feed_in: float32 [768, 3072], P('fsdp')
- grad_feed_out: float32 [3072, 768], P('fsdp')
- grad_task_table: float32 [8, 64], P(None, 'fsdp')
- grad_hyper_in: float32 [64, 128], P(None, 'fsdp')
- grad_maker_down: float32 [128, 55296], P(None, 'fsdp')
- grad_maker_up: float32 [128, 55296], P(None, 'fsdp')
- grad_maker_norm: float32 [128, 2304], P(None, 'fsdp')
The draws below stay inside these ranges and needn't reach their ends.
Inputs may be any that keep to these rules, and one draw needn't show every extreme that they name: `target_len`: row g lists the target lengths of the 6 sequences of group g; they sum to 384, and some entry of every row is 128. `source_len`: row g lists the memory lengths of the 6 sequences of group g; they sum to 768, and some entry of every row is 512.
All inputs are finite; a program needn't handle non-finite values.
Results may differ from the reference program's by a relative error of at most 0.035.
Values may be sent and summed in bfloat16 or wider, within the bound.
No kernel may reach another device: no remote copies, remote signals or barrier semaphores. Data moves between devices by JAX's collectives and lax.ppermute only.
A program may use at most 320 MiB of HBM per device.

```python
import math
from functools import partial
import jax
import jax.numpy as jnp
import numpy as np
from jax import lax

D = 768
HEADS = 12
HEAD_DIM = 64
FF = 3072
ADAPT = 24
EMBED = 64
HYPER = 128
NTASK = 8
TGT_MAX = 128
ENC_MAX = 512
TOK_DEV = 384
SEQ_DEV = 6
MEM_DEV = 768
TOKENS = 12288
MEMROWS = 24576
DEVICES = 32


def set_ends(array, key, smallest, high):
    dims = array.shape
    place = [jax.random.randint(jax.random.fold_in(key, axis), (), 0, dims[axis]) for axis in range(len(dims))]
    array = array.at[tuple(place)].set(smallest)
    longest = dims.index(max(dims))
    place[longest] = (place[longest] + 1) % dims[longest]
    return array.at[tuple(place)].set(high)


def steps_of(own_key, shape, cuts, low, high):
    def one(position, parts):
        heights = jax.random.uniform(jax.random.fold_in(jax.random.fold_in(own_key, 6), position), (parts,), jnp.float32, low / len(cuts), high / len(cuts))
        return jnp.repeat(jnp.exp(heights), shape[position] // parts).reshape((-1,) + (1,) * (len(shape) - position - 1))

    factor_of = one(*cuts[0])
    for cut in cuts[1:]:
        factor_of = factor_of * one(*cut)
    return factor_of


def length_profile(amount, total, reach, lean):
    loads = [(1 << 20) // math.isqrt(rank ** lean) + 1 for rank in range(2, amount + 1)]
    surplus, holding = total - reach - (amount - 1), [1] * (amount - 1)
    while surplus > 0:
        candidates = [i for i in range(amount - 1) if holding[i] < reach]
        pool, budget = sum([loads[i] for i in candidates]), surplus
        for i in candidates:
            extra = min(reach - holding[i], max(1, budget * loads[i] // pool), surplus)
            holding[i] = holding[i] + extra
            surplus = surplus - extra
    return np.array([reach] + holding)


def ragged_sizes(key, amount, total, limit, skew):
    if amount == 2:
        one = jax.random.randint(key, (), max(1, total - limit), min(limit, total - 1) + 1)
        return jnp.stack([one, total - one])
    sizes = jnp.asarray(length_profile(amount, total, limit, skew), jnp.int32)
    pairs = (amount - 1) // 2
    giver, receiver = sizes[1:1 + 2 * pairs:2], sizes[2:2 + 2 * pairs:2]
    margin = jnp.minimum(giver - 1, limit - receiver)
    passed = jax.random.randint(jax.random.fold_in(key, 1), (pairs,), 0, 1 << 20) % (margin + 1)
    sizes = sizes.at[1:1 + 2 * pairs:2].set(giver - passed).at[2:2 + 2 * pairs:2].set(receiver + passed)
    return sizes[jax.random.permutation(jax.random.fold_in(key, 2), amount)]


def bell_draw(own_key, extent, scale, limit, cuts=(), held_as=jnp.bfloat16):
    values = scale * jax.random.normal(own_key, extent, jnp.float32)
    if cuts:
        values = values * steps_of(own_key, extent, cuts, -0.22, 0.18)
    return jnp.clip(values, -limit, limit).astype(held_as)


def setup_inputs(seed: int = 0) -> dict:
    key_list = jax.random.split(jax.random.key(seed), 20)
    tokens = bell_draw(key_list[0], (TOKENS, D), 1.0, 6.0, ((0, 32),))
    memory = bell_draw(key_list[1], (MEMROWS, D), 1.0, 6.0, ((0, 32),))
    out_grad = bell_draw(key_list[2], (TOKENS, D), 1.0, 6.0, ((0, 32),))
    target_len = jax.vmap(lambda own: ragged_sizes(own, SEQ_DEV, TOK_DEV, TGT_MAX, 2))(jax.random.split(key_list[3], DEVICES)).reshape((DEVICES, SEQ_DEV)).astype(jnp.int32)
    source_len = jax.vmap(lambda own: ragged_sizes(own, SEQ_DEV, MEM_DEV, ENC_MAX, 3))(jax.random.split(key_list[4], DEVICES)).reshape((DEVICES, SEQ_DEV)).astype(jnp.int32)
    task_ids = set_ends(jax.random.randint(key_list[5], (DEVICES, SEQ_DEV), 0, NTASK), jax.random.fold_in(key_list[5], 1), 0, NTASK - 1).astype(jnp.int32)
    norm_gains = jnp.clip(1.0 + 0.15 * jax.random.normal(key_list[6], (3, D), jnp.float32), 0.25, 1.75).astype(jnp.bfloat16)
    self_qkv = bell_draw(key_list[7], (D, 3 * D), D ** -0.5, 0.21875, ((0, 16),))
    self_out = bell_draw(key_list[8], (D, D), (D // 8) ** -0.5, 0.625, ((0, 16),))
    cross_query = bell_draw(key_list[9], (D, D), D ** -0.5, 0.21875, ((0, 16),))
    cross_keyval = bell_draw(key_list[10], (D, 2 * D), D ** -0.5, 0.21875, ((0, 16),))
    cross_out = bell_draw(key_list[11], (D, D), (D // 16) ** -0.5, 0.875, ((0, 16),))
    feed_in = bell_draw(key_list[12], (D, FF), D ** -0.5, 0.21875, ((0, 16),))
    feed_out = bell_draw(key_list[13], (FF, D), FF ** -0.5, 0.109375, ((0, 16),))
    task_table = bell_draw(key_list[14], (NTASK, EMBED), 1.0, 5.0, ((1, 16),))
    hyper_in = bell_draw(key_list[15], (EMBED, HYPER), EMBED ** -0.5, 0.75, ((1, 16),))
    maker_down = bell_draw(key_list[16], (HYPER, 3 * D * ADAPT), (HYPER * D // 3) ** -0.5, 0.03125, ((1, 16),))
    maker_up = bell_draw(key_list[17], (HYPER, 3 * D * ADAPT), (HYPER * 12) ** -0.5, 0.15625, ((1, 16),))
    maker_norm = bell_draw(key_list[18], (HYPER, 3 * D), (HYPER * 8) ** -0.5, 0.1875, ((1, 16),))
    return dict(tokens=tokens, memory=memory, out_grad=out_grad, target_len=target_len, source_len=source_len, task_ids=task_ids, norm_gains=norm_gains, self_qkv=self_qkv, self_out=self_out, cross_query=cross_query, cross_keyval=cross_keyval, cross_out=cross_out, feed_in=feed_in, feed_out=feed_out, task_table=task_table, hyper_in=hyper_in, maker_down=maker_down, maker_up=maker_up, maker_norm=maker_norm)


norm_epsilon = 1e-06
masked_score = -1000000000.0
highest = lax.Precision.HIGHEST

@jax.custom_vjp
def low(v):
    return lax.optimization_barrier(v.astype(jnp.bfloat16)).astype(jnp.float32)

@jax.custom_vjp
def low_back(v):
    return v

def low_keep(v):
    return (low(v), None)

def low_pass(kept, grad):
    return (grad,)

def back_keep(v):
    return (v, None)

def back_low(kept, grad):
    return (low(grad),)
low.defvjp(low_keep, low_pass)
low_back.defvjp(back_keep, back_low)

def product(left, right):
    return jnp.dot(left, right, precision=highest)

def rms_scale(values, gain):
    return values * lax.rsqrt(lax.optimization_barrier(jnp.mean(values * values, axis=-1, keepdims=True)) + norm_epsilon) * gain

def segment_rows(lengths, count):
    ends = jnp.cumsum(lengths).astype(jnp.int32)
    places = jnp.arange(count, dtype=jnp.int32)
    return lax.optimization_barrier(jnp.sum((places[:, None] >= ends[None, :]).astype(jnp.int32), axis=1)).astype(jnp.int32)

def attend(queries, keys, values, allowed):
    rows = queries.shape[0]
    query_heads = queries.reshape(rows, HEADS, HEAD_DIM)
    key_heads = keys.reshape(keys.shape[0], HEADS, HEAD_DIM)
    value_heads = values.reshape(values.shape[0], HEADS, HEAD_DIM)
    scores = jnp.einsum('qhd,khd->hqk', query_heads, key_heads, precision=highest) * HEAD_DIM ** (-0.5)
    scores = low_back(jnp.where(allowed[None], scores, masked_score))
    probs = low(jax.nn.softmax(scores, axis=-1))
    mixed = jnp.einsum('hqk,khd->qhd', probs, value_heads, precision=highest)
    return mixed.reshape(rows, HEADS * HEAD_DIM)

def self_block(block):
    queries, keys, values, seg_rows = block
    places = jnp.arange(seg_rows.shape[0], dtype=jnp.int32)
    allowed = (seg_rows[:, None] == seg_rows[None, :]) & (places[:, None] >= places[None, :])
    return attend(queries, keys, values, allowed)

def cross_block(block):
    queries, keys, values, tok_seg, mem_seg = block
    return attend(queries, keys, values, tok_seg[:, None] == mem_seg[None, :])

def adapter(branch, index, made, onehot, widemask):
    made_down, made_up, made_norm = made
    span = D * ADAPT
    down = made_down[:, index * span:(index + 1) * span].reshape(NTASK, D, ADAPT)
    down = jnp.transpose(down, (1, 0, 2)).reshape(D, NTASK * ADAPT)
    up = made_up[:, index * span:(index + 1) * span].reshape(NTASK * ADAPT, D)
    row_gain = product(onehot, made_norm[:, index * D:(index + 1) * D])
    normed = low(rms_scale(branch, row_gain))
    squeezed = low_back(product(normed, down) * widemask)
    lifted = low(jax.nn.gelu(squeezed))
    return branch + low_back(product(lifted, up))

def blocks(values, rows):
    return values.reshape(-1, rows, values.shape[-1])

def forward(floats, tok_seg, mem_seg, onehot, widemask):
    tokens, memory, norm_gains, self_qkv, self_out, cross_query, cross_keyval, cross_out, feed_in, feed_out, task_table, hyper_in, maker_down, maker_up, maker_norm = floats
    hidden = low(jax.nn.silu(product(task_table, hyper_in)))
    made = (low(product(hidden, maker_down)), low(product(hidden, maker_up)), 1.0 + low(product(hidden, maker_norm)))
    normed1 = low(rms_scale(tokens, norm_gains[0]))
    projected = low(low_back(product(normed1, self_qkv)))
    mixed = lax.map(jax.checkpoint(self_block), (blocks(projected[:, :D], TOK_DEV), blocks(projected[:, D:2 * D], TOK_DEV), blocks(projected[:, 2 * D:], TOK_DEV), tok_seg)).reshape(-1, D)
    mixed = low(low_back(mixed))
    stream = tokens + adapter(low_back(product(mixed, self_out)), 0, made, onehot, widemask)
    normed2 = low(rms_scale(stream, norm_gains[1]))
    queries = low(low_back(product(normed2, cross_query)))
    memory_kv = low(low_back(product(memory, cross_keyval)))
    mixed = lax.map(jax.checkpoint(cross_block), (blocks(queries, TOK_DEV), blocks(memory_kv[:, :D], MEM_DEV), blocks(memory_kv[:, D:], MEM_DEV), tok_seg, mem_seg)).reshape(-1, D)
    mixed = low(low_back(mixed))
    stream = stream + adapter(low_back(product(mixed, cross_out)), 1, made, onehot, widemask)
    normed3 = low(rms_scale(stream, norm_gains[2]))
    pre_feed = low_back(product(normed3, feed_in))
    active = low(jax.nn.gelu(pre_feed))
    return stream + adapter(low_back(product(active, feed_out)), 2, made, onehot, widemask)

def reference(tokens, memory, out_grad, target_len, source_len, task_ids, norm_gains, self_qkv, self_out, cross_query, cross_keyval, cross_out, feed_in, feed_out, task_table, hyper_in, maker_down, maker_up, maker_norm):
    tok_seg = jax.vmap(partial(segment_rows, count=TOK_DEV))(target_len)
    mem_seg = jax.vmap(partial(segment_rows, count=MEM_DEV))(source_len)
    row_task = jnp.take_along_axis(task_ids, tok_seg, axis=1).reshape(-1)
    onehot = (row_task[:, None] == jnp.arange(NTASK, dtype=jnp.int32)[None, :]).astype(jnp.float32)
    widemask = jnp.repeat(onehot, ADAPT, axis=1)
    floats = tuple((item.astype(jnp.float32) for item in (tokens, memory, norm_gains, self_qkv, self_out, cross_query, cross_keyval, cross_out, feed_in, feed_out, task_table, hyper_in, maker_down, maker_up, maker_norm)))

    def layer(weights):
        return forward(weights, tok_seg, mem_seg, onehot, widemask)
    output, pull = jax.vjp(layer, floats)
    grads, = pull(out_grad.astype(jnp.float32))
    return (output.astype(jnp.bfloat16), grads[0], grads[1], grads[2], grads[3], grads[4], grads[5], grads[6], grads[7], grads[8], grads[9], grads[10], grads[11], grads[12], grads[13], grads[14])
```

```python
import functools
import math

import jax
import jax.numpy as jnp
from jax import lax
from jax.experimental import pallas as pl
from jax.experimental.pallas import tpu as pltpu
from jax.sharding import PartitionSpec as P

norm_epsilon = 1e-06
masked_score = -1000000000.0
highest = lax.Precision.HIGHEST


def matmul(left, right):
    return jnp.dot(left, right, preferred_element_type=jnp.float32)


def exact_rows(left, right):
    return lax.dot_general(
        left, right, (((0,), (0,)), ((), ())), precision=highest, preferred_element_type=jnp.float32
    )


def exact_cols(left, right):
    return lax.dot_general(
        left, right, (((1,), (1,)), ((), ())), precision=highest, preferred_element_type=jnp.float32
    )


def segment_rows(lengths, count):
    ends = jnp.cumsum(lengths)
    places = jnp.arange(count, dtype=jnp.int32)
    return jnp.sum((places[:, None] >= ends[None, :]).astype(jnp.int32), axis=1)


def dot(left, right):
    return jnp.dot(left, right, preferred_element_type=jnp.float32)


def dot_nt(left, right):
    return lax.dot_general(
        left, right, (((1,), (1,)), ((), ())), preferred_element_type=jnp.float32
    )


def dot_tn(left, right):
    return lax.dot_general(
        left, right, (((0,), (0,)), ((), ())), preferred_element_type=jnp.float32
    )


def rms_rate(values):
    return lax.rsqrt(jnp.mean(values * values, axis=-1, keepdims=True) + norm_epsilon)


def rms_back(values, rate, gain, grad):
    scaled = grad * gain
    inner = jnp.mean(scaled * values, axis=-1, keepdims=True)
    return rate * (scaled - values * (rate * rate * inner)), grad * values * rate


gelu_slope = math.sqrt(2.0 / math.pi)
gelu_cube = 0.044715


def gelu(values):
    inner = gelu_slope * values * (1.0 + gelu_cube * values * values)
    return 0.5 * values * (1.0 + jnp.tanh(inner))


def gelu_back(values):
    square = values * values
    bent = jnp.tanh(gelu_slope * values * (1.0 + gelu_cube * square))
    slope = gelu_slope * (1.0 + 3.0 * gelu_cube * square)
    return 0.5 * (1.0 + bent) + 0.5 * values * (1.0 - bent * bent) * slope


def halves(dtype):
    lane = lax.broadcasted_iota(jnp.int32, (1, 128), 1)
    first = (lane < 64).astype(jnp.float32)
    return first.astype(dtype), (1.0 - first).astype(dtype)


def lanes(start):
    return pl.ds(pl.multiple_of(start, 128), 128)


def attend_forward(queries, keys, values, starts, cap, probs, mixed):
    factor = math.log2(math.e) / 8.0
    marks = halves(jnp.bfloat16)

    def pair(p, _):
        query = queries[:, lanes(starts[0] + p * 128)].T
        key = keys[:, lanes(starts[1] + p * 128)]
        value = values[:, lanes(starts[2] + p * 128)].T
        parts = []
        for head in (0, 1):
            scores = jnp.minimum(dot(key * marks[head], query) * factor, cap[...])
            weights = jnp.exp2(scores - jnp.max(scores, axis=0, keepdims=True))
            weights = weights * (1.0 / jnp.sum(weights, axis=0, keepdims=True))
            weights = weights.astype(jnp.bfloat16)
            probs[2 * p + head] = weights
            parts.append(dot(value[head * 64 : (head + 1) * 64], weights))
        mixed[:, lanes(p * 128)] = jnp.concatenate(parts, axis=0).T.astype(jnp.bfloat16)
        return 0

    lax.fori_loop(0, mixed.shape[1] // 128, pair, 0)


def attend_backward(queries, keys, values, starts, probs, grad_mixed, grads, places):
    marks = halves(jnp.bfloat16)
    first, second = halves(jnp.float32)

    def pair(p, _):
        query = queries[:, lanes(starts[0] + p * 128)]
        key = keys[:, lanes(starts[1] + p * 128)]
        value = values[:, lanes(starts[2] + p * 128)]
        grad = grad_mixed[:, lanes(p * 128)]
        key_turned = key.T
        grad_turned = grad.T
        grad_query, grad_key, grad_value = [], 0.0, 0.0
        for head, mark in ((0, first), (1, second)):
            weights = probs[2 * p + head]
            grad_value += dot(weights, grad) * mark
            wide = weights.astype(jnp.float32)
            product = wide * dot(value * marks[head], grad_turned)
            product = product - wide * jnp.sum(product, axis=0, keepdims=True)
            product = product.astype(jnp.bfloat16)
            grad_key += dot(product, query) * mark
            grad_query.append(dot(key_turned[head * 64 : (head + 1) * 64], product))
        grad_query = jnp.concatenate(grad_query, axis=0).T * 0.125
        grads[0][:, lanes(places[0] + p * 128)] = grad_query.astype(jnp.bfloat16)
        grads[1][:, lanes(places[1] + p * 128)] = (grad_key * 0.125).astype(jnp.bfloat16)
        grads[2][:, lanes(places[2] + p * 128)] = grad_value.astype(jnp.bfloat16)
        return 0

    lax.fori_loop(0, grad_mixed.shape[1] // 128, pair, 0)


def adapter_forward(branch, tasks, cond, down, up, mask):
    gain = 1.0 + dot(tasks[...], cond[...])
    normed = (branch * rms_rate(branch) * gain).astype(jnp.bfloat16)
    squeezed = dot(normed, down[...]) * mask[...].astype(jnp.float32)
    return branch + dot(gelu(squeezed).astype(jnp.bfloat16), up[...]), squeezed


def adapter_backward(branch, squeezed, tasks, cond, down, up, mask, grad, outs):
    low = grad.astype(jnp.bfloat16)
    outs[1][...] = dot_tn(gelu(squeezed).astype(jnp.bfloat16), low).astype(jnp.bfloat16)
    grad_squeezed = (gelu_back(squeezed) * dot_nt(low, up[...])).astype(jnp.bfloat16) * mask[...]
    gain = 1.0 + dot(tasks[...], cond[...])
    rate = rms_rate(branch)
    normed = (branch * rate * gain).astype(jnp.bfloat16)
    outs[0][...] = dot_tn(normed, grad_squeezed).astype(jnp.bfloat16)
    grad_branch, grad_gain = rms_back(branch, rate, gain, dot_nt(grad_squeezed, down[...]))
    outs[2][...] = dot_tn(tasks[...], grad_gain.astype(jnp.bfloat16))
    return grad + grad_branch


def whole_unit(weight):
    return weight.reshape(-1, weight.shape[-1])


def load_units(packed, first, held, sems):
    copies = []
    for u in range(held.shape[0]):
        copy = pltpu.make_async_copy(packed.at[:, first + u], held.at[u], sems.at[u])
        copy.start()
        copies.append(copy)
    return copies


def emit(place, outs, unit, grad):
    if len(outs) == 1:
        outs[0][0, 0, unit] = grad.astype(jnp.bfloat16)
        return
    rows = outs[0].shape[-2]
    for j in range(8):
        even = grad[2 * j * rows : (2 * j + 1) * rows].astype(jnp.bfloat16)
        odd = grad[(2 * j + 1) * rows : (2 * j + 2) * rows].astype(jnp.bfloat16)
        emit_block(place, outs, unit, j, even, odd)


def emit_block(place, outs, unit, j, even, odd):
    at = ((j & 1) ^ place[1], (j // 2 - place[0]) & 3, unit)
    if len(outs[0].shape) == 6:
        half = outs[0].shape[3]
        at = ((unit // half) ^ place[3],) + at[:2] + (unit % half,)
    outs[0][at] = jnp.where(place[2] == 0, odd, even)
    outs[1][at] = jnp.where(place[2] == 0, even, odd)


def first_kernel(
    tokens, gains, packed, cap, tasks, cond, down, up, mask,
    normed, projected, probs, mixed, branch, squeezed, stream,
    held, sems,
):
    cond, down, up = cond.at[0], down.at[0], up.at[0]
    copies = load_units(packed, 0, held, sems)
    wide = tokens[...].astype(jnp.float32)
    normed[...] = (wide * rms_rate(wide) * gains[0:1]).astype(jnp.bfloat16)
    width = wide.shape[1]
    for u in range(3):
        copies[u].wait()
        projected[:, u * width : (u + 1) * width] = dot(normed[...], whole_unit(held[u])).astype(
            jnp.bfloat16
        )
    attend_forward(projected, projected, projected, (0, width, 2 * width), cap, probs, mixed)
    copies[3].wait()
    branch[...] = dot(mixed[...], whole_unit(held[3]))
    adapted, squeezed[...] = adapter_forward(branch[...], tasks, cond, down, up, mask)
    stream[...] = tokens[...].astype(jnp.float32) + adapted


def second_kernel(
    stream, gains, packed, memory, cap, tasks, cond, down, up, mask,
    normed, query, keyval, probs, mixed, branch, squeezed, result,
    held, sems,
):
    cond, down, up = cond.at[1], down.at[1], up.at[1]
    copies = load_units(packed, 4, held, sems)
    wide = stream[...]
    normed[...] = (wide * rms_rate(wide) * gains[1:2]).astype(jnp.bfloat16)
    width = wide.shape[1]
    copies[0].wait()
    query[...] = dot(normed[...], whole_unit(held[0])).astype(jnp.bfloat16)
    for u in range(2):
        copies[1 + u].wait()
        keyval[:, u * width : (u + 1) * width] = dot(memory[...], whole_unit(held[1 + u])).astype(
            jnp.bfloat16
        )
    attend_forward(query, keyval, keyval, (0, 0, width), cap, probs, mixed)
    copies[3].wait()
    branch[...] = dot(mixed[...], whole_unit(held[3]))
    adapted, squeezed[...] = adapter_forward(branch[...], tasks, cond, down, up, mask)
    result[...] = stream[...] + adapted


def third_kernel(
    place, stream, gains, packed, out_grad, tasks, cond, down, up, mask,
    result, normed, before, grad_branch, grad_down, grad_up, grad_cond, *rest,
):
    cond, down, up = cond.at[2], down.at[2], up.at[2]
    outs, (held_in, held_out, active, total, sems) = rest[:-5], rest[-5:]
    units = active.shape[0]
    copies = load_units(packed, 8, held_in, sems)
    last = pltpu.make_async_copy(packed.at[:, 8 + units :], held_out, sems.at[units])
    last.start()
    wide = stream[...]
    normed[...] = (wide * rms_rate(wide) * gains[2:3]).astype(jnp.bfloat16)
    for copy in copies:
        copy.wait()

    def ahead(u, _):
        value = dot(normed[...], whole_unit(held_in[u]))
        before[u] = value
        active[u] = gelu(value).astype(jnp.bfloat16)
        return 0

    lax.fori_loop(0, units, ahead, 0)
    last.wait()
    total[...] = jnp.zeros_like(total)

    def gather(u, _):
        total[...] += dot(active[u], out_rows(held_out, units, u))
        return 0

    lax.fori_loop(0, units, gather, 0)
    branch = total[...]
    adapted, squeezed = adapter_forward(branch, tasks, cond, down, up, mask)
    result[...] = (stream[...] + adapted).astype(jnp.bfloat16)
    grad_branch[...] = adapter_backward(
        branch, squeezed, tasks, cond, down, up, mask,
        out_grad[...].astype(jnp.float32), (grad_down, grad_up, grad_cond),
    ).astype(jnp.bfloat16)
    half = active.shape[2] // 2

    def out_share(j, _):
        columns = pl.ds(pl.multiple_of((j & 1) * half, half), half)
        grad = dot_tn(active[j // 2, :, columns], grad_branch[...]).astype(jnp.bfloat16)
        if len(outs) == 1:
            outs[0][0, 0, j // 2, columns] = grad
        else:
            rows = outs[0].shape[-2]
            for u in range(4):
                emit_block(
                    place, outs, u, j,
                    grad[u * rows : (u + 1) * rows], grad[(4 + u) * rows : (5 + u) * rows],
                )
        return 0

    lax.fori_loop(0, 2 * units, out_share, 0)


def out_rows(held_out, units, u):
    if held_out.shape[0] == 1:
        return whole_unit(held_out[0, u])
    share = held_out.shape[0] // units
    return whole_unit(held_out[pl.ds(u * share, share)])


def fourth_kernel(
    place, stream, gains, packed, out_grad, normed, before, grad_branch,
    grad_stream, grad_gain, *rest,
):
    outs, (held_in, held_out, total, sems) = rest[:-4], rest[-4:]
    units = before.shape[0]
    copies = load_units(packed, 8, held_in, sems)
    last = pltpu.make_async_copy(packed.at[:, 8 + units :], held_out, sems.at[units])
    last.start()
    for copy in copies:
        copy.wait()
    last.wait()
    total[...] = jnp.zeros_like(total)

    def back(u, _):
        grad = dot_nt(grad_branch[...], out_rows(held_out, units, u)) * gelu_back(before[u])
        grad = grad.astype(jnp.bfloat16)
        emit(place, outs, u, dot_tn(normed[...], grad))
        total[...] += dot_nt(grad, whole_unit(held_in[u]))
        return 0

    lax.fori_loop(0, units, back, 0)
    wide = stream[...]
    grad, gain_rows = rms_back(wide, rms_rate(wide), gains[2:3], total[...])
    grad_stream[...] = out_grad[...].astype(jnp.float32) + grad
    grad_gain[...] = jnp.sum(gain_rows, axis=0, keepdims=True)


def branch_kernel(
    index, unit, grad_result, packed, branch, squeezed, tasks, cond, down, up, mask,
    grad_branch, grad_mixed, grad_down, grad_up, grad_cond,
    held, sems,
):
    cond, down, up = cond.at[index], down.at[index], up.at[index]
    (copy,) = load_units(packed, unit, held, sems)
    grad_branch[...] = adapter_backward(
        branch[...], squeezed[...], tasks, cond, down, up, mask,
        grad_result[...], (grad_down, grad_up, grad_cond),
    ).astype(jnp.bfloat16)
    copy.wait()
    grad_mixed[...] = dot_nt(grad_branch[...], whole_unit(held[0])).astype(jnp.bfloat16)


def cross_kernel(
    place, grad_result, stream, gains, packed, memory, normed, query, keyval, probs, mixed,
    grad_branch, grad_mixed,
    grad_stream, grad_memory, grad_gain, *rest,
):
    outs, (held, grad_query, grad_keyval, sems) = rest[:-4], rest[-4:]
    copies = load_units(packed, 4, held, sems)
    width = stream.shape[1]
    attend_backward(
        query, keyval, keyval, (0, 0, width), probs, grad_mixed,
        (grad_query, grad_keyval, grad_keyval), (0, 0, width),
    )
    emit(place, outs, 3, dot_tn(mixed[...], grad_branch[...]))
    emit(place, outs, 0, dot_tn(normed[...], grad_query[...]))
    for copy in copies:
        copy.wait()
    for u in range(2):
        grad = grad_keyval[:, u * width : (u + 1) * width]
        emit(place, outs, 1 + u, dot_tn(memory[...], grad))
        if u == 0:
            grad_memory[...] = dot_nt(grad, whole_unit(held[1 + u]))
        else:
            grad_memory[...] += dot_nt(grad, whole_unit(held[1 + u]))
    wide = stream[...]
    grad, gain_rows = rms_back(
        wide, rms_rate(wide), gains[1:2], dot_nt(grad_query[...], whole_unit(held[0]))
    )
    grad_stream[...] = grad_result[...] + grad
    grad_gain[...] = jnp.sum(gain_rows, axis=0, keepdims=True)


def self_kernel(
    place, grad_stream, tokens, gains, packed, normed, projected, probs, mixed, grad_branch, grad_mixed,
    grad_tokens, grad_gain, *rest,
):
    outs, (held, grad_projected, total, sems) = rest[:-4], rest[-4:]
    copies = load_units(packed, 0, held, sems)
    width = tokens.shape[1]
    attend_backward(
        projected, projected, projected, (0, width, 2 * width), probs, grad_mixed,
        (grad_projected,) * 3, (0, width, 2 * width),
    )
    emit(place, outs, 3, dot_tn(mixed[...], grad_branch[...]))
    for u in range(3):
        copies[u].wait()
        grad = grad_projected[:, u * width : (u + 1) * width]
        emit(place, outs, u, dot_tn(normed[...], grad))
        if u == 0:
            total[...] = dot_nt(grad, whole_unit(held[u]))
        else:
            total[...] += dot_nt(grad, whole_unit(held[u]))
    wide = tokens[...].astype(jnp.float32)
    grad, gain_rows = rms_back(wide, rms_rate(wide), gains[0:1], total[...])
    grad_tokens[...] = grad_stream[...] + grad
    grad_gain[...] = jnp.sum(gain_rows, axis=0, keepdims=True)


def sum_kernel(*refs):
    total = refs[0][...].astype(jnp.float32)
    for ref in refs[1:-1]:
        total = total + ref[...].astype(jnp.float32)
    refs[-1][...] = total.astype(jnp.bfloat16)


def swap(values, axis, count, mate):
    return lax.ppermute(values, axis, [(i, mate(i)) for i in range(count)])


def place_parts():
    place = lax.axis_index("fsdp")
    return place // 4, (place // 2) % 2, place % 2


def ring_gather(block):
    z, y, core = place_parts()
    shifted = [swap(block, "fsdp", 16, lambda i, d=d: (i + 4 * d) % 16) for d in (3, 2, 1)]
    line = jnp.stack(shifted[:1] + shifted[1:] + [block])
    line = lax.dynamic_slice_in_dim(jnp.concatenate([line, line]), 3 - z, 4, 0)
    other = swap(line, "fsdp", 16, lambda i: i ^ 2)
    both = jnp.stack([jnp.where(y == 0, line, other), jnp.where(y == 0, other, line)], axis=1)
    other = swap(both, "fsdp", 16, lambda i: i ^ 1)
    whole = jnp.stack([jnp.where(core == 0, both, other), jnp.where(core == 0, other, both)], axis=2)
    return whole.reshape((16,) + block.shape)


def add_low(left, right):
    return (left.astype(jnp.float32) + right.astype(jnp.float32)).astype(jnp.bfloat16)


def core_swap(sent):
    return swap(sent, "fsdp", 16, lambda i: i ^ 1)


def y_swap(sent):
    return swap(sent, "fsdp", 16, lambda i: i ^ 2)


def x_swap(sent):
    return swap(sent, "dp", 2, lambda i: i ^ 1)


def z_parts(kept, got):
    return [add_low(kept[d], got[d]) for d in range(4)]


def z_swaps(parts):
    return [swap(parts[d], "fsdp", 16, lambda i, d=d: (i + 4 * d) % 16) for d in (1, 2, 3)]


def z_total(parts, far):
    total = parts[0].astype(jnp.float32)
    for part in far:
        total = total + part.astype(jnp.float32)
    return total.astype(jnp.bfloat16)


def both_halves(total, other, first_x):
    return jnp.concatenate(
        [jnp.where(first_x, total, other), jnp.where(first_x, other, total)]
    ).astype(jnp.float32)


def after(values, *others):
    return lax.optimization_barrier((values, others))[0]


def ring_sum(values):
    for bit in (1, 2, 4, 8):
        values = values + swap(values, "fsdp", 16, lambda i, bit=bit: i ^ bit)
    return values


def gather_shards(block, ring):
    return ring_gather(block) if ring else lax.all_gather(block, "fsdp", axis=0)


def block_share(blocks):
    part = lax.psum_scatter(blocks, "fsdp", scatter_dimension=0, tiled=False)
    return lax.psum(part.astype(jnp.float32), "dp")


def ring_order(blocks):
    z, y, core = place_parts()
    parts = blocks.reshape((4, 2, 2) + blocks.shape[1:])
    line = lax.dynamic_slice_in_dim(jnp.concatenate([parts, parts]), z, 4, 0)
    ordered = [jnp.where(y == 0, line[:, b], line[:, 1 - b]) for b in (0, 1)]
    sent = jnp.stack([jnp.where(core == 0, part[:, 1], part[:, 0]) for part in ordered])
    kept = jnp.stack([jnp.where(core == 0, part[:, 0], part[:, 1]) for part in ordered])
    return sent, kept


def share_of(grads, devices, by_rows):
    whole = grads[0][0, 0]
    count, width = whole.shape[0], whole.shape[-1]
    if by_rows:
        return block_share(whole.reshape(devices, count, -1, width))
    blocks = jnp.transpose(whole.reshape(count, devices, -1, width), (1, 0, 2, 3))
    return block_share(blocks)


def sum_shards(values, ring):
    return ring_sum(values) if ring else lax.psum(values, "fsdp")


def units_of(shard, width):
    rows, columns = shard.shape
    return jnp.transpose(shard.reshape(rows, columns // width, width), (1, 0, 2))


def joined(units):
    return jnp.transpose(units, (1, 0, 2)).reshape(units.shape[1], -1)


def call(kernel, operands, shapes, scratch, flops, packed_at=None, place_first=False):
    specs = [pl.BlockSpec(memory_space=pltpu.VMEM) for _ in operands]
    if packed_at is not None:
        specs[packed_at] = pl.BlockSpec(memory_space=pl.ANY)
    if place_first:
        specs[0] = pl.BlockSpec(memory_space=pltpu.SMEM)
    outs = [jax.ShapeDtypeStruct(shape, dtype) for shape, dtype in shapes]
    moved = sum(math.prod(shape) * jnp.dtype(dtype).itemsize for shape, dtype in shapes)
    moved += sum(operand.size * operand.dtype.itemsize for operand in operands)
    return pl.pallas_call(
        kernel,
        out_shape=outs,
        in_specs=specs,
        out_specs=[pl.BlockSpec(memory_space=pltpu.VMEM) for _ in outs],
        scratch_shapes=scratch,
        compiler_params=pltpu.CompilerParams(vmem_limit_bytes=60 * 1024 * 1024),
        cost_estimate=pl.CostEstimate(flops=flops, bytes_accessed=moved, transcendentals=0),
    )(*operands)


def per_device(
    devices,
    ring,
    tokens,
    memory,
    out_grad,
    target_len,
    source_len,
    task_ids,
    norm_gains,
    self_qkv,
    self_out,
    cross_query,
    cross_keyval,
    cross_out,
    feed_in,
    feed_out,
    task_table,
    hyper_in,
    maker_down,
    maker_up,
    maker_norm,
):
    width = tokens.shape[1]
    tasks = task_table.shape[0]
    embed = hyper_in.shape[0]
    table_width = task_table.shape[1]
    hyper_width = hyper_in.shape[1]
    gain_width = norm_gains.shape[1]
    down_span = maker_down.shape[1]
    norm_span = maker_norm.shape[1]
    bottleneck = down_span * devices // (3 * width)
    down_rows = 3 * width // devices
    piece = math.gcd(width, down_span)
    down_flat = down_span * tasks // piece
    small = jnp.concatenate(
        [
            jnp.pad(task_table.T, ((0, 0), (0, 128 - tasks))),
            jnp.pad(hyper_in.T, ((0, 0), (0, 128 - embed))),
            jnp.pad(norm_gains, ((0, 0), (0, 128 - gain_width))),
            jnp.zeros((-(table_width + hyper_width + 3) % 16, 128), jnp.bfloat16),
        ]
    )
    small = gather_shards(small, ring)
    whole_table = small[:, :table_width, :tasks].reshape(-1, tasks).T
    whole_hyper = small[:, table_width : table_width + hyper_width, :embed].reshape(-1, embed).T
    first = table_width + hyper_width
    whole_gains = jnp.transpose(small[:, first : first + 3, :gain_width], (1, 0, 2)).reshape(3, width)
    packed = jnp.concatenate(
        [
            units_of(shard, width).reshape(-1, width)
            for shard in (self_qkv, self_out, cross_query, cross_keyval, cross_out, feed_in, feed_out)
        ]
    )
    packed = lax.all_gather(packed, "fsdp", axis=0)
    unit = width // devices
    ff_units = feed_in.shape[1] // width
    packed = packed.reshape(devices, -1, unit, width)
    if not ring:
        layer = jnp.transpose(packed[:, : 8 + ff_units], (1, 0, 2, 3)).reshape(-1, width, width)
        last = packed[:, 8 + ff_units :].reshape(-1, width, width)
        packed = jnp.concatenate([layer, last])[None]
    pre_hidden = matmul(whole_table, whole_hyper)
    hidden = jax.nn.silu(pre_hidden).astype(jnp.bfloat16)
    own_down = matmul(hidden, maker_down).astype(jnp.bfloat16)
    own_up = matmul(hidden, maker_up).astype(jnp.bfloat16)
    own_norm = matmul(hidden, maker_norm).astype(jnp.bfloat16)
    own_down = jnp.transpose(own_down.reshape(tasks, down_rows, bottleneck), (1, 0, 2))
    made = jnp.concatenate(
        [
            own_down.reshape(down_flat, piece),
            own_up.reshape(down_flat, piece),
            jnp.pad(own_norm, ((0, 0), (0, max(piece, norm_span) - norm_span))).reshape(-1, piece),
        ]
    )
    made = gather_shards(made, ring)
    made_down = made[:, :down_flat].reshape(3, width, tasks * bottleneck)
    made_up = made[:, down_flat : 2 * down_flat].reshape(devices, tasks, down_span // piece, piece)
    made_up = jnp.transpose(made_up, (1, 0, 2, 3)).reshape(tasks, 3, bottleneck, width)
    made_up = jnp.transpose(made_up, (1, 0, 2, 3)).reshape(3, tasks * bottleneck, width)
    made_cond = made[:, 2 * down_flat :].reshape(devices, tasks, -1)[:, :, :norm_span]
    made_cond = jnp.transpose(made_cond, (1, 0, 2)).reshape(tasks, 3, width)
    made_cond = jnp.pad(jnp.transpose(made_cond, (1, 0, 2)), ((0, 0), (0, 128 - tasks), (0, 0)))
    tok_seg = segment_rows(target_len[0], tokens.shape[0])
    mem_seg = segment_rows(source_len[0], memory.shape[0])
    sequences = jnp.arange(target_len.shape[1], dtype=jnp.int32)
    row_task = jnp.sum(
        jnp.where(tok_seg[:, None] == sequences[None, :], task_ids[0][None, :], 0), axis=1
    )
    onehot = (row_task[:, None] == jnp.arange(128, dtype=jnp.int32)[None, :]).astype(jnp.bfloat16)
    mask = jnp.repeat(onehot[:, :tasks], bottleneck, axis=1)
    places = jnp.arange(tokens.shape[0], dtype=jnp.int32)
    self_allowed = (tok_seg[:, None] == tok_seg[None, :]) & (places[:, None] <= places[None, :])
    cross_allowed = mem_seg[:, None] == tok_seg[None, :]
    self_cap = jnp.where(self_allowed, -masked_score * 1e20, masked_score).astype(jnp.float32)
    cross_cap = jnp.where(cross_allowed, -masked_score * 1e20, masked_score).astype(jnp.float32)
    gains = jnp.pad(whole_gains.astype(jnp.float32), ((0, 5), (0, 0)))
    place = lax.axis_index("fsdp")
    here = jnp.stack([place // 4, (place // 2) % 2, place % 2, lax.axis_index("dp")]).astype(jnp.int32)
    adapters = (onehot, made_cond, made_down, made_up, mask)
    rows, memory_rows = tokens.shape[0], memory.shape[0]
    heads = width // 64
    low, full = jnp.bfloat16, jnp.float32
    span = tasks * bottleneck
    held_unit = packed.shape[:1] + packed.shape[2:]

    def held(count):
        return pltpu.VMEM((count,) + held_unit, low)

    def grad_shapes(count, by_x=False):
        if ring and by_x:
            return [((2, 2, 4, count // 2, unit, width), low)] * 2
        if ring:
            return [((2, 4, count, unit, width), low)] * 2
        return [((1, 1, count, width, width), low)]

    made_shapes = [((width, span), low), ((span, width), low), ((128, width), full)]
    gain_shape = [((1, width), full)]
    busy = 1700000000
    normed1, projected, probs1, mixed1, branch1, squeezed1, stream1 = call(
        first_kernel,
        (tokens, gains, packed, self_cap) + adapters,
        [
            ((rows, width), low),
            ((rows, 3 * width), low),
            ((heads, rows, rows), low),
            ((rows, width), low),
            ((rows, width), full),
            ((rows, span), full),
            ((rows, width), full),
        ],
        [held(4), pltpu.SemaphoreType.DMA((4,))],
        16 * busy,
        packed_at=2,
    )
    normed2, query2, keyval2, probs2, mixed2, branch2, squeezed2, stream2 = call(
        second_kernel,
        (stream1, gains, packed, memory, cross_cap) + adapters,
        [
            ((rows, width), low),
            ((rows, width), low),
            ((memory_rows, 2 * width), low),
            ((heads, memory_rows, rows), low),
            ((rows, width), low),
            ((rows, width), full),
            ((rows, span), full),
            ((rows, width), full),
        ],
        [held(4), pltpu.SemaphoreType.DMA((4,))],
        21 * busy,
        packed_at=2,
    )
    held_out = (packed.shape[0], ff_units) + packed.shape[2:]
    result, normed3, before, grad_branch, *found = call(
        third_kernel,
        (here, stream2, gains, packed, out_grad) + adapters,
        [((rows, width), low), ((rows, width), low), ((ff_units, rows, width), full), ((rows, width), low)]
        + made_shapes
        + grad_shapes(ff_units, True),
        [
            held(ff_units),
            pltpu.VMEM(held_out, low),
            pltpu.VMEM((ff_units, rows, width), low),
            pltpu.VMEM((rows, width), full),
            pltpu.SemaphoreType.DMA((ff_units + 1,)),
        ],
        22 * busy,
        packed_at=3,
        place_first=True,
    )
    made_three, grads_out = found[:3], found[3:]
    if ring:
        got_out = core_swap(grads_out[0])
    grad_stream, grad_gain_three, *grads_in = call(
        fourth_kernel,
        (here, stream2, gains, packed, out_grad, normed3, before, grad_branch),
        [((rows, width), full)] + gain_shape + grad_shapes(ff_units),
        [
            held(ff_units),
            pltpu.VMEM(held_out, low),
            pltpu.VMEM((rows, width), full),
            pltpu.SemaphoreType.DMA((ff_units + 1,)),
        ],
        18 * busy,
        packed_at=3,
        place_first=True,
    )
    if ring:
        got_in = core_swap(grads_in[0])
        got_out = after(got_out, grad_gain_three)
        sent_out, kept_out = (add_low(grads_out[1][b], got_out[b]) for b in (1, 0))
        other_out = x_swap(sent_out)
        grad_stream = after(grad_stream, sent_out)

    def branch_back(index, unit_at, grad_result, branch, squeezed):
        return call(
            functools.partial(branch_kernel, index, unit_at),
            (grad_result, packed, branch, squeezed) + adapters,
            [((rows, width), low)] * 2 + made_shapes,
            [held(1), pltpu.SemaphoreType.DMA((1,))],
            30 * busy,
            packed_at=1,
        )

    grad_branch, grad_mixed, *made_two = branch_back(1, 7, grad_stream, branch2, squeezed2)
    if ring:
        got_in = after(got_in, grad_mixed)
        sent_in, kept_in = (add_low(grads_in[1][b], got_in[b]) for b in (1, 0))
        other_in = y_swap(sent_in)
        grad_mixed = after(grad_mixed, sent_in)
    grad_stream, grad_memory, grad_gain_two, *grads_cross = call(
        cross_kernel,
        (here, grad_stream, stream1, gains, packed, memory)
        + (normed2, query2, keyval2, probs2, mixed2, grad_branch, grad_mixed),
        [((rows, width), full), ((memory_rows, width), full)] + gain_shape + grad_shapes(4, True),
        [
            held(3),
            pltpu.VMEM((rows, width), low),
            pltpu.VMEM((memory_rows, 2 * width), low),
            pltpu.SemaphoreType.DMA((3,)),
        ],
        24 * busy,
        packed_at=4,
        place_first=True,
    )
    if ring:
        got_cross = core_swap(grads_cross[0])
        other_out, other_in = after((other_out, other_in), grad_gain_two)
        sum_out = add_low(kept_out, other_out)
        other_out = y_swap(sum_out[1])
        parts_in = z_parts(kept_in, other_in)
        far_in = z_swaps(parts_in)
        grad_stream = after(grad_stream, sum_out, parts_in)
    grad_branch, grad_mixed, *made_one = branch_back(0, 3, grad_stream, branch1, squeezed1)
    if ring:
        got_cross = after(got_cross, grad_mixed)
        sent_cross, kept_cross = (add_low(grads_cross[1][b], got_cross[b]) for b in (1, 0))
        other_cross = x_swap(sent_cross)
        grad_mixed = after(grad_mixed, sent_cross)
    grad_tokens, grad_gain_one, *grads_self = call(
        self_kernel,
        (here, grad_stream, tokens, gains, packed)
        + (normed1, projected, probs1, mixed1, grad_branch, grad_mixed),
        [((rows, width), full)] + gain_shape + grad_shapes(4),
        [
            held(3),
            pltpu.VMEM((rows, 3 * width), low),
            pltpu.VMEM((rows, width), full),
            pltpu.SemaphoreType.DMA((3,)),
        ],
        18 * busy,
        packed_at=4,
        place_first=True,
    )
    grad_down = jnp.stack([made_one[0], made_two[0], made_three[0]])
    grad_up = jnp.stack([made_one[1], made_two[1], made_three[1]])
    grad_up = jnp.transpose(grad_up.reshape(3, tasks, bottleneck, width), (1, 0, 2, 3))
    grad_up = grad_up.reshape(tasks, devices, down_span // piece, piece)
    grad_norm = jnp.concatenate([made_one[2], made_two[2], made_three[2]], axis=1)[:tasks]
    grad_norm = grad_norm.astype(jnp.bfloat16)
    grad_norm = jnp.transpose(grad_norm.reshape(tasks, devices, norm_span), (1, 0, 2))
    made_blocks = jnp.concatenate(
            [
                grad_down.reshape(devices, down_flat, piece),
                jnp.transpose(grad_up, (1, 0, 2, 3)).reshape(devices, down_flat, piece),
                jnp.pad(grad_norm, ((0, 0), (0, 0), (0, max(piece, norm_span) - norm_span))).reshape(
                    devices, -1, piece
                ),
            ],
            axis=1,
        )
    if ring:
        first_x = lax.axis_index("dp") == 0
        sent_made, kept_made = ring_order(made_blocks)
        got_self, got_made = core_swap(grads_self[0]), core_swap(sent_made)
        far_in, other_cross, other_out = after((far_in, other_cross, other_out), grad_gain_one)
        total_in = call(sum_kernel, (parts_in[0], *far_in), [(parts_in[0].shape, low)], [], 100 * busy)[0]
        got_self, got_made = after((got_self, got_made), total_in)
        sent_self, kept_self = (add_low(grads_self[1][b], got_self[b]) for b in (1, 0))
        sum_cross = add_low(kept_cross, other_cross)
        parts_out = z_parts(sum_out[0], other_out)
        sum_made = add_low(kept_made, got_made)
        sent_self, sum_cross, parts_out, total_in, sum_made = lax.optimization_barrier(
            (sent_self, sum_cross, parts_out, total_in, sum_made)
        )
        flight = (y_swap(sent_self), z_swaps(parts_out), x_swap(total_in), y_swap(sum_made[1]))
        other_self, far_out, other_in, other_made = lax.optimization_barrier(flight)
        share_in = total_in.astype(jnp.float32) + other_in.astype(jnp.float32)
        parts_self = z_parts(kept_self, other_self)
        total_out = z_total(parts_out, far_out)
        parts_made = z_parts(sum_made[0], other_made)
        parts_self, total_out, parts_made = lax.optimization_barrier((parts_self, total_out, parts_made))
        flight = (z_swaps(parts_self), y_swap(sum_cross[1]), x_swap(total_out), z_swaps(parts_made))
        far_self, other_cross, other_out, far_made = lax.optimization_barrier(flight)
        share_out = both_halves(total_out, other_out, first_x)
        total_self = z_total(parts_self, far_self)
        parts_cross = z_parts(sum_cross[0], other_cross)
        total_made = z_total(parts_made, far_made)
        total_self, parts_cross, total_made = lax.optimization_barrier((total_self, parts_cross, total_made))
        flight = (x_swap(total_self), z_swaps(parts_cross), x_swap(total_made))
        other_self, far_cross, other_made = lax.optimization_barrier(flight)
        share_self = total_self.astype(jnp.float32) + other_self.astype(jnp.float32)
        total_cross = z_total(parts_cross, far_cross)
        share_cross = both_halves(total_cross, x_swap(total_cross), first_x)
        share_made = total_made.astype(jnp.float32) + other_made.astype(jnp.float32)
    else:
        share_in, share_out, share_cross, share_self = (
            share_of(grads, devices, grads is grads_out)
            for grads in (grads_in, grads_out, grads_cross, grads_self)
        )
        share_made = block_share(made_blocks)
    out_feed_in = joined(share_in)
    out_feed_out = share_out.reshape(-1, width)
    out_query = share_cross[0]
    out_keyval = joined(share_cross[1:3])
    out_cross_out = share_cross[3]
    out_qkv = joined(share_self[:3])
    out_self_out = share_self[3]
    norm_rows = tasks * max(1, norm_span // piece)
    own_down = jnp.transpose(
        share_made[:down_flat].reshape(down_rows, tasks, bottleneck), (1, 0, 2)
    ).reshape(tasks, down_span)
    own_up = share_made[down_flat : 2 * down_flat].reshape(tasks, down_span)
    own_norm = share_made[2 * down_flat : 2 * down_flat + norm_rows].reshape(tasks, -1)[:, :norm_span]
    hidden_wide = hidden.astype(jnp.float32)
    grad_hidden = (
        exact_cols(own_down, maker_down.astype(jnp.float32))
        + exact_cols(own_up, maker_up.astype(jnp.float32))
        + exact_cols(own_norm, maker_norm.astype(jnp.float32))
    )
    grad_gains = jnp.concatenate([grad_gain_one, grad_gain_two, grad_gain_three])
    grad_gains = grad_gains + x_swap(grad_gains) if ring else lax.psum(grad_gains, "dp")
    sums = sum_shards(jnp.concatenate([grad_hidden, grad_gains.reshape(-1, 128)]), ring)
    grad_hidden = sums[:tasks]
    out_gains = lax.dynamic_slice_in_dim(
        sums[tasks:].reshape(3, width), place * gain_width, gain_width, 1
    )
    _, silu_pull = jax.vjp(jax.nn.silu, pre_hidden)
    grad_pre_hidden = silu_pull(grad_hidden)[0]
    own_hyper = lax.dynamic_slice_in_dim(whole_hyper, place * table_width, table_width, 0)
    out_table = exact_cols(grad_pre_hidden, own_hyper.astype(jnp.float32))
    own_pre = lax.dynamic_slice_in_dim(grad_pre_hidden, place * hyper_width, hyper_width, 1)
    out_hyper = exact_rows(whole_table.astype(jnp.float32), own_pre)
    out_down = exact_rows(hidden_wide, own_down)
    out_up = exact_rows(hidden_wide, own_up)
    out_norm = exact_rows(hidden_wide, own_norm)
    return (
        result.astype(jnp.bfloat16),
        grad_tokens,
        grad_memory,
        out_gains,
        out_qkv,
        out_self_out,
        out_query,
        out_keyval,
        out_cross_out,
        out_feed_in,
        out_feed_out,
        out_table,
        out_hyper,
        out_down,
        out_up,
        out_norm,
    )


def solution(mesh):
    placed = (
        P(("fsdp", "dp"), None),
        P(("fsdp", "dp"), None),
        P(("fsdp", "dp"), None),
        P(("fsdp", "dp"), None),
        P(("fsdp", "dp"), None),
        P(("fsdp", "dp"), None),
        P(None, "fsdp"),
        P("fsdp", None),
        P("fsdp", None),
        P("fsdp", None),
        P("fsdp", None),
        P("fsdp", None),
        P("fsdp", None),
        P("fsdp", None),
        P(None, "fsdp"),
        P(None, "fsdp"),
        P(None, "fsdp"),
        P(None, "fsdp"),
        P(None, "fsdp"),
    )
    devices = mesh.shape["fsdp"]
    ring = devices == 16 and mesh.shape["dp"] == 2
    return jax.shard_map(
        functools.partial(per_device, devices, ring),
        mesh=mesh,
        in_specs=placed,
        out_specs=(
            P(("fsdp", "dp"), None),
            P(("fsdp", "dp"), None),
            P(("fsdp", "dp"), None),
            P(None, "fsdp"),
            P("fsdp", None),
            P("fsdp", None),
            P("fsdp", None),
            P("fsdp", None),
            P("fsdp", None),
            P("fsdp", None),
            P("fsdp", None),
            P(None, "fsdp"),
            P(None, "fsdp"),
            P(None, "fsdp"),
            P(None, "fsdp"),
            P(None, "fsdp"),
        ),
        check_vma=False,
    )
```

```python
import functools
import math

import jax
import jax.numpy as jnp
from jax import lax
from jax.experimental import pallas as pl
from jax.experimental.pallas import tpu as pltpu
from jax.sharding import PartitionSpec as P

norm_epsilon = 1e-06
masked_score = -1000000000.0
highest = lax.Precision.HIGHEST


def matmul(left, right):
    return jnp.dot(left, right, preferred_element_type=jnp.float32)


def exact_rows(left, right):
    return lax.dot_general(
        left, right, (((0,), (0,)), ((), ())), precision=highest, preferred_element_type=jnp.float32
    )


def exact_cols(left, right):
    return lax.dot_general(
        left, right, (((1,), (1,)), ((), ())), precision=highest, preferred_element_type=jnp.float32
    )


def segment_rows(lengths, count):
    ends = jnp.cumsum(lengths)
    places = jnp.arange(count, dtype=jnp.int32)
    return jnp.sum((places[:, None] >= ends[None, :]).astype(jnp.int32), axis=1)


def dot(left, right):
    return jnp.dot(left, right, preferred_element_type=jnp.float32)


def dot_nt(left, right):
    return lax.dot_general(
        left, right, (((1,), (1,)), ((), ())), preferred_element_type=jnp.float32
    )


def dot_tn(left, right):
    return lax.dot_general(
        left, right, (((0,), (0,)), ((), ())), preferred_element_type=jnp.float32
    )


def rms_rate(values):
    return lax.rsqrt(jnp.mean(values * values, axis=-1, keepdims=True) + norm_epsilon)


def rms_back(values, rate, gain, grad):
    scaled = grad * gain
    inner = jnp.mean(scaled * values, axis=-1, keepdims=True)
    return rate * (scaled - values * (rate * rate * inner)), grad * values * rate


gelu_slope = math.sqrt(2.0 / math.pi)
gelu_cube = 0.044715


def gelu(values):
    inner = gelu_slope * values * (1.0 + gelu_cube * values * values)
    return 0.5 * values * (1.0 + jnp.tanh(inner))


def gelu_back(values):
    square = values * values
    bent = jnp.tanh(gelu_slope * values * (1.0 + gelu_cube * square))
    slope = gelu_slope * (1.0 + 3.0 * gelu_cube * square)
    return 0.5 * (1.0 + bent) + 0.5 * values * (1.0 - bent * bent) * slope


def halves(dtype):
    lane = lax.broadcasted_iota(jnp.int32, (1, 128), 1)
    first = (lane < 64).astype(jnp.float32)
    return first.astype(dtype), (1.0 - first).astype(dtype)


def lanes(start):
    return pl.ds(pl.multiple_of(start, 128), 128)


class Fetched:
    def __init__(self, source, held, sems, count):
        self.source, self.held, self.sems, self.count = source, held, sems, count
        self.waiting, self.shape, self.started = count == 1, held.shape, False

    def start(self):
        if not self.started:
            for k in range(self.count):
                self.part(k).start()
        self.started = True

    def part(self, k):
        if self.count == 1:
            return pltpu.make_async_copy(self.source, self.held, self.sems.at[0])
        size = self.shape[0] // self.count
        at = pl.ds(k * size, size)
        return pltpu.make_async_copy(self.source.at[at], self.held.at[at], self.sems.at[k])

    def ready(self):
        self.start()
        if self.waiting:
            self.part(0).wait()
            self.waiting = False
        return self.held

    def __getitem__(self, at):
        return self.ready()[at]

    @property
    def at(self):
        return self.ready().at


class Shipped:
    def __init__(self, target, held, sems):
        self.target, self.held, self.sems = target, held, sems
        self.shape, self.parts = held.shape, None

    def __getitem__(self, at):
        return self.held[at]

    def __setitem__(self, at, values):
        self.held[at] = values

    @property
    def at(self):
        return self.held.at

    def copy(self, k, part):
        return pltpu.make_async_copy(part(self.held, k), part(self.target, k), self.sems.at[k])

    def ship(self):
        self.leave(0, lambda ref, k: ref)

    def leave(self, k, part):
        self.parts = part
        self.copy(k, part).start()

    def settle(self):
        if self.parts is None:
            self.ship()
        if self.sems.shape[0] == 1:
            self.copy(0, self.parts).wait()
        else:
            lax.fori_loop(0, self.sems.shape[0], lambda k, _: self.copy(k, self.parts).wait() or 0, 0)


def ready(*refs):
    return [ref.ready() if isinstance(ref, Fetched) else ref for ref in refs]


def sides(turned):
    none = jnp.zeros_like(turned[:64])
    return jnp.concatenate(
        [jnp.concatenate([turned[:64], none], axis=0), jnp.concatenate([none, turned[64:]], axis=0)], axis=1
    )


def own_sides(both):
    half = both.shape[1] // 2
    return jnp.concatenate([both[:64, :half], both[64:, half:]], axis=0)


def attend_forward(queries, keys, values, starts, cap, weights, scales, mixed):
    factor = math.log2(math.e) / 8.0
    for p in range(mixed.shape[1] // 128):
        query, key, value = (
            ref[:, start + p * 128 : start + p * 128 + 128]
            for ref, start in zip((queries, keys, values), starts)
        )
        limit = cap[...]
        scores = dot(key, sides(query.T)) * factor
        scores = jnp.minimum(scores, jnp.concatenate([limit, limit], axis=1))
        powers = jnp.exp2(scores - jnp.max(scores, axis=0, keepdims=True))
        scale = 1.0 / jnp.sum(powers, axis=0, keepdims=True)
        powers = powers.astype(jnp.bfloat16)
        weights[p] = powers
        weights.leave(p, one_pair)
        scales[p] = scale
        found = own_sides(dot(value.T, powers) * scale)
        mixed[:, p * 128 : p * 128 + 128] = found.T.astype(jnp.bfloat16)
    mixed.ship()
    scales.ship()


def one_pair(ref, k):
    return ref.at[k]


def attend_backward(queries, keys, values, starts, weights, scales, grad_mixed, grads, places, beside):
    marks = halves(jnp.bfloat16)
    pairs = grad_mixed.shape[1] // 128
    weights.started = True
    for p in (0, 1):
        weights.part(p).start()
    for p in range(pairs):
        query, key, value = (
            ref[:, start + p * 128 : start + p * 128 + 128]
            for ref, start in zip((queries, keys, values), starts)
        )
        scale = scales[p]
        grad = sides(grad_mixed[:, p * 128 : p * 128 + 128].T)
        grad = (grad.astype(jnp.float32) * scale).astype(jnp.bfloat16)
        if p == 1:
            beside()
        if p + 2 < pairs:
            weights.part(p + 2).start()
        weights.part(p).wait()
        powers = weights.held[p]
        wide = powers.astype(jnp.float32)
        product = wide * dot(value, grad)
        total = jnp.sum(product, axis=0, keepdims=True) * scale
        product = (product - wide * total).astype(jnp.bfloat16)
        query = jnp.concatenate([query * marks[0], query * marks[1]], axis=0)
        columns = [slice(place + p * 128, place + p * 128 + 128) for place in places]
        grads[2][:, columns[2]] = dot(powers, grad.T).astype(jnp.bfloat16)
        grads[1][:, columns[1]] = (dot(product, query) * 0.125).astype(jnp.bfloat16)
        grads[0][:, columns[0]] = (own_sides(dot(key.T, product)).T * 0.125).astype(jnp.bfloat16)


def adapter_forward(branch, index, tasks, cond, down, up, mask):
    gain = 1.0 + dot(tasks[...], cond[index])
    normed = (branch * rms_rate(branch) * gain).astype(jnp.bfloat16)
    squeezed = dot(normed, down[index]) * mask[...].astype(jnp.float32)
    return branch + dot(gelu(squeezed).astype(jnp.bfloat16), up[index]), squeezed


def adapter_backward(branch, squeezed, index, tasks, cond, down, up, mask, grad, outs):
    low = grad.astype(jnp.bfloat16)
    outs[1][...] = dot_tn(gelu(squeezed).astype(jnp.bfloat16), low)
    grad_squeezed = (gelu_back(squeezed) * dot_nt(low, up[index])).astype(jnp.bfloat16) * mask[...]
    gain = 1.0 + dot(tasks[...], cond[index])
    rate = rms_rate(branch)
    normed = (branch * rate * gain).astype(jnp.bfloat16)
    outs[0][...] = dot_tn(normed, grad_squeezed).astype(jnp.bfloat16)
    grad_branch, grad_gain = rms_back(branch, rate, gain, dot_nt(grad_squeezed, down[index]))
    outs[2][...] = dot_tn(tasks[...], grad_gain.astype(jnp.bfloat16))[: outs[2].shape[0]]
    return grad + grad_branch


def whole_unit(weight):
    return weight.reshape(-1, weight.shape[-1])


def unit_copy(packed, first, held, sems, u):
    return pltpu.make_async_copy(packed.at[:, first + u], held.at[u], sems.at[u])


def load_units(packed, first, held, sems):
    copies = [unit_copy(packed, first, held, sems, u) for u in range(held.shape[0])]
    for copy in copies:
        copy.start()
    return copies


def rows_copy(packed, held, sems, u):
    units = held.shape[1]
    if held.shape[0] == 1:
        return pltpu.make_async_copy(packed.at[:, 8 + units + u], held.at[:, u], sems.at[units + u])
    share = held.shape[0] // units
    at = pl.ds(u * share, share)
    return pltpu.make_async_copy(packed.at[at, 8 + units :], held.at[at], sems.at[units + u])


def out_rows(held, u):
    units = held.shape[1]
    if held.shape[0] == 1:
        return whole_unit(held[0, u])
    share = held.shape[0] // units
    return whole_unit(held[pl.ds(u * share, share)])


def emit(place, outs, unit, grad):
    if len(outs) == 1:
        outs[0][0, 0, unit] = grad.astype(jnp.bfloat16)
    else:
        rows = outs[0].shape[-2]
        grad = grad.astype(jnp.bfloat16)
        for j in range(8):
            even = grad[2 * j * rows : (2 * j + 1) * rows]
            odd = grad[(2 * j + 1) * rows : (2 * j + 2) * rows]
            emit_block(place, outs, unit, j, even, odd)
    for out in outs:
        out.leave(unit, functools.partial(unit_part, place))


def unit_part(place, ref, unit):
    return ref.at[:, :, :, unit] if len(ref.shape) == 6 else ref.at[:, :, unit]


def emit_block(place, outs, unit, j, even, odd):
    at = ((j & 1) ^ place[1], (j // 2 - place[0]) & 3, unit)
    for out, block in zip(outs, (jnp.where(place[2] == 0, odd, even), jnp.where(place[2] == 0, even, odd))):
        if len(out.shape) == 6:
            half = out.shape[5]
            for x in (0, 1):
                out[(x ^ place[3],) + at] = block[:, x * half : (x + 1) * half]
        else:
            out[at] = block


def attention_kernel(
    tokens, gains, packed, self_cap, tasks, cond, down, up, mask, memory, cross_cap,
    first_normed, projected, first_weights, first_scales, first_mixed, first_branch, first_squeezed, stream,
    normed, query, keyval, weights, scales, mixed, branch, squeezed, result,
    held, sems,
):
    made = (tasks, cond, down, up, mask)
    copies = [unit_copy(packed, 0, held, sems, u) for u in range(8)]
    copies[0].start()
    wide = tokens[...].astype(jnp.float32)
    first_normed[...] = (wide * rms_rate(wide) * gains[0:1]).astype(jnp.bfloat16)
    first_normed.ship()
    width = wide.shape[1]
    copies[1].start()
    for u in range(3):
        copies[u + 2].start()
        copies[u].wait()
        projected[:, u * width : (u + 1) * width] = dot(first_normed[...], whole_unit(held[u])).astype(
            jnp.bfloat16
        )
    projected.ship()
    for operand in (*made, memory, cross_cap):
        operand.start()
    for copy in copies[5:]:
        copy.start()
    attend_forward(
        projected, projected, projected, (0, width, 2 * width), self_cap, first_weights, first_scales, first_mixed
    )
    copies[3].wait()
    first_branch[...] = dot(first_mixed[...], whole_unit(held[3]))
    first_branch.ship()
    adapted, first_squeezed[...] = adapter_forward(first_branch[...], 0, *made)
    first_squeezed.ship()
    wide = tokens[...].astype(jnp.float32) + adapted
    stream[...] = wide
    stream.ship()
    normed[...] = (wide * rms_rate(wide) * gains[1:2]).astype(jnp.bfloat16)
    normed.ship()
    copies[4].wait()
    query[...] = dot(normed[...], whole_unit(held[4])).astype(jnp.bfloat16)
    query.ship()
    for u in range(2):
        copies[5 + u].wait()
        keyval[:, u * width : (u + 1) * width] = dot(memory[...], whole_unit(held[5 + u])).astype(
            jnp.bfloat16
        )
    keyval.ship()
    attend_forward(query, keyval, keyval, (0, 0, width), cross_cap, weights, scales, mixed)
    copies[7].wait()
    branch[...] = dot(mixed[...], whole_unit(held[7]))
    branch.ship()
    adapted, squeezed[...] = adapter_forward(branch[...], 1, *made)
    result[...] = stream[...] + adapted


def feed_kernel(
    place, stream, gains, packed, tasks, cond, down, up, mask, out_grad,
    result, grad_stream, grad_down, grad_up, grad_cond, grad_gain, *rest,
):
    made = (tasks, cond, down, up, mask)
    outs, (held_in, held_out, normed, before, active, grad_branch, total, sems) = rest[:-8], rest[-8:]
    ahead, outs = outs[: len(outs) // 2], outs[len(outs) // 2 :]
    units = active.shape[0]

    def start(u):
        unit_copy(packed, 8, held_in, sems, u).start()
        rows_copy(packed, held_out, sems, u).start()

    start(0)
    wide = stream[...]
    normed[...] = (wide * rms_rate(wide) * gains[2:3]).astype(jnp.bfloat16)
    total[...] = jnp.zeros_like(total)
    for u in range(units):
        if u + 1 < units:
            start(u + 1)
        else:
            for operand in (*made, out_grad):
                operand.start()
        unit_copy(packed, 8, held_in, sems, u).wait()
        value = dot(normed[...], whole_unit(held_in[u]))
        before[u] = value
        active[u] = gelu(value).astype(jnp.bfloat16)
        rows_copy(packed, held_out, sems, u).wait()
        total[...] += dot(active[u], out_rows(held_out, u))
    branch = total[...]
    adapted, squeezed = adapter_forward(branch, 0, *made)
    result[...] = (stream[...] + adapted).astype(jnp.bfloat16)
    result.ship()
    grad_branch[...] = adapter_backward(
        branch, squeezed, 0, *made, out_grad[...].astype(jnp.float32), (grad_down, grad_up, grad_cond)
    ).astype(jnp.bfloat16)
    for out in (grad_down, grad_up, grad_cond):
        out.ship()
    half = active.shape[2] // 2

    def row_part(ref, j):
        if len(outs) == 1:
            return ref.at[0, 0, j // 2, pl.ds((j & 1) * half, half)]
        return ref.at[:, (j & 1) ^ place[1], (j // 2 - place[0]) & 3]

    for j in range(2 * units):
        columns = slice((j & 1) * half, (j & 1) * half + half)
        grad = dot_tn(active[j // 2, :, columns], grad_branch[...]).astype(jnp.bfloat16)
        if len(outs) == 1:
            ahead[0][0, 0, j // 2, columns] = grad
        else:
            rows = outs[0].shape[-2]
            for u in range(4):
                emit_block(
                    place, ahead, u, j,
                    grad[u * rows : (u + 1) * rows], grad[(4 + u) * rows : (5 + u) * rows],
                )
        for out in ahead:
            out.leave(j, row_part)
    total[...] = jnp.zeros_like(total)
    for u in range(units):
        grad = dot_nt(grad_branch[...], out_rows(held_out, u))
        grad = (grad * gelu_back(before[u])).astype(jnp.bfloat16)
        emit(place, outs, u, dot_tn(normed[...], grad))
        total[...] += dot_nt(grad, whole_unit(held_in[u]))
    wide = stream[...]
    grad, gain_rows = rms_back(wide, rms_rate(wide), gains[2:3], total[...])
    grad_stream[...] = out_grad[...].astype(jnp.float32) + grad
    grad_gain[...] = jnp.sum(gain_rows, axis=0, keepdims=True)


def branch_kernel(unit, place, grad_result, packed, squeezed, branch, tasks, cond, down, up, mask, *rest):
    *rest, held, sems = rest
    (copy,) = load_units(packed, unit, held, sems)
    others = 12 if len(rest) > 5 else 0
    others, (grad_branch, grad_mixed, *found) = rest[:others], rest[others:]
    low = grad_result[...]
    for operand in others[6:]:
        operand.start()
    grad_branch[...] = adapter_backward(
        branch[...], squeezed[...], 0, tasks, cond, down, up, mask, low, found[:3]
    ).astype(jnp.bfloat16)
    for out in (grad_branch, *found[:3]):
        out.ship()
    copy.wait()
    grad_mixed[...] = dot_nt(grad_branch[...], whole_unit(held[0])).astype(jnp.bfloat16)
    grad_mixed.ship()
    if others:
        emit_made(place, [found[:3], others[:3], others[3:6]], found[3:5], found[-1])
        own, sent, *parts = found[5:-1]
        for z in range(4):
            sent[z] = low_sum(*(part[1, z] for part in others[6:9]))
        sent.ship()
        for z in range(4):
            parts[z][...] = low_sum(*(part[z] for part in others[9:]))
            parts[z].ship()
        for z in range(4):
            own[z] = low_sum(*(part[0, z] for part in others[6:9]))


def low_sum(*parts):
    total = parts[0].astype(jnp.float32)
    for part in parts[1:]:
        total = total + part.astype(jnp.float32)
    return total.astype(jnp.bfloat16)


def first_sums(kept_cross, got_cross, other_cross, kept_made, got_made, other_made, own_out, other_out, sent_cross, *parts):
    half = other_out.shape[-1]
    for z in range(4):
        parts[z][:2] = low_sum(kept_made[z], got_made[z], other_made[z])
        for u in range(4):
            columns = slice((u & 1) * half, (u & 1) * half + half)
            parts[z][2 + u // 2, :, columns] = low_sum(own_out[z, u], other_out[z, u])
        parts[z].ship()
    for z in range(4):
        sent_cross[z] = low_sum(kept_cross[z], got_cross[z], other_cross[z])


def kept_sums(kept, got, other, *rest):
    for z in range(4):
        rest[-1][z] = low_sum(kept[z], got[z], other[z])
    if len(rest) > 1:
        rest[-2][...] = low_sum(*(ref[...] for ref in rest[:4]))


def second_sums(*refs):
    total_in, kept_self, got_self, other_self, own_cross, other_cross = refs[4:10]
    totals, made, sent_self, *parts = refs[10:]
    for z in range(4):
        sent_self[z] = low_sum(kept_self[z], got_self[z], other_self[z])
    sent_self.ship()
    made[...] = low_sum(*(ref[:2] for ref in refs[:4]))
    made.ship()
    for z in range(4):
        parts[z][...] = low_sum(own_cross[z], other_cross[z])
        parts[z].ship()
    units = total_in.shape[0]
    totals[units:] = low_sum(*(ref[2:] for ref in refs[:4]))
    totals[:units] = total_in[...]


def feed_outs(place, total, other, out_in, out_out):
    wide = total.shape[-1]
    units, rows, half = out_in.shape[1] // wide, out_in.shape[0], wide // 2
    for u in range(units):
        out_in[:, u * wide : (u + 1) * wide] = total[u].astype(jnp.float32) + other[u].astype(jnp.float32)
    for u in range(units):
        at = (units + u // 2, slice(None), slice((u & 1) * half, (u & 1) * half + half))
        join(place, total[at], other[at], out_out, slice(u * rows, (u + 1) * rows), 0)


def join(place, own, other, out, rows, column):
    own, other = own.astype(jnp.float32), other.astype(jnp.float32)
    half = own.shape[-1]
    out[rows, column : column + half] = jnp.where(place[3] == 0, own, other)
    out[rows, column + half : column + 2 * half] = jnp.where(place[3] == 0, other, own)


def unit_outs(place, total, other, *outs):
    unit, wide = 0, 2 * total.shape[-1]
    for out in outs:
        for column in range(0, out.shape[1], wide):
            join(place, total[unit], other[unit], out, slice(None), column)
            unit += 1


def third_sums(*refs):
    own_self, other_self, total_cross, *parts = refs[4:]
    for z in range(4):
        parts[z][...] = low_sum(own_self[z], other_self[z])
        parts[z].ship()
    total_cross[...] = low_sum(*(ref[...] for ref in refs[:4]))


def emit_made(place, made, outs, block):
    rows, wide = outs[0].shape[3], block.shape[2]
    piece, span = wide // 2, wide // 3
    block[...] = jnp.zeros_like(block)
    cond = jnp.concatenate([part[2][...] for part in made], axis=1)
    columns = cond.shape[1] // 16
    for j in range(8):
        for core in (0, 1):
            for slot in range(3):
                at = 3 * (2 * j + core) + slot
                part = made[at // 16][0][(at % 16) * rows : (at % 16 + 1) * rows]
                block[core, :, slot * span : slot * span + part.shape[1]] = part.astype(jnp.float32)
        emit_block(place, outs, 0, j, *(block[core].astype(jnp.bfloat16) for core in (0, 1)))
    for out in outs:
        out.leave(0, functools.partial(unit_part, place))
    block[...] = jnp.zeros_like(block)
    for j in range(8):
        for core in (0, 1):
            owner = 2 * j + core
            for slot in range(9):
                at = 9 * owner + slot
                row, half = (at % 48) // 2, at % 2
                part = made[at // 48][1][row * 8 : row * 8 + 8, half * piece : (half + 1) * piece]
                block[core, slot // 2 * 8 : slot // 2 * 8 + 8, slot % 2 * piece : (slot % 2 + 1) * piece] = part
            turned = pltpu.roll(cond, (cond.shape[1] - owner * columns) % cond.shape[1], 1)
            block[core, 40:48, :span] = turned[:, :span]
        emit_block(place, outs, 1, j, *(block[core].astype(jnp.bfloat16) for core in (0, 1)))
    for out in outs:
        out.leave(1, functools.partial(unit_part, place))


def cross_kernel(
    place, grad_mixed, packed, query, keyval, weights, scales, mixed, grad_branch, normed, memory, stream, gains, grad_result,
    grad_stream, grad_memory, grad_gain, *rest,
):
    outs, (held, grad_query, grad_keyval, sems) = rest[:-4], rest[-4:]
    copies = [unit_copy(packed, 4, held, sems, u) for u in range(3)]
    width = stream.shape[1]

    def beside():
        for copy in (mixed, grad_branch, normed, memory, *copies, stream, gains, grad_result):
            copy.start()

    attend_backward(
        query, keyval, keyval, (0, 0, width), weights, scales, grad_mixed,
        (grad_query, grad_keyval, grad_keyval), (0, 0, width), beside,
    )
    emit(place, outs, 3, dot_tn(mixed[...], grad_branch[...]))
    emit(place, outs, 0, dot_tn(normed[...], grad_query[...]))
    for copy in copies:
        copy.wait()
    for u in range(2):
        grad = grad_keyval[:, u * width : (u + 1) * width]
        emit(place, outs, 1 + u, dot_tn(memory[...], grad))
        if u == 0:
            grad_memory[...] = dot_nt(grad, whole_unit(held[1 + u]))
        else:
            grad_memory[...] += dot_nt(grad, whole_unit(held[1 + u]))
    grad_memory.ship()
    wide = stream[...]
    grad, gain_rows = rms_back(
        wide, rms_rate(wide), gains[1:2], dot_nt(grad_query[...], whole_unit(held[0]))
    )
    grad_stream[...] = grad_result[...] + grad
    grad_gain[...] = jnp.sum(gain_rows, axis=0, keepdims=True)


def self_kernel(
    place, grad_mixed, packed, projected, weights, scales, mixed, grad_branch, normed, tokens, gains, grad_stream,
    grad_tokens, grad_gain, *rest,
):
    outs, (held, grad_projected, total, sems) = rest[:-4], rest[-4:]
    copies = [unit_copy(packed, 0, held, sems, u) for u in range(3)]
    width = tokens.shape[1]

    def beside():
        for copy in (mixed, grad_branch, normed, *copies, tokens, gains, grad_stream):
            copy.start()

    attend_backward(
        projected, projected, projected, (0, width, 2 * width), weights, scales, grad_mixed,
        (grad_projected,) * 3, (0, width, 2 * width), beside,
    )
    emit(place, outs, 3, dot_tn(mixed[...], grad_branch[...]))
    for u in range(3):
        copies[u].wait()
        grad = grad_projected[:, u * width : (u + 1) * width]
        emit(place, outs, u, dot_tn(normed[...], grad))
        if u == 0:
            total[...] = dot_nt(grad, whole_unit(held[u]))
        else:
            total[...] += dot_nt(grad, whole_unit(held[u]))
    wide = tokens[...].astype(jnp.float32)
    grad, gain_rows = rms_back(wide, rms_rate(wide), gains[0:1], total[...])
    grad_tokens[...] = grad_stream[...] + grad
    grad_gain[...] = jnp.sum(gain_rows, axis=0, keepdims=True)


def sum_kernel(*refs):
    refs[-1][...] = low_sum(*(ref[...] for ref in refs[:-1]))


def swap(values, axis, count, mate):
    return lax.ppermute(values, axis, [(i, mate(i)) for i in range(count)])


def place_parts():
    place = lax.axis_index("fsdp")
    return place // 4, (place // 2) % 2, place % 2


def ring_gather(block):
    z, y, core = place_parts()
    shifted = [swap(block, "fsdp", 16, lambda i, d=d: (i + 4 * d) % 16) for d in (3, 2, 1)]
    line = jnp.stack(shifted[:1] + shifted[1:] + [block])
    line = lax.dynamic_slice_in_dim(jnp.concatenate([line, line]), 3 - z, 4, 0)
    other = swap(line, "fsdp", 16, lambda i: i ^ 2)
    both = jnp.stack([jnp.where(y == 0, line, other), jnp.where(y == 0, other, line)], axis=1)
    other = swap(both, "fsdp", 16, lambda i: i ^ 1)
    whole = jnp.stack([jnp.where(core == 0, both, other), jnp.where(core == 0, other, both)], axis=2)
    return whole.reshape((16,) + block.shape)


def add_low(left, right):
    return (left.astype(jnp.float32) + right.astype(jnp.float32)).astype(jnp.bfloat16)


def core_swap(sent):
    return swap(sent, "fsdp", 16, lambda i: i ^ 1)


def y_swap(sent):
    return swap(sent, "fsdp", 16, lambda i: i ^ 2)


def x_swap(sent):
    return swap(sent, "dp", 2, lambda i: i ^ 1)


def z_swaps(parts):
    return [swap(parts[d], "fsdp", 16, lambda i, d=d: (i + 4 * d) % 16) for d in (1, 2, 3)]


def both_halves(own, other, first_x):
    return jnp.concatenate([jnp.where(first_x, own, other), jnp.where(first_x, other, own)], axis=-1)


def after(values, *others):
    return lax.optimization_barrier((values, others))[0]


def ring_step(values, bit):
    return values + swap(values, "fsdp", 16, lambda i: i ^ bit)


def gather_shards(block, ring):
    return ring_gather(block) if ring else lax.all_gather(block, "fsdp", axis=0)


def block_share(blocks):
    part = lax.psum_scatter(blocks, "fsdp", scatter_dimension=0, tiled=False)
    return lax.psum(part.astype(jnp.float32), "dp")


def share_of(grads, devices, by_rows):
    whole = grads[0][0, 0]
    count, width = whole.shape[0], whole.shape[-1]
    if by_rows:
        return block_share(whole.reshape(devices, count, -1, width))
    blocks = jnp.transpose(whole.reshape(count, devices, -1, width), (1, 0, 2, 3))
    return block_share(blocks)


def sum_shards(values, ring):
    return ring_sum(values) if ring else lax.psum(values, "fsdp")


def units_of(shard, width):
    rows, columns = shard.shape
    return jnp.transpose(shard.reshape(rows, columns // width, width), (1, 0, 2))


def joined(units):
    return jnp.transpose(units, (1, 0, 2)).reshape(units.shape[1], -1)


def view_shape(shape, view):
    return tuple(at.size for at in view if not isinstance(at, int)) + tuple(shape[len(view) :])


def call(kernel, operands, shapes, scratch, flops, raw=(), split=None, parts=None, later=(), views=None):
    split, parts, views = split or {}, parts or {}, views or {}
    scalars = operands[0].ndim == 1
    moved_in = [i for i in range(int(scalars), len(operands)) if i not in raw]
    specs = [pl.BlockSpec(memory_space=pl.ANY) for _ in operands]
    if scalars:
        specs[0] = pl.BlockSpec(memory_space=pltpu.SMEM)
    outs = [jax.ShapeDtypeStruct(shape, dtype) for shape, dtype in shapes]
    buffers = [pltpu.VMEM(view_shape(operands[i].shape, views.get(i, ())), operands[i].dtype) for i in moved_in]
    buffers += [pltpu.VMEM(shape, dtype) for shape, dtype in shapes]
    buffers += [pltpu.SemaphoreType.DMA((split.get(i, 1),)) for i in moved_in]
    buffers += [pltpu.SemaphoreType.DMA((parts.get(k, 1),)) for k in range(len(outs))]

    def body(*refs):
        ins, results = list(refs[: len(operands)]), refs[len(operands) : len(operands) + len(outs)]
        own = refs[len(operands) + len(outs) : len(refs) - len(buffers)]
        held = refs[len(refs) - len(buffers) :]
        held, sems = held[: len(buffers) // 2], held[len(buffers) // 2 :]
        for k, i in enumerate(moved_in):
            source = ins[i].at[views[i]] if i in views else ins[i]
            ins[i] = Fetched(source, held[k], sems[k], split.get(i, 1))
            if i not in later:
                ins[i].start()
        results = [
            Shipped(target, *rest) for target, *rest in zip(results, held[len(moved_in) :], sems[len(moved_in) :])
        ]
        kernel(*ins, *results, *own)
        for operand in ins:
            ready(operand)
        for result in results:
            result.settle()

    moved = sum(math.prod(shape) * jnp.dtype(dtype).itemsize for shape, dtype in shapes)
    moved += sum(operand.size * operand.dtype.itemsize for operand in operands)
    return pl.pallas_call(
        body,
        out_shape=outs,
        in_specs=specs,
        out_specs=[pl.BlockSpec(memory_space=pl.ANY) for _ in outs],
        scratch_shapes=list(scratch) + buffers,
        compiler_params=pltpu.CompilerParams(vmem_limit_bytes=60 * 1024 * 1024),
        cost_estimate=pl.CostEstimate(flops=flops, bytes_accessed=moved, transcendentals=0),
    )(*operands)


def per_device(
    devices,
    ring,
    tokens,
    memory,
    out_grad,
    target_len,
    source_len,
    task_ids,
    norm_gains,
    self_qkv,
    self_out,
    cross_query,
    cross_keyval,
    cross_out,
    feed_in,
    feed_out,
    task_table,
    hyper_in,
    maker_down,
    maker_up,
    maker_norm,
):
    width = tokens.shape[1]
    tasks = task_table.shape[0]
    embed = hyper_in.shape[0]
    table_width = task_table.shape[1]
    hyper_width = hyper_in.shape[1]
    gain_width = norm_gains.shape[1]
    down_span = maker_down.shape[1]
    norm_span = maker_norm.shape[1]
    bottleneck = down_span * devices // (3 * width)
    down_rows = 3 * width // devices
    unit = width // devices
    ff_units = feed_in.shape[1] // width
    small = jnp.concatenate(
        [
            jnp.pad(task_table.T, ((0, 0), (0, 128 - tasks))),
            jnp.pad(hyper_in.T, ((0, 0), (0, 128 - embed))),
            jnp.pad(norm_gains, ((0, 0), (0, 128 - gain_width))),
            jnp.zeros((-(table_width + hyper_width + 3) % 16, 128), jnp.bfloat16),
        ]
    )
    small = gather_shards(small, ring)
    whole_table = small[:, :table_width, :tasks].reshape(-1, tasks).T
    whole_hyper = small[:, table_width : table_width + hyper_width, :embed].reshape(-1, embed).T
    first = table_width + hyper_width
    whole_gains = jnp.transpose(small[:, first : first + 3, :gain_width], (1, 0, 2)).reshape(3, width)
    layer = [self_qkv, self_out, cross_query, cross_keyval, cross_out, feed_in]
    layer = [units_of(w, width) for w in layer] + [feed_out.reshape(ff_units, unit, width)]
    packed = jnp.concatenate([w.reshape(-1, width) for w in layer])
    packed = lax.all_gather(packed, "fsdp", axis=0).reshape(devices, -1, unit, width)
    if not ring:
        first = jnp.transpose(packed[:, : 8 + ff_units], (1, 0, 2, 3)).reshape(-1, width, width)
        last = packed[:, 8 + ff_units :].reshape(-1, width, width)
        packed = jnp.concatenate([first, last])[None]
    pre_hidden = matmul(whole_table, whole_hyper)
    hidden = jax.nn.silu(pre_hidden).astype(jnp.bfloat16)
    own_down = matmul(hidden, maker_down).astype(jnp.bfloat16)
    own_up = matmul(hidden, maker_up).astype(jnp.bfloat16)
    own_norm = matmul(hidden, maker_norm).astype(jnp.bfloat16)
    span = tasks * bottleneck
    own_down = jnp.transpose(own_down.reshape(tasks, down_rows, bottleneck), (1, 2, 0)).reshape(-1, span)
    if ring:
        third, piece = width // 3, width // 2
        own_down = jnp.pad(own_down.reshape(3, unit, span), ((0, 0), (0, 0), (0, third - span)))
        own_down = jnp.transpose(own_down, (1, 0, 2)).reshape(unit, width)
        own_up = jnp.pad(own_up, ((0, 0), (0, 10 * piece - down_span))).reshape(tasks, 5, width)
        own_up = jnp.transpose(own_up, (1, 0, 2)).reshape(5 * tasks, width)
        own_norm = jnp.pad(own_norm, ((0, 0), (0, width - norm_span)))
        made = jnp.concatenate([own_down, own_up, own_norm])
        first_x = lax.axis_index("dp") == 0
        made = ring_gather(jnp.where(first_x, made[:, : width // 2], made[:, width // 2 :]))
        made = both_halves(made, x_swap(made), first_x)
        made_down = made[:, :unit].reshape(devices, unit, 3, third)[..., :span]
        made_down = jnp.transpose(made_down, (0, 2, 1, 3)).reshape(3, width, span)
        made_up = made[:, unit : unit + 5 * tasks].reshape(devices, 5, tasks, 2, piece)
        made_up = jnp.transpose(made_up, (0, 1, 3, 2, 4)).reshape(devices, 10, tasks, piece)[:, :9]
        made_up = jnp.transpose(made_up.reshape(3, bottleneck, 2, tasks, piece), (0, 1, 3, 2, 4))
        made_up = made_up.reshape(3, span, width)
        made_cond = made[:, unit + 5 * tasks :, :norm_span]
    else:
        made_down = lax.all_gather(own_down, "fsdp", axis=0, tiled=True).reshape(3, width, span)
        made_up = lax.all_gather(own_up, "fsdp", axis=1, tiled=True).reshape(tasks, 3, bottleneck, width)
        made_up = jnp.transpose(made_up, (1, 2, 0, 3)).reshape(3, span, width)
        made_cond = lax.all_gather(own_norm, "fsdp", axis=0)
    made_cond = jnp.transpose(made_cond, (1, 0, 2)).reshape(tasks, 3, width)
    made_cond = jnp.pad(jnp.transpose(made_cond, (1, 0, 2)), ((0, 0), (0, 128 - tasks), (0, 0)))
    tok_seg = segment_rows(target_len[0], tokens.shape[0])
    mem_seg = segment_rows(source_len[0], memory.shape[0])
    sequences = jnp.arange(target_len.shape[1], dtype=jnp.int32)
    row_task = jnp.sum(
        jnp.where(tok_seg[:, None] == sequences[None, :], task_ids[0][None, :], 0), axis=1
    )
    onehot = (row_task[:, None] == jnp.arange(128, dtype=jnp.int32)[None, :]).astype(jnp.bfloat16)
    mask = jnp.tile(onehot[:, :tasks], (1, bottleneck))
    places = jnp.arange(tokens.shape[0], dtype=jnp.int32)
    self_allowed = (tok_seg[:, None] == tok_seg[None, :]) & (places[:, None] <= places[None, :])
    cross_allowed = mem_seg[:, None] == tok_seg[None, :]
    self_cap = jnp.where(self_allowed, -masked_score * 1e20, masked_score).astype(jnp.float32)
    cross_cap = jnp.where(cross_allowed, -masked_score * 1e20, masked_score).astype(jnp.float32)
    gains = jnp.pad(whole_gains.astype(jnp.float32), ((0, 5), (0, 0)))
    place = lax.axis_index("fsdp")
    here = jnp.stack([place // 4, (place // 2) % 2, place % 2, lax.axis_index("dp")]).astype(jnp.int32)
    adapters = (onehot, made_cond, made_down, made_up, mask)
    rows, memory_rows = tokens.shape[0], memory.shape[0]
    pairs = width // 128
    low, full = jnp.bfloat16, jnp.float32
    held_unit = packed.shape[:1] + packed.shape[2:]

    def held(count):
        return pltpu.VMEM((count,) + held_unit, low)

    def grad_shapes(count, by_x=False):
        if ring and by_x:
            return [((2, 2, 4, count, unit, width // 2), low)] * 2
        if ring:
            return [((2, 4, count, unit, width), low)] * 2
        return [((1, 1, count, width, width), low)]

    made_shapes = [((width, span), low), ((span, width), full), ((tasks, width), full)]
    gain_shape = [((1, width), full)]
    busy = 1700000000
    scale_shape = ((pairs, 1, 2 * rows), full)
    float_rows, low_rows = ((rows, width), full), ((rows, width), low)
    found = call(
        attention_kernel,
        (tokens, gains, packed, self_cap) + adapters + (memory, cross_cap),
        [low_rows, ((rows, 3 * width), low), ((pairs, rows, 2 * rows), low), scale_shape, low_rows, float_rows]
        + [((rows, span), full), float_rows, low_rows, low_rows, ((memory_rows, 2 * width), low)]
        + [((pairs, memory_rows, 2 * rows), low), scale_shape, low_rows, float_rows]
        + [((rows, span), full), float_rows],
        [held(8), pltpu.SemaphoreType.DMA((8,))],
        37 * busy,
        raw=(2,),
        parts={2: pairs, 11: pairs},
        later=(4, 5, 6, 7, 8, 9, 10),
    )
    normed1, projected, weights1, scales1, mixed1, branch1, squeezed1, stream1, *found = found
    normed2, query2, keyval2, weights2, scales2, mixed2, branch2, squeezed2, stream2 = found
    held_out = (packed.shape[0], ff_units) + packed.shape[2:]
    sets = 2 if ring else 1
    result, grad_stream, *found = call(
        feed_kernel,
        (here, stream2, gains, packed) + adapters + (out_grad,),
        [low_rows, float_rows] + made_shapes + gain_shape + grad_shapes(ff_units, True) + grad_shapes(ff_units),
        [
            held(ff_units),
            pltpu.VMEM(held_out, low),
            pltpu.VMEM((rows, width), low),
            pltpu.VMEM((ff_units, rows, width), full),
            pltpu.VMEM((ff_units, rows, width), low),
            pltpu.VMEM((rows, width), low),
            pltpu.VMEM((rows, width), full),
            pltpu.SemaphoreType.DMA((2 * ff_units,)),
        ],
        36 * busy,
        raw=(3,),
        parts={6 + k: (2 if k < sets else 1) * ff_units for k in range(2 * sets)},
        later=(4, 5, 6, 7, 8, 9),
        views=dict.fromkeys((5, 6, 7), (pl.ds(2, 1),)),
    )
    made_three, grad_gain_three, grads_out, grads_in = found[:3], found[3], found[4 : 4 + sets], found[4 + sets :]

    def branch_back(index, unit_at, grad_result, branch, squeezed, others, shapes):
        return call(
            functools.partial(branch_kernel, unit_at),
            (here, grad_result, packed, squeezed, branch) + adapters + others,
            [low_rows] * 2 + made_shapes + shapes,
            [pltpu.VMEM((2, unit, width), full)] * int(bool(others)) + [held(1), pltpu.SemaphoreType.DMA((1,))],
            30 * busy,
            raw=(2,),
            parts={5: 2, 6: 2} if others else {},
            later=tuple(range(16, 22)) if others else (),
            views=dict.fromkeys((6, 7, 8), (pl.ds(index, 1),))
            | (dict.fromkeys((16, 17, 19, 20), (0,)) if others else {}),
        )

    if ring:
        got_out, got_in = core_swap(grads_out[0]), core_swap(grads_in[0])
    grad_branch, grad_mixed, *made_two = branch_back(1, 7, grad_stream, branch2, squeezed2, (), [])
    if ring:
        got_out, got_in = after((got_out, got_in), grad_mixed)
        sent_out, sent_in = (add_low(kept[1], got[1]) for (_, kept), got in ((grads_out, got_out), (grads_in, got_in)))
        other_out, other_in = x_swap(sent_out), y_swap(sent_in)
        grad_mixed = after(grad_mixed, sent_out, sent_in)
    grad_stream, grad_memory, grad_gain_two, *grads_cross = call(
        cross_kernel,
        (here, grad_mixed, packed, query2, keyval2, weights2, scales2, mixed2, grad_branch, normed2)
        + (memory, stream1, gains, grad_stream),
        [float_rows, ((memory_rows, width), full)] + gain_shape + grad_shapes(4, True),
        [
            held(3),
            pltpu.VMEM((rows, width), low),
            pltpu.VMEM((memory_rows, 2 * width), low),
            pltpu.SemaphoreType.DMA((3,)),
        ],
        24 * busy,
        raw=(2,),
        split={5: pairs},
        parts={3: 4, 4: 4},
        later=(5,) + tuple(range(7, 14)),
    )
    others, shapes = (), []
    if ring:
        got_cross = core_swap(grads_cross[0])
        others = (*made_two, *made_three, grads_out[1], got_out, other_out, grads_in[1], got_in, other_in)
        shapes = [((2, 4, 2, unit, width), low)] * 2
        shapes += [((4, ff_units, unit, width // 2), low)] * 2 + [((ff_units, unit, width), low)] * 4
    grad_branch, grad_mixed, *made_one = branch_back(0, 3, grad_stream, branch1, squeezed1, others, shapes)
    if ring:
        sent_made, kept_made, own_out, sent_out, *parts_in = made_one[3:]
        got_made = core_swap(sent_made)
        got_cross = after(got_cross, grad_mixed)
        sent_cross = add_low(grads_cross[1][1], got_cross[1])
        other_cross = x_swap(sent_cross)
        sent_out, parts_in = after((sent_out, parts_in), sent_cross)
        other_out, far_in = y_swap(sent_out), z_swaps(parts_in)
        sent_made = add_low(kept_made[1], after(got_made, sent_cross)[1])
        other_made = y_swap(sent_made)
        grad_mixed = after(grad_mixed, sent_made)
    grad_tokens, grad_gain_one, *grads_self = call(
        self_kernel,
        (here, grad_mixed, packed, projected, weights1, scales1, mixed1, grad_branch, normed1, tokens, gains)
        + (grad_stream,),
        [float_rows] + gain_shape + grad_shapes(4, True),
        [
            held(3),
            pltpu.VMEM((rows, 3 * width), low),
            pltpu.VMEM((rows, width), full),
            pltpu.SemaphoreType.DMA((3,)),
        ],
        18 * busy,
        raw=(2,),
        split={4: pairs},
        parts={2: 4, 3: 4},
        later=(4,) + tuple(range(6, 12)),
    )

    def own_made(share):
        own_down = share[0].reshape(unit, 3, third)[:, :, :span]
        own_down = jnp.transpose(own_down, (1, 0, 2)).reshape(down_rows, bottleneck, tasks)
        own_down = jnp.transpose(own_down, (2, 0, 1)).reshape(tasks, down_span)
        own_up = share[1, : 5 * tasks].reshape(5, tasks, width)
        own_up = jnp.transpose(own_up, (1, 0, 2)).reshape(tasks, 5 * width)[:, :down_span]
        return own_down, own_up, share[1, 5 * tasks :, :norm_span]

    def hidden_of(own_down, own_up, own_norm):
        return (
            dot_nt(own_down.astype(jnp.bfloat16), maker_down)
            + dot_nt(own_up.astype(jnp.bfloat16), maker_up)
            + dot_nt(own_norm.astype(jnp.bfloat16), maker_norm)
        )

    grad_gains = jnp.concatenate([grad_gain_one, grad_gain_two, grad_gain_three]).reshape(-1, 128)
    if ring:
        got_self = core_swap(grads_self[0])
        flight = (far_in, other_cross, other_made, other_out)
        far_in, other_cross, other_made, other_out = after(flight, grad_gain_one)
        halves_y, column_half = ((4, 4, unit, width // 2), low), ((4, unit, width // 2), low)
        whole_part = ((4, unit, width), low)
        sent_cross, *parts = call(
            first_sums,
            (grads_cross[1], got_cross, other_cross, kept_made, got_made, other_made, own_out, other_out),
            [halves_y] + [whole_part] * 4,
            [],
            100 * busy,
            views={0: (0, 1), 1: (0, 1), 2: (1,), 3: (0,), 4: (0,)},
        )
        sent_self = add_low(grads_self[1][1], after(got_self, sent_cross)[1])
        other_self = x_swap(sent_self)
        parts, sent_cross = after((parts, sent_cross), sent_self)
        far = z_swaps(parts)
        kept_cross, far_in = after((grads_cross[1], far_in), sent_self)
        total_in, own_cross = call(
            kept_sums,
            (kept_cross, got_cross, other_cross, parts_in[0], *far_in),
            [whole_part, halves_y],
            [],
            100 * busy,
            views={0: (0, 0), 1: (0, 0), 2: (0,)},
        )
        other_cross = y_swap(sent_cross)
        totals, total_made, sent_self, *parts = call(
            second_sums,
            (parts[0], *far, total_in, grads_self[1], got_self, other_self, own_cross, other_cross),
            [((6, unit, width), low), ((2, unit, width), low), halves_y] + [column_half] * 4,
            [],
            5 * busy,
            views={5: (0, 1), 6: (0, 1), 7: (1,)},
        )
        other_made, far, other_totals = x_swap(total_made), z_swaps(parts), x_swap(totals)
        (own_self,) = call(
            kept_sums,
            (after(grads_self[1], other_made), got_self, other_self),
            [halves_y],
            [],
            100 * busy,
            views={0: (0, 0), 1: (0, 0), 2: (0,)},
        )
        other_self = y_swap(sent_self)
        other_gains = x_swap(after(grad_gains, total_made))
        share_made = total_made.astype(jnp.float32) + other_made.astype(jnp.float32)
        own_down, own_up, own_norm = own_made(share_made)
        sums = jnp.concatenate([hidden_of(own_down, own_up, own_norm), grad_gains + other_gains])
        sums = ring_step(sums, 1)
        total_cross, *parts = call(
            third_sums, (parts[0], *far, own_self, other_self), [column_half] * 5, [], 5 * busy
        )
        other_cross, far = x_swap(total_cross), z_swaps(parts)
        sums = ring_step(after(sums, total_cross), 2)
        shapes = [((unit, ff_units * width), full), ((ff_units * unit, width), full)]
        out_feed_in, out_feed_out = call(
            feed_outs, (here, totals, after(other_totals, sums)), shapes, [], 100 * busy
        )
        for part in z_swaps([sums] * 4):
            sums = sums + part
        far = after(far, sums)
        total_self = call(sum_kernel, (parts[0], *far), [column_half], [], 5 * busy)[0]
        other_self, other_cross = x_swap(total_self), after(other_cross, total_self)
        shapes = [((unit, count * width), full) for count in (1, 2, 1)]
        out_query, out_keyval, out_cross_out = call(
            unit_outs, (here, total_cross, other_cross), shapes, [], 100 * busy
        )
        shapes = [((unit, count * width), full) for count in (3, 1)]
        out_qkv, out_self_out = call(unit_outs, (here, total_self, other_self), shapes, [], busy)
    else:
        share_in, share_out, share_cross, share_self = (
            share_of(grads, devices, grads is grads_out)
            for grads in (grads_in, grads_out, grads_cross, grads_self)
        )
        made = (made_one, made_two, made_three)
        grad_down = jnp.concatenate([part[0] for part in made]).reshape(devices, -1)
        grad_up = jnp.stack([part[1] for part in made]).reshape(3, bottleneck, tasks, width)
        grad_up = jnp.transpose(grad_up, (2, 0, 1, 3)).reshape(tasks, devices, down_span)
        grad_norm = jnp.concatenate([part[2] for part in made], axis=1)
        grad_norm = grad_norm.reshape(tasks, devices, norm_span)
        blocks = [grad_down.astype(jnp.bfloat16)] + [
            jnp.transpose(part.astype(jnp.bfloat16), (1, 0, 2)).reshape(devices, -1)
            for part in (grad_up, grad_norm)
        ]
        out_feed_in, out_feed_out = joined(share_in), share_out.reshape(-1, width)
        out_query, out_keyval, out_cross_out = share_cross[0], joined(share_cross[1:3]), share_cross[3]
        out_qkv, out_self_out = joined(share_self[:3]), share_self[3]
        share_made = block_share(jnp.concatenate(blocks, axis=1))
        sizes = (0, tasks * down_span, 2 * tasks * down_span, share_made.shape[0])
        own_down, own_up, own_norm = (share_made[a:b] for a, b in zip(sizes, sizes[1:]))
        own_down = jnp.transpose(own_down.reshape(down_rows, bottleneck, tasks), (2, 0, 1))
        own_down, own_up = own_down.reshape(tasks, down_span), own_up.reshape(tasks, down_span)
        own_norm = own_norm.reshape(tasks, norm_span)
        sums = jnp.concatenate([hidden_of(own_down, own_up, own_norm), lax.psum(grad_gains, "dp")])
        sums = lax.psum(sums, "fsdp")
    grad_hidden = sums[:tasks]
    out_gains = lax.dynamic_slice_in_dim(
        sums[tasks:].reshape(3, width), place * gain_width, gain_width, 1
    )
    _, silu_pull = jax.vjp(jax.nn.silu, pre_hidden)
    grad_pre_hidden = silu_pull(grad_hidden)[0]
    own_hyper = lax.dynamic_slice_in_dim(whole_hyper, place * table_width, table_width, 0)
    out_table = exact_cols(grad_pre_hidden, own_hyper.astype(jnp.float32))
    own_pre = lax.dynamic_slice_in_dim(grad_pre_hidden, place * hyper_width, hyper_width, 1)
    out_hyper = exact_rows(whole_table.astype(jnp.float32), own_pre)
    out_down, out_up, out_norm = (
        dot_tn(hidden, own.astype(jnp.bfloat16)) for own in (own_down, own_up, own_norm)
    )
    return (
        result.astype(jnp.bfloat16),
        grad_tokens,
        grad_memory,
        out_gains,
        out_qkv,
        out_self_out,
        out_query,
        out_keyval,
        out_cross_out,
        out_feed_in,
        out_feed_out,
        out_table,
        out_hyper,
        out_down,
        out_up,
        out_norm,
    )


def solution(mesh):
    placed = (
        P(("fsdp", "dp"), None),
        P(("fsdp", "dp"), None),
        P(("fsdp", "dp"), None),
        P(("fsdp", "dp"), None),
        P(("fsdp", "dp"), None),
        P(("fsdp", "dp"), None),
        P(None, "fsdp"),
        P("fsdp", None),
        P("fsdp", None),
        P("fsdp", None),
        P("fsdp", None),
        P("fsdp", None),
        P("fsdp", None),
        P("fsdp", None),
        P(None, "fsdp"),
        P(None, "fsdp"),
        P(None, "fsdp"),
        P(None, "fsdp"),
        P(None, "fsdp"),
    )
    devices = mesh.shape["fsdp"]
    ring = devices == 16 and mesh.shape["dp"] == 2
    return jax.shard_map(
        functools.partial(per_device, devices, ring),
        mesh=mesh,
        in_specs=placed,
        out_specs=(
            P(("fsdp", "dp"), None),
            P(("fsdp", "dp"), None),
            P(("fsdp", "dp"), None),
            P(None, "fsdp"),
            P("fsdp", None),
            P("fsdp", None),
            P("fsdp", None),
            P("fsdp", None),
            P("fsdp", None),
            P("fsdp", None),
            P("fsdp", None),
            P(None, "fsdp"),
            P(None, "fsdp"),
            P(None, "fsdp"),
            P(None, "fsdp"),
            P(None, "fsdp"),
        ),
        check_vma=False,
    )
```

```python
import functools
import math

import jax
import jax.numpy as jnp
from jax import lax
from jax.experimental import pallas as pl
from jax.experimental.pallas import tpu as pltpu
from jax.sharding import PartitionSpec as P

norm_epsilon = 1e-06
masked_score = -1000000000.0
highest = lax.Precision.HIGHEST


def matmul(left, right):
    return jnp.dot(left, right, preferred_element_type=jnp.float32)


def exact_rows(left, right):
    return lax.dot_general(
        left, right, (((0,), (0,)), ((), ())), precision=highest, preferred_element_type=jnp.float32
    )


def exact_cols(left, right):
    return lax.dot_general(
        left, right, (((1,), (1,)), ((), ())), precision=highest, preferred_element_type=jnp.float32
    )


def segment_rows(lengths, count):
    ends = jnp.cumsum(lengths)
    places = jnp.arange(count, dtype=jnp.int32)
    return jnp.sum((places[:, None] >= ends[None, :]).astype(jnp.int32), axis=1)


def dot(left, right):
    return jnp.dot(left, right, preferred_element_type=jnp.float32)


def dot_nt(left, right):
    return lax.dot_general(
        left, right, (((1,), (1,)), ((), ())), preferred_element_type=jnp.float32
    )


def dot_tn(left, right):
    return lax.dot_general(
        left, right, (((0,), (0,)), ((), ())), preferred_element_type=jnp.float32
    )


def rms_rate(values):
    return lax.rsqrt(jnp.mean(values * values, axis=-1, keepdims=True) + norm_epsilon)


def rms_back(values, rate, gain, grad):
    scaled = grad * gain
    inner = jnp.mean(scaled * values, axis=-1, keepdims=True)
    return rate * (scaled - values * (rate * rate * inner)), grad * values * rate


gelu_slope = math.sqrt(2.0 / math.pi)
gelu_cube = 0.044715


def gelu(values):
    inner = gelu_slope * values * (1.0 + gelu_cube * values * values)
    return 0.5 * values * (1.0 + jnp.tanh(inner))


def gelu_back(values):
    square = values * values
    bent = jnp.tanh(gelu_slope * values * (1.0 + gelu_cube * square))
    slope = gelu_slope * (1.0 + 3.0 * gelu_cube * square)
    return 0.5 * (1.0 + bent) + 0.5 * values * (1.0 - bent * bent) * slope


def halves(dtype):
    lane = lax.broadcasted_iota(jnp.int32, (1, 128), 1)
    first = (lane < 64).astype(jnp.float32)
    return first.astype(dtype), (1.0 - first).astype(dtype)


def lanes(start):
    return pl.ds(pl.multiple_of(start, 128), 128)


class Fetched:
    def __init__(self, source, held, sems, count):
        self.source, self.held, self.sems, self.count = source, held, sems, count
        self.waiting, self.shape, self.started = count == 1, held.shape, False

    def start(self):
        if not self.started:
            for k in range(self.count):
                self.part(k).start()
        self.started = True

    def part(self, k):
        if self.count == 1:
            return pltpu.make_async_copy(self.source, self.held, self.sems.at[0])
        size = self.shape[0] // self.count
        at = pl.ds(k * size, size)
        return pltpu.make_async_copy(self.source.at[at], self.held.at[at], self.sems.at[k])

    def ready(self):
        self.start()
        if self.waiting:
            self.part(0).wait()
            self.waiting = False
        return self.held

    def __getitem__(self, at):
        return self.ready()[at]

    @property
    def at(self):
        return self.ready().at


class Shipped:
    def __init__(self, target, held, sems):
        self.target, self.held, self.sems = target, held, sems
        self.shape, self.parts = held.shape, None

    def __getitem__(self, at):
        return self.held[at]

    def __setitem__(self, at, values):
        self.held[at] = values

    @property
    def at(self):
        return self.held.at

    def copy(self, k, part):
        return pltpu.make_async_copy(part(self.held, k), part(self.target, k), self.sems.at[k])

    def ship(self):
        self.leave(0, lambda ref, k: ref)

    def leave(self, k, part):
        self.parts = part
        self.copy(k, part).start()

    def settle(self):
        if self.parts is None:
            self.ship()
        if self.sems.shape[0] == 1:
            self.copy(0, self.parts).wait()
        else:
            lax.fori_loop(0, self.sems.shape[0], lambda k, _: self.copy(k, self.parts).wait() or 0, 0)


def ready(*refs):
    return [ref.ready() if isinstance(ref, Fetched) else ref for ref in refs]


def sides(turned):
    none = jnp.zeros_like(turned[:64])
    return jnp.concatenate(
        [jnp.concatenate([turned[:64], none], axis=0), jnp.concatenate([none, turned[64:]], axis=0)], axis=1
    )


def own_sides(both):
    half = both.shape[1] // 2
    return jnp.concatenate([both[:64, :half], both[64:, half:]], axis=0)


def attend_forward(queries, keys, values, starts, cap, weights, scales, mixed):
    factor = math.log2(math.e) / 8.0
    queries, keys, values, cap = ready(queries, keys, values, cap)

    def pair(p, _):
        query, key, value = (
            ref[:, lanes(start + p * 128)] for ref, start in zip((queries, keys, values), starts)
        )
        limit = cap[...]
        scores = dot(key, sides(query.T)) * factor
        scores = jnp.minimum(scores, jnp.concatenate([limit, limit], axis=1))
        powers = jnp.exp2(scores - jnp.max(scores, axis=0, keepdims=True))
        scale = 1.0 / jnp.sum(powers, axis=0, keepdims=True)
        powers = powers.astype(jnp.bfloat16)
        weights[p] = powers
        weights.leave(p, one_pair)
        scales[p] = scale
        found = own_sides(dot(value.T, powers) * scale)
        mixed[:, lanes(p * 128)] = found.T.astype(jnp.bfloat16)
        return 0

    lax.fori_loop(0, mixed.shape[1] // 128, pair, 0, unroll=3)
    mixed.ship()
    scales.ship()


def one_pair(ref, k):
    return ref.at[k]


def attend_backward(queries, keys, values, starts, weights, scales, grad_mixed, grads, places, beside):
    marks = halves(jnp.bfloat16)
    pairs = grad_mixed.shape[1] // 128
    weights.started = True
    for p in (0, 1):
        weights.part(p).start()
    for p in range(pairs):
        query, key, value = (
            ref[:, start + p * 128 : start + p * 128 + 128]
            for ref, start in zip((queries, keys, values), starts)
        )
        scale = scales[p]
        grad = sides(grad_mixed[:, p * 128 : p * 128 + 128].T)
        grad = (grad.astype(jnp.float32) * scale).astype(jnp.bfloat16)
        if p == 1:
            beside()
        if p + 2 < pairs:
            weights.part(p + 2).start()
        weights.part(p).wait()
        powers = weights.held[p]
        wide = powers.astype(jnp.float32)
        product = wide * dot(value, grad)
        total = jnp.sum(product, axis=0, keepdims=True) * scale
        product = (product - wide * total).astype(jnp.bfloat16)
        query = jnp.concatenate([query * marks[0], query * marks[1]], axis=0)
        columns = [slice(place + p * 128, place + p * 128 + 128) for place in places]
        grads[2][:, columns[2]] = dot(powers, grad.T).astype(jnp.bfloat16)
        grads[1][:, columns[1]] = (dot(product, query) * 0.125).astype(jnp.bfloat16)
        grads[0][:, columns[0]] = (own_sides(dot(key.T, product)).T * 0.125).astype(jnp.bfloat16)


def adapter_forward(branch, index, tasks, cond, down, up, mask):
    gain = 1.0 + dot(tasks[...], cond[index])
    normed = (branch * rms_rate(branch) * gain).astype(jnp.bfloat16)
    squeezed = dot(normed, down[index]) * mask[...].astype(jnp.float32)
    return branch + dot(gelu(squeezed).astype(jnp.bfloat16), up[index]), squeezed


def adapter_backward(branch, squeezed, index, tasks, cond, down, up, mask, grad, outs):
    low = grad.astype(jnp.bfloat16)
    outs[1][...] = dot_tn(gelu(squeezed).astype(jnp.bfloat16), low)
    grad_squeezed = (gelu_back(squeezed) * dot_nt(low, up[index])).astype(jnp.bfloat16) * mask[...]
    gain = 1.0 + dot(tasks[...], cond[index])
    rate = rms_rate(branch)
    normed = (branch * rate * gain).astype(jnp.bfloat16)
    outs[0][...] = dot_tn(normed, grad_squeezed).astype(jnp.bfloat16)
    grad_branch, grad_gain = rms_back(branch, rate, gain, dot_nt(grad_squeezed, down[index]))
    outs[2][...] = dot_tn(tasks[...], grad_gain.astype(jnp.bfloat16))[: outs[2].shape[0]]
    return grad + grad_branch


def whole_unit(weight):
    return weight.reshape(-1, weight.shape[-1])


def unit_copy(packed, first, held, sems, u):
    return pltpu.make_async_copy(packed.at[:, first + u], held.at[u], sems.at[u])


def load_units(packed, first, held, sems):
    copies = [unit_copy(packed, first, held, sems, u) for u in range(held.shape[0])]
    for copy in copies:
        copy.start()
    return copies


def rows_copy(packed, held, sems, u):
    units = held.shape[1]
    if held.shape[0] == 1:
        return pltpu.make_async_copy(packed.at[:, 8 + units + u], held.at[:, u], sems.at[units + u])
    share = held.shape[0] // units
    at = pl.ds(u * share, share)
    return pltpu.make_async_copy(packed.at[at, 8 + units :], held.at[at], sems.at[units + u])


def out_rows(held, u):
    units = held.shape[1]
    if held.shape[0] == 1:
        return whole_unit(held[0, u])
    share = held.shape[0] // units
    return whole_unit(held[pl.ds(u * share, share)])


def emit(place, outs, unit, grad):
    if len(outs) == 1:
        outs[0][0, 0, unit] = grad.astype(jnp.bfloat16)
    else:
        rows = outs[0].shape[-2]
        grad = grad.astype(jnp.bfloat16)
        for j in range(8):
            even = grad[2 * j * rows : (2 * j + 1) * rows]
            odd = grad[(2 * j + 1) * rows : (2 * j + 2) * rows]
            emit_block(place, outs, unit, j, even, odd)
    for out in outs:
        out.leave(unit, functools.partial(unit_part, place))


def unit_part(place, ref, unit):
    return ref.at[:, :, :, unit] if len(ref.shape) == 6 else ref.at[:, :, unit]


def emit_block(place, outs, unit, j, even, odd):
    at = ((j & 1) ^ place[1], (j // 2 - place[0]) & 3, unit)
    for out, block in zip(outs, (jnp.where(place[2] == 0, odd, even), jnp.where(place[2] == 0, even, odd))):
        if len(out.shape) == 6:
            half = out.shape[5]
            for x in (0, 1):
                out[(x ^ place[3],) + at] = block[:, x * half : (x + 1) * half]
        else:
            out[at] = block


def attention_kernel(
    tokens, gains, packed, self_cap, tasks, cond, down, up, mask, memory, cross_cap,
    first_normed, projected, first_weights, first_scales, first_mixed, first_branch, first_squeezed, stream,
    normed, query, keyval, weights, scales, mixed, branch, squeezed, result,
    held, sems,
):
    made = (tasks, cond, down, up, mask)
    copies = [unit_copy(packed, 0, held, sems, u) for u in range(8)]
    copies[0].start()
    wide = tokens[...].astype(jnp.float32)
    first_normed[...] = (wide * rms_rate(wide) * gains[0:1]).astype(jnp.bfloat16)
    first_normed.ship()
    width = wide.shape[1]
    copies[1].start()
    for u in range(3):
        copies[u + 2].start()
        copies[u].wait()
        projected[:, u * width : (u + 1) * width] = dot(first_normed[...], whole_unit(held[u])).astype(
            jnp.bfloat16
        )
    projected.ship()
    for operand in (*made, memory, cross_cap):
        operand.start()
    for copy in copies[5:]:
        copy.start()
    attend_forward(
        projected, projected, projected, (0, width, 2 * width), self_cap, first_weights, first_scales, first_mixed
    )
    copies[3].wait()
    first_branch[...] = dot(first_mixed[...], whole_unit(held[3]))
    first_branch.ship()
    adapted, first_squeezed[...] = adapter_forward(first_branch[...], 0, *made)
    first_squeezed.ship()
    wide = tokens[...].astype(jnp.float32) + adapted
    stream[...] = wide
    stream.ship()
    normed[...] = (wide * rms_rate(wide) * gains[1:2]).astype(jnp.bfloat16)
    normed.ship()
    copies[4].wait()
    query[...] = dot(normed[...], whole_unit(held[4])).astype(jnp.bfloat16)
    query.ship()
    for u in range(2):
        copies[5 + u].wait()
        keyval[:, u * width : (u + 1) * width] = dot(memory[...], whole_unit(held[5 + u])).astype(
            jnp.bfloat16
        )
    keyval.ship()
    attend_forward(query, keyval, keyval, (0, 0, width), cross_cap, weights, scales, mixed)
    copies[7].wait()
    branch[...] = dot(mixed[...], whole_unit(held[7]))
    branch.ship()
    adapted, squeezed[...] = adapter_forward(branch[...], 1, *made)
    result[...] = stream[...] + adapted


def feed_kernel(
    place, stream, gains, packed, tasks, cond, down, up, mask, out_grad,
    result, grad_stream, grad_down, grad_up, grad_cond, grad_gain, *rest,
):
    made = (tasks, cond, down, up, mask)
    outs, (held_in, held_out, normed, before, active, grad_branch, total, sems) = rest[:-8], rest[-8:]
    ahead, outs = outs[: len(outs) // 2], outs[len(outs) // 2 :]
    units = active.shape[0]

    def start(u):
        unit_copy(packed, 8, held_in, sems, u).start()
        rows_copy(packed, held_out, sems, u).start()

    start(0)
    wide = stream[...]
    normed[...] = (wide * rms_rate(wide) * gains[2:3]).astype(jnp.bfloat16)
    total[...] = jnp.zeros_like(total)
    for u in range(units):
        if u + 1 < units:
            start(u + 1)
        else:
            for operand in (*made, out_grad):
                operand.start()
        unit_copy(packed, 8, held_in, sems, u).wait()
        value = dot(normed[...], whole_unit(held_in[u]))
        before[u] = value
        active[u] = gelu(value).astype(jnp.bfloat16)
        rows_copy(packed, held_out, sems, u).wait()
        total[...] += dot(active[u], out_rows(held_out, u))
    branch = total[...]
    adapted, squeezed = adapter_forward(branch, 0, *made)
    result[...] = (stream[...] + adapted).astype(jnp.bfloat16)
    result.ship()
    grad_branch[...] = adapter_backward(
        branch, squeezed, 0, *made, out_grad[...].astype(jnp.float32), (grad_down, grad_up, grad_cond)
    ).astype(jnp.bfloat16)
    for out in (grad_down, grad_up, grad_cond):
        out.ship()
    half = active.shape[2] // 2

    def row_part(ref, j):
        if len(outs) == 1:
            return ref.at[0, 0, j // 2, pl.ds((j & 1) * half, half)]
        return ref.at[:, (j & 1) ^ place[1], (j // 2 - place[0]) & 3]

    for j in range(2 * units):
        columns = slice((j & 1) * half, (j & 1) * half + half)
        grad = dot_tn(active[j // 2, :, columns], grad_branch[...]).astype(jnp.bfloat16)
        if len(outs) == 1:
            ahead[0][0, 0, j // 2, columns] = grad
        else:
            rows = outs[0].shape[-2]
            for u in range(4):
                emit_block(
                    place, ahead, u, j,
                    grad[u * rows : (u + 1) * rows], grad[(4 + u) * rows : (5 + u) * rows],
                )
        for out in ahead:
            out.leave(j, row_part)
    total[...] = jnp.zeros_like(total)
    for u in range(units):
        grad = dot_nt(grad_branch[...], out_rows(held_out, u))
        grad = (grad * gelu_back(before[u])).astype(jnp.bfloat16)
        emit(place, outs, u, dot_tn(normed[...], grad))
        total[...] += dot_nt(grad, whole_unit(held_in[u]))
    wide = stream[...]
    grad, gain_rows = rms_back(wide, rms_rate(wide), gains[2:3], total[...])
    grad_stream[...] = out_grad[...].astype(jnp.float32) + grad
    grad_gain[...] = jnp.sum(gain_rows, axis=0, keepdims=True)


def branch_kernel(unit, place, grad_result, packed, squeezed, branch, tasks, cond, down, up, mask, *rest):
    *rest, held, sems = rest
    (copy,) = load_units(packed, unit, held, sems)
    others = 12 if len(rest) > 5 else 0
    others, (grad_branch, grad_mixed, *found) = rest[:others], rest[others:]
    low = grad_result[...]
    for operand in others[6:]:
        operand.start()
    grad_branch[...] = adapter_backward(
        branch[...], squeezed[...], 0, tasks, cond, down, up, mask, low, found[:3]
    ).astype(jnp.bfloat16)
    for out in (grad_branch, *found[:3]):
        out.ship()
    copy.wait()
    grad_mixed[...] = dot_nt(grad_branch[...], whole_unit(held[0])).astype(jnp.bfloat16)
    grad_mixed.ship()
    if others:
        emit_made(place, [found[:3], others[:3], others[3:6]], found[3:5], found[-1])
        own, sent, *parts = found[5:-1]
        half = others[6].shape[-1]
        pairs = [(z, u, (z, u // 2, slice(None), slice((u & 1) * half, (u & 1) * half + half)))
                 for z in range(4) for u in range(others[6].shape[2])]
        for z, u, at in pairs:
            sent[at] = low_sum(*(part[1, z, u] for part in others[6:9]))
        sent.ship()
        for z in range(4):
            parts[z][...] = low_sum(*(part[z] for part in others[9:]))
            parts[z].ship()
        for z, u, at in pairs:
            own[at] = low_sum(*(part[0, z, u] for part in others[6:9]))


def low_sum(*parts):
    total = parts[0].astype(jnp.float32)
    for part in parts[1:]:
        total = total + part.astype(jnp.float32)
    return total.astype(jnp.bfloat16)


def first_sums(kept_cross, got_cross, other_cross, kept_made, got_made, own_out, other_y, sent_cross, *parts):
    units = own_out.shape[1]
    for z in range(4):
        parts[z][:2] = low_sum(kept_made[z], got_made[z], other_y[z, units:])
        parts[z][2:] = low_sum(own_out[z], other_y[z, :units])
        parts[z].ship()
    for z in range(4):
        sent_cross[z] = low_sum(kept_cross[z], got_cross[z], other_cross[z])


def kept_sums(kept, got, other, *rest):
    for z in range(4):
        rest[-1][z] = low_sum(kept[z], got[z], other[z])
    if len(rest) > 1:
        rest[-2][...] = low_sum(*(ref[...] for ref in rest[:4]))


def second_sums(*refs):
    total_in, kept_self, got_self, other_self, own_cross, other_cross = refs[4:10]
    gains, totals, made, sent_self, *parts = refs[10:]
    for z in range(4):
        sent_self[z] = low_sum(kept_self[z], got_self[z], other_self[z])
    sent_self.ship()
    made[:2] = low_sum(*(ref[:2] for ref in refs[:4]))
    rows = gains.shape[0]
    below = jnp.zeros((made.shape[1] - rows, made.shape[2]), jnp.float32)
    made[2] = jnp.concatenate([gains[...], below], axis=0).astype(jnp.bfloat16)
    made.ship()
    for z in range(4):
        parts[z][...] = low_sum(own_cross[z], other_cross[z])
        parts[z].ship()
    units = total_in.shape[0]
    totals[units:] = low_sum(*(ref[2:] for ref in refs[:4]))
    totals[:units] = total_in[...]


def join(place, own, other, out, rows, column):
    own, other = own.astype(jnp.float32), other.astype(jnp.float32)
    half = own.shape[-1]
    out[rows, column : column + half] = jnp.where(place[3] == 0, own, other)
    out[rows, column + half : column + 2 * half] = jnp.where(place[3] == 0, other, own)


def out_kernel(
    place, total, other, total_self, other_self,
    out_in, out_out, *outs,
):
    wide = total.shape[-1]
    units, rows, half = out_in.shape[1] // wide, out_in.shape[0], wide // 2
    for u in range(units):
        out_in[:, u * wide : (u + 1) * wide] = total[u].astype(jnp.float32) + other[u].astype(jnp.float32)
    out_in.ship()

    def pair(ref, first, u):
        return ref[first + u // 2, :, (u & 1) * half : (u & 1) * half + half]

    for u in range(units):
        join(place, pair(total, units, u), pair(other, units, u), out_out, slice(u * rows, (u + 1) * rows), 0)
    out_out.ship()
    first = units + units // 2
    columns = [(pair(total, first, u), pair(other, first, u)) for u in range(4)]
    columns += [(total_self[u], other_self[u]) for u in range(4)]
    for out in outs:
        for column in range(0, out.shape[1], wide):
            join(place, *columns.pop(0), out, slice(None), column)
        out.ship()


def third_sums(*refs):
    own_self, other_self, totals, both, *parts = refs[4:]
    for z in range(4):
        parts[z][...] = low_sum(own_self[z], other_self[z])
        parts[z].ship()
    count, half = totals.shape[0], own_self.shape[-1]
    for u in range(4):
        at = (count + u // 2, slice(None), slice((u & 1) * half, (u & 1) * half + half))
        both[at] = low_sum(*(ref[u] for ref in refs[:4]))
    both[:count] = totals[...]


def emit_made(place, made, outs, block):
    rows, wide = outs[0].shape[3], block.shape[2]
    piece, span = wide // 2, wide // 3
    block[...] = jnp.zeros_like(block)
    cond = jnp.concatenate([part[2][...] for part in made], axis=1)
    columns = cond.shape[1] // 16
    for j in range(8):
        for core in (0, 1):
            for slot in range(3):
                at = 3 * (2 * j + core) + slot
                part = made[at // 16][0][(at % 16) * rows : (at % 16 + 1) * rows]
                block[core, :, slot * span : slot * span + part.shape[1]] = part.astype(jnp.float32)
        emit_block(place, outs, 0, j, *(block[core].astype(jnp.bfloat16) for core in (0, 1)))
    for out in outs:
        out.leave(0, functools.partial(unit_part, place))
    block[...] = jnp.zeros_like(block)
    for j in range(8):
        for core in (0, 1):
            owner = 2 * j + core
            for slot in range(9):
                at = 9 * owner + slot
                row, half = (at % 48) // 2, at % 2
                part = made[at // 48][1][row * 8 : row * 8 + 8, half * piece : (half + 1) * piece]
                block[core, slot // 2 * 8 : slot // 2 * 8 + 8, slot % 2 * piece : (slot % 2 + 1) * piece] = part
            turned = pltpu.roll(cond, (cond.shape[1] - owner * columns) % cond.shape[1], 1)
            block[core, 40:48, :span] = turned[:, :span]
        emit_block(place, outs, 1, j, *(block[core].astype(jnp.bfloat16) for core in (0, 1)))
    for out in outs:
        out.leave(1, functools.partial(unit_part, place))


def cross_kernel(
    place, grad_mixed, packed, query, keyval, weights, scales, mixed, grad_branch, normed, memory, stream, gains, grad_result,
    grad_stream, grad_memory, grad_gain, *rest,
):
    outs, (held, grad_query, grad_keyval, sems) = rest[:-4], rest[-4:]
    copies = [unit_copy(packed, 4, held, sems, u) for u in range(3)]
    width = stream.shape[1]

    def beside():
        for copy in (mixed, grad_branch, normed, memory, *copies, stream, gains, grad_result):
            copy.start()

    attend_backward(
        query, keyval, keyval, (0, 0, width), weights, scales, grad_mixed,
        (grad_query, grad_keyval, grad_keyval), (0, 0, width), beside,
    )
    emit(place, outs, 3, dot_tn(mixed[...], grad_branch[...]))
    emit(place, outs, 0, dot_tn(normed[...], grad_query[...]))
    for copy in copies:
        copy.wait()
    for u in range(2):
        grad = grad_keyval[:, u * width : (u + 1) * width]
        emit(place, outs, 1 + u, dot_tn(memory[...], grad))
        if u == 0:
            grad_memory[...] = dot_nt(grad, whole_unit(held[1 + u]))
        else:
            grad_memory[...] += dot_nt(grad, whole_unit(held[1 + u]))
    grad_memory.ship()
    wide = stream[...]
    grad, gain_rows = rms_back(
        wide, rms_rate(wide), gains[1:2], dot_nt(grad_query[...], whole_unit(held[0]))
    )
    grad_stream[...] = grad_result[...] + grad
    grad_gain[...] = jnp.sum(gain_rows, axis=0, keepdims=True)


def self_kernel(
    place, grad_mixed, packed, projected, weights, scales, mixed, grad_branch, normed, tokens, gains, grad_stream,
    grad_tokens, grad_gain, *rest,
):
    outs, (held, grad_projected, total, sems) = rest[:-4], rest[-4:]
    copies = [unit_copy(packed, 0, held, sems, u) for u in range(3)]
    width = tokens.shape[1]

    def beside():
        for copy in (mixed, grad_branch, normed, *copies, tokens, gains, grad_stream):
            copy.start()

    attend_backward(
        projected, projected, projected, (0, width, 2 * width), weights, scales, grad_mixed,
        (grad_projected,) * 3, (0, width, 2 * width), beside,
    )
    emit(place, outs, 3, dot_tn(mixed[...], grad_branch[...]))
    for u in range(3):
        copies[u].wait()
        grad = grad_projected[:, u * width : (u + 1) * width]
        emit(place, outs, u, dot_tn(normed[...], grad))
        if u == 0:
            total[...] = dot_nt(grad, whole_unit(held[u]))
        else:
            total[...] += dot_nt(grad, whole_unit(held[u]))
    wide = tokens[...].astype(jnp.float32)
    grad, gain_rows = rms_back(wide, rms_rate(wide), gains[0:1], total[...])
    grad_tokens[...] = grad_stream[...] + grad
    grad_gain[...] = jnp.sum(gain_rows, axis=0, keepdims=True)


def pack_kernel(*refs):
    shards, packed = refs[:-1], refs[-1]
    rows, width = packed.shape[1:]
    unit = 0
    for shard in shards:
        for row in range(0, shard.shape[0], rows):
            for column in range(0, shard.shape[1], width):
                packed[unit] = shard[row : row + rows, column : column + width]
                unit += 1


def sum_kernel(*refs):
    refs[-1][...] = low_sum(*(ref[...] for ref in refs[:-1]))


def swap(values, axis, count, mate):
    return lax.ppermute(values, axis, [(i, mate(i)) for i in range(count)])


def place_parts():
    place = lax.axis_index("fsdp")
    return place // 4, (place // 2) % 2, place % 2


def ring_gather(block):
    z, y, core = place_parts()
    shifted = [swap(block, "fsdp", 16, lambda i, d=d: (i + 4 * d) % 16) for d in (3, 2, 1)]
    line = jnp.stack(shifted[:1] + shifted[1:] + [block])
    line = lax.dynamic_slice_in_dim(jnp.concatenate([line, line]), 3 - z, 4, 0)
    other = swap(line, "fsdp", 16, lambda i: i ^ 2)
    both = jnp.stack([jnp.where(y == 0, line, other), jnp.where(y == 0, other, line)], axis=1)
    other = swap(both, "fsdp", 16, lambda i: i ^ 1)
    whole = jnp.stack([jnp.where(core == 0, both, other), jnp.where(core == 0, other, both)], axis=2)
    return whole.reshape((16,) + block.shape)


def add_low(left, right):
    return (left.astype(jnp.float32) + right.astype(jnp.float32)).astype(jnp.bfloat16)


def core_swap(sent):
    return swap(sent, "fsdp", 16, lambda i: i ^ 1)


def y_swap(sent):
    return swap(sent, "fsdp", 16, lambda i: i ^ 2)


def x_swap(sent):
    return swap(sent, "dp", 2, lambda i: i ^ 1)


def z_swaps(parts):
    return [swap(parts[d], "fsdp", 16, lambda i, d=d: (i + 4 * d) % 16) for d in (1, 2, 3)]


def both_halves(own, other, first_x):
    return jnp.concatenate([jnp.where(first_x, own, other), jnp.where(first_x, other, own)], axis=-1)


def after(values, *others):
    return lax.optimization_barrier((values, others))[0]


def ring_step(values, bit):
    return values + swap(values, "fsdp", 16, lambda i: i ^ bit)


def gather_shards(block, ring):
    return ring_gather(block) if ring else lax.all_gather(block, "fsdp", axis=0)


def block_share(blocks):
    part = lax.psum_scatter(blocks, "fsdp", scatter_dimension=0, tiled=False)
    return lax.psum(part.astype(jnp.float32), "dp")


def share_of(grads, devices, by_rows):
    whole = grads[0][0, 0]
    count, width = whole.shape[0], whole.shape[-1]
    if by_rows:
        return block_share(whole.reshape(devices, count, -1, width))
    blocks = jnp.transpose(whole.reshape(count, devices, -1, width), (1, 0, 2, 3))
    return block_share(blocks)


def sum_shards(values, ring):
    return ring_sum(values) if ring else lax.psum(values, "fsdp")


def units_of(shard, width):
    rows, columns = shard.shape
    return jnp.transpose(shard.reshape(rows, columns // width, width), (1, 0, 2))


def joined(units):
    return jnp.transpose(units, (1, 0, 2)).reshape(units.shape[1], -1)


def view_shape(shape, view):
    return tuple(at.size for at in view if not isinstance(at, int)) + tuple(shape[len(view) :])


def call(kernel, operands, shapes, scratch, flops, raw=(), split=None, parts=None, later=(), views=None):
    split, parts, views = split or {}, parts or {}, views or {}
    scalars = operands[0].ndim == 1
    moved_in = [i for i in range(int(scalars), len(operands)) if i not in raw]
    specs = [pl.BlockSpec(memory_space=pl.ANY) for _ in operands]
    if scalars:
        specs[0] = pl.BlockSpec(memory_space=pltpu.SMEM)
    outs = [jax.ShapeDtypeStruct(shape, dtype) for shape, dtype in shapes]
    buffers = [pltpu.VMEM(view_shape(operands[i].shape, views.get(i, ())), operands[i].dtype) for i in moved_in]
    buffers += [pltpu.VMEM(shape, dtype) for shape, dtype in shapes]
    buffers += [pltpu.SemaphoreType.DMA((split.get(i, 1),)) for i in moved_in]
    buffers += [pltpu.SemaphoreType.DMA((parts.get(k, 1),)) for k in range(len(outs))]

    def body(*refs):
        ins, results = list(refs[: len(operands)]), refs[len(operands) : len(operands) + len(outs)]
        own = refs[len(operands) + len(outs) : len(refs) - len(buffers)]
        held = refs[len(refs) - len(buffers) :]
        held, sems = held[: len(buffers) // 2], held[len(buffers) // 2 :]
        for k, i in enumerate(moved_in):
            source = ins[i].at[views[i]] if i in views else ins[i]
            ins[i] = Fetched(source, held[k], sems[k], split.get(i, 1))
            if i not in later:
                ins[i].start()
        results = [
            Shipped(target, *rest) for target, *rest in zip(results, held[len(moved_in) :], sems[len(moved_in) :])
        ]
        kernel(*ins, *results, *own)
        for operand in ins:
            ready(operand)
        for result in results:
            result.settle()

    moved = sum(math.prod(shape) * jnp.dtype(dtype).itemsize for shape, dtype in shapes)
    moved += sum(operand.size * operand.dtype.itemsize for operand in operands)
    return pl.pallas_call(
        body,
        out_shape=outs,
        in_specs=specs,
        out_specs=[pl.BlockSpec(memory_space=pl.ANY) for _ in outs],
        scratch_shapes=list(scratch) + buffers,
        compiler_params=pltpu.CompilerParams(vmem_limit_bytes=60 * 1024 * 1024),
        cost_estimate=pl.CostEstimate(flops=flops, bytes_accessed=moved, transcendentals=0),
    )(*operands)


def per_device(
    devices,
    ring,
    tokens,
    memory,
    out_grad,
    target_len,
    source_len,
    task_ids,
    norm_gains,
    self_qkv,
    self_out,
    cross_query,
    cross_keyval,
    cross_out,
    feed_in,
    feed_out,
    task_table,
    hyper_in,
    maker_down,
    maker_up,
    maker_norm,
):
    width = tokens.shape[1]
    tasks = task_table.shape[0]
    embed = hyper_in.shape[0]
    table_width = task_table.shape[1]
    hyper_width = hyper_in.shape[1]
    gain_width = norm_gains.shape[1]
    down_span = maker_down.shape[1]
    norm_span = maker_norm.shape[1]
    bottleneck = down_span * devices // (3 * width)
    down_rows = 3 * width // devices
    unit = width // devices
    ff_units = feed_in.shape[1] // width
    small = jnp.concatenate(
        [
            jnp.pad(task_table.T, ((0, 0), (0, 128 - tasks))),
            jnp.pad(hyper_in.T, ((0, 0), (0, 128 - embed))),
            jnp.pad(norm_gains, ((0, 0), (0, 128 - gain_width))),
            jnp.zeros((-(table_width + hyper_width + 3) % 16, 128), jnp.bfloat16),
        ]
    )
    small = gather_shards(small, ring)
    whole_table = small[:, :table_width, :tasks].reshape(-1, tasks).T
    whole_hyper = small[:, table_width : table_width + hyper_width, :embed].reshape(-1, embed).T
    first = table_width + hyper_width
    whole_gains = jnp.transpose(small[:, first : first + 3, :gain_width], (1, 0, 2)).reshape(3, width)
    layer = [self_qkv, self_out, cross_query, cross_keyval, cross_out, feed_in]
    if ring:
        shape = ((8 + 2 * ff_units, unit, width), jnp.bfloat16)
        (packed,) = call(pack_kernel, (*layer, feed_out), [shape], [], 1)
        packed = packed.reshape(-1, width)
    else:
        layer = [units_of(w, width) for w in layer] + [feed_out.reshape(ff_units, unit, width)]
        packed = jnp.concatenate([w.reshape(-1, width) for w in layer])
    packed = lax.all_gather(packed, "fsdp", axis=0).reshape(devices, -1, unit, width)
    if not ring:
        first = jnp.transpose(packed[:, : 8 + ff_units], (1, 0, 2, 3)).reshape(-1, width, width)
        last = packed[:, 8 + ff_units :].reshape(-1, width, width)
        packed = jnp.concatenate([first, last])[None]
    pre_hidden = matmul(whole_table, whole_hyper)
    hidden = jax.nn.silu(pre_hidden).astype(jnp.bfloat16)
    own_down = matmul(hidden, maker_down).astype(jnp.bfloat16)
    own_up = matmul(hidden, maker_up).astype(jnp.bfloat16)
    own_norm = matmul(hidden, maker_norm).astype(jnp.bfloat16)
    span = tasks * bottleneck
    own_down = jnp.transpose(own_down.reshape(tasks, down_rows, bottleneck), (1, 2, 0)).reshape(-1, span)
    if ring:
        third, piece = width // 3, width // 2
        own_down = jnp.pad(own_down.reshape(3, unit, span), ((0, 0), (0, 0), (0, third - span)))
        own_down = jnp.transpose(own_down, (1, 0, 2)).reshape(unit, width)
        own_up = jnp.pad(own_up, ((0, 0), (0, 10 * piece - down_span))).reshape(tasks, 5, width)
        own_up = jnp.transpose(own_up, (1, 0, 2)).reshape(5 * tasks, width)
        own_norm = jnp.pad(own_norm, ((0, 0), (0, width - norm_span)))
        made = jnp.concatenate([own_down, own_up, own_norm])
        first_x = lax.axis_index("dp") == 0
        made = ring_gather(jnp.where(first_x, made[:, : width // 2], made[:, width // 2 :]))
        made = both_halves(made, x_swap(made), first_x)
        made_down = made[:, :unit].reshape(devices, unit, 3, third)[..., :span]
        made_down = jnp.transpose(made_down, (0, 2, 1, 3)).reshape(3, width, span)
        made_up = made[:, unit : unit + 5 * tasks].reshape(devices, 5, tasks, 2, piece)
        made_up = jnp.transpose(made_up, (0, 1, 3, 2, 4)).reshape(devices, 10, tasks, piece)[:, :9]
        made_up = jnp.transpose(made_up.reshape(3, bottleneck, 2, tasks, piece), (0, 1, 3, 2, 4))
        made_up = made_up.reshape(3, span, width)
        made_cond = made[:, unit + 5 * tasks :, :norm_span]
    else:
        made_down = lax.all_gather(own_down, "fsdp", axis=0, tiled=True).reshape(3, width, span)
        made_up = lax.all_gather(own_up, "fsdp", axis=1, tiled=True).reshape(tasks, 3, bottleneck, width)
        made_up = jnp.transpose(made_up, (1, 2, 0, 3)).reshape(3, span, width)
        made_cond = lax.all_gather(own_norm, "fsdp", axis=0)
    made_cond = jnp.transpose(made_cond, (1, 0, 2)).reshape(tasks, 3, width)
    made_cond = jnp.pad(jnp.transpose(made_cond, (1, 0, 2)), ((0, 0), (0, 128 - tasks), (0, 0)))
    tok_seg = segment_rows(target_len[0], tokens.shape[0])
    mem_seg = segment_rows(source_len[0], memory.shape[0])
    sequences = jnp.arange(target_len.shape[1], dtype=jnp.int32)
    row_task = jnp.sum(
        jnp.where(tok_seg[:, None] == sequences[None, :], task_ids[0][None, :], 0), axis=1
    )
    onehot = (row_task[:, None] == jnp.arange(128, dtype=jnp.int32)[None, :]).astype(jnp.bfloat16)
    mask = jnp.tile(onehot[:, :tasks], (1, bottleneck))
    places = jnp.arange(tokens.shape[0], dtype=jnp.int32)
    self_allowed = (tok_seg[:, None] == tok_seg[None, :]) & (places[:, None] <= places[None, :])
    cross_allowed = mem_seg[:, None] == tok_seg[None, :]
    self_cap = jnp.where(self_allowed, -masked_score * 1e20, masked_score).astype(jnp.float32)
    cross_cap = jnp.where(cross_allowed, -masked_score * 1e20, masked_score).astype(jnp.float32)
    gains = jnp.pad(whole_gains.astype(jnp.float32), ((0, 5), (0, 0)))
    place = lax.axis_index("fsdp")
    here = jnp.stack([place // 4, (place // 2) % 2, place % 2, lax.axis_index("dp")]).astype(jnp.int32)
    adapters = (onehot, made_cond, made_down, made_up, mask)
    rows, memory_rows = tokens.shape[0], memory.shape[0]
    pairs = width // 128
    low, full = jnp.bfloat16, jnp.float32
    held_unit = packed.shape[:1] + packed.shape[2:]

    def held(count):
        return pltpu.VMEM((count,) + held_unit, low)

    def grad_shapes(count, by_x=False):
        if ring and by_x:
            return [((2, 2, 4, count, unit, width // 2), low)] * 2
        if ring:
            return [((2, 4, count, unit, width), low)] * 2
        return [((1, 1, count, width, width), low)]

    made_shapes = [((width, span), low), ((span, width), full), ((tasks, width), full)]
    gain_shape = [((1, width), full)]
    busy = 1700000000
    scale_shape = ((pairs, 1, 2 * rows), full)
    float_rows, low_rows = ((rows, width), full), ((rows, width), low)
    found = call(
        attention_kernel,
        (tokens, gains, packed, self_cap) + adapters + (memory, cross_cap),
        [low_rows, ((rows, 3 * width), low), ((pairs, rows, 2 * rows), low), scale_shape, low_rows, float_rows]
        + [((rows, span), full), float_rows, low_rows, low_rows, ((memory_rows, 2 * width), low)]
        + [((pairs, memory_rows, 2 * rows), low), scale_shape, low_rows, float_rows]
        + [((rows, span), full), float_rows],
        [held(8), pltpu.SemaphoreType.DMA((8,))],
        37 * busy,
        raw=(2,),
        parts={2: pairs, 11: pairs},
        later=(4, 5, 6, 7, 8, 9, 10),
    )
    normed1, projected, weights1, scales1, mixed1, branch1, squeezed1, stream1, *found = found
    normed2, query2, keyval2, weights2, scales2, mixed2, branch2, squeezed2, stream2 = found
    held_out = (packed.shape[0], ff_units) + packed.shape[2:]
    sets = 2 if ring else 1
    result, grad_stream, *found = call(
        feed_kernel,
        (here, stream2, gains, packed) + adapters + (out_grad,),
        [low_rows, float_rows] + made_shapes + gain_shape + grad_shapes(ff_units, True) + grad_shapes(ff_units),
        [
            held(ff_units),
            pltpu.VMEM(held_out, low),
            pltpu.VMEM((rows, width), low),
            pltpu.VMEM((ff_units, rows, width), full),
            pltpu.VMEM((ff_units, rows, width), low),
            pltpu.VMEM((rows, width), low),
            pltpu.VMEM((rows, width), full),
            pltpu.SemaphoreType.DMA((2 * ff_units,)),
        ],
        36 * busy,
        raw=(3,),
        parts={6 + k: (2 if k < sets else 1) * ff_units for k in range(2 * sets)},
        later=(4, 5, 6, 7, 8, 9),
        views=dict.fromkeys((5, 6, 7), (pl.ds(2, 1),)),
    )
    made_three, grad_gain_three, grads_out, grads_in = found[:3], found[3], found[4 : 4 + sets], found[4 + sets :]

    def branch_back(index, unit_at, grad_result, branch, squeezed, others, shapes):
        return call(
            functools.partial(branch_kernel, unit_at),
            (here, grad_result, packed, squeezed, branch) + adapters + others,
            [low_rows] * 2 + made_shapes + shapes,
            [pltpu.VMEM((2, unit, width), full)] * int(bool(others)) + [held(1), pltpu.SemaphoreType.DMA((1,))],
            30 * busy,
            raw=(2,),
            parts={5: 2, 6: 2} if others else {},
            later=tuple(range(16, 22)) if others else (),
            views=dict.fromkeys((6, 7, 8), (pl.ds(index, 1),))
            | (dict.fromkeys((16, 17, 19, 20), (0,)) if others else {}),
        )

    if ring:
        got_out, got_in = core_swap(grads_out[0]), core_swap(grads_in[0])
    grad_branch, grad_mixed, *made_two = branch_back(1, 7, grad_stream, branch2, squeezed2, (), [])
    if ring:
        got_out, got_in = after((got_out, got_in), grad_mixed)
        sent_out, sent_in = (add_low(kept[1], got[1]) for (_, kept), got in ((grads_out, got_out), (grads_in, got_in)))
        other_out, other_in = x_swap(sent_out), y_swap(sent_in)
        grad_mixed = after(grad_mixed, sent_out, sent_in)
    grad_stream, grad_memory, grad_gain_two, *grads_cross = call(
        cross_kernel,
        (here, grad_mixed, packed, query2, keyval2, weights2, scales2, mixed2, grad_branch, normed2)
        + (memory, stream1, gains, grad_stream),
        [float_rows, ((memory_rows, width), full)] + gain_shape + grad_shapes(4, True),
        [
            held(3),
            pltpu.VMEM((rows, width), low),
            pltpu.VMEM((memory_rows, 2 * width), low),
            pltpu.SemaphoreType.DMA((3,)),
        ],
        24 * busy,
        raw=(2,),
        split={5: pairs},
        parts={3: 4, 4: 4},
        later=(5,) + tuple(range(7, 14)),
    )
    others, shapes = (), []
    if ring:
        got_cross = core_swap(grads_cross[0])
        others = (*made_two, *made_three, grads_out[1], got_out, other_out, grads_in[1], got_in, other_in)
        shapes = [((2, 4, 2, unit, width), low)] * 2
        shapes += [((4, ff_units // 2, unit, width), low)] * 2 + [((ff_units, unit, width), low)] * 4
    grad_branch, grad_mixed, *made_one = branch_back(0, 3, grad_stream, branch1, squeezed1, others, shapes)
    if ring:
        sent_made, kept_made, own_out, sent_out, *parts_in = made_one[3:]
        got_made = core_swap(sent_made)
        got_cross = after(got_cross, grad_mixed)
        sent_cross = add_low(grads_cross[1][1], got_cross[1])
        other_cross = x_swap(sent_cross)
        far_in = z_swaps(after(parts_in, sent_cross))
        sent_made = add_low(kept_made[1], after(got_made, sent_cross)[1])
        other_y = y_swap(jnp.concatenate([sent_out, sent_made], axis=1))
        grad_mixed = after(grad_mixed, sent_made)
    grad_tokens, grad_gain_one, *grads_self = call(
        self_kernel,
        (here, grad_mixed, packed, projected, weights1, scales1, mixed1, grad_branch, normed1, tokens, gains)
        + (grad_stream,),
        [float_rows] + gain_shape + grad_shapes(4, True),
        [
            held(3),
            pltpu.VMEM((rows, 3 * width), low),
            pltpu.VMEM((rows, width), full),
            pltpu.SemaphoreType.DMA((3,)),
        ],
        busy,
        raw=(2,),
        split={4: pairs},
        parts={2: 4, 3: 4},
        later=(4,) + tuple(range(6, 12)),
    )

    def own_made(share):
        own_down = share[0].reshape(unit, 3, third)[:, :, :span]
        own_down = jnp.transpose(own_down, (1, 0, 2)).reshape(down_rows, bottleneck, tasks)
        own_down = jnp.transpose(own_down, (2, 0, 1)).reshape(tasks, down_span)
        own_up = share[1, : 5 * tasks].reshape(5, tasks, width)
        own_up = jnp.transpose(own_up, (1, 0, 2)).reshape(tasks, 5 * width)[:, :down_span]
        return own_down, own_up, share[1, 5 * tasks :, :norm_span]

    def hidden_of(own_down, own_up, own_norm):
        return (
            dot_nt(own_down.astype(jnp.bfloat16), maker_down)
            + dot_nt(own_up.astype(jnp.bfloat16), maker_up)
            + dot_nt(own_norm.astype(jnp.bfloat16), maker_norm)
        )

    grad_gains = jnp.concatenate([grad_gain_one, grad_gain_two, grad_gain_three])
    if ring:
        got_self = core_swap(grads_self[0])
        flight = (far_in, other_cross, other_y)
        far_in, other_cross, other_y = after(flight, grad_gain_one)
        halves_y, column_half = ((4, 4, unit, width // 2), low), ((4, unit, width // 2), low)
        whole_part = ((4, unit, width), low)
        sent_cross, *parts = call(
            first_sums,
            (grads_cross[1], got_cross, other_cross, kept_made, got_made, own_out, other_y),
            [halves_y] + [whole_part] * 4,
            [],
            100 * busy,
            views={0: (0, 1), 1: (0, 1), 2: (1,), 3: (0,), 4: (0,)},
        )
        sent_self = add_low(grads_self[1][1], after(got_self, sent_cross)[1])
        other_self = x_swap(sent_self)
        parts, sent_cross = after((parts, sent_cross), sent_self)
        far = z_swaps(parts)
        kept_cross, far_in = after((grads_cross[1], far_in), sent_self)
        total_in, own_cross = call(
            kept_sums,
            (kept_cross, got_cross, other_cross, parts_in[0], *far_in),
            [whole_part, halves_y],
            [],
            100 * busy,
            views={0: (0, 0), 1: (0, 0), 2: (0,)},
        )
        other_cross = y_swap(sent_cross)
        totals, total_made, sent_self, *parts = call(
            second_sums,
            (parts[0], *far, total_in, grads_self[1], got_self, other_self, own_cross, other_cross)
            + (grad_gains,),
            [((6, unit, width), low), ((3, unit, width), low), halves_y] + [column_half] * 4,
            [],
            5 * busy,
            views={5: (0, 1), 6: (0, 1), 7: (1,)},
        )
        other_made, far = x_swap(total_made), z_swaps(parts)
        (own_self,) = call(
            kept_sums,
            (after(grads_self[1], other_made), got_self, other_self),
            [halves_y],
            [],
            100 * busy,
            views={0: (0, 0), 1: (0, 0), 2: (0,)},
        )
        other_self = y_swap(sent_self)
        share_made = total_made.astype(jnp.float32) + other_made.astype(jnp.float32)
        own_down, own_up, own_norm = own_made(share_made[:2])
        sums = jnp.concatenate(
            [hidden_of(own_down, own_up, own_norm), share_made[2, :3].reshape(-1, 128)]
        )
        sums = ring_step(sums, 1)
        totals, *parts = call(
            third_sums,
            (parts[0], *far, own_self, other_self, totals),
            [((8, unit, width), low)] + [column_half] * 4,
            [],
            5 * busy,
        )
        other_totals, far = x_swap(totals), z_swaps(parts)
        sums = ring_step(after(sums, totals), 2)
        for part in z_swaps([sums] * 4):
            sums = sums + part
        far = after(far, sums)
        total_self = call(sum_kernel, (parts[0], *far), [column_half], [], 5 * busy)[0]
        other_self = x_swap(total_self)
        sums, own_down, own_up, own_norm = after((sums, own_down, own_up, own_norm), total_self)
        shapes = [((unit, ff_units * width), full), ((ff_units * unit, width), full)]
        shapes += [((unit, count * width), full) for count in (1, 2, 1, 3, 1)]
        out_feed_in, out_feed_out, out_query, out_keyval, out_cross_out, out_qkv, out_self_out = call(
            out_kernel, (here, totals, other_totals, total_self, other_self), shapes, [], busy
        )
    else:
        share_in, share_out, share_cross, share_self = (
            share_of(grads, devices, grads is grads_out)
            for grads in (grads_in, grads_out, grads_cross, grads_self)
        )
        made = (made_one, made_two, made_three)
        grad_down = jnp.concatenate([part[0] for part in made]).reshape(devices, -1)
        grad_up = jnp.stack([part[1] for part in made]).reshape(3, bottleneck, tasks, width)
        grad_up = jnp.transpose(grad_up, (2, 0, 1, 3)).reshape(tasks, devices, down_span)
        grad_norm = jnp.concatenate([part[2] for part in made], axis=1)
        grad_norm = grad_norm.reshape(tasks, devices, norm_span)
        blocks = [grad_down.astype(jnp.bfloat16)] + [
            jnp.transpose(part.astype(jnp.bfloat16), (1, 0, 2)).reshape(devices, -1)
            for part in (grad_up, grad_norm)
        ]
        out_feed_in, out_feed_out = joined(share_in), share_out.reshape(-1, width)
        out_query, out_keyval, out_cross_out = share_cross[0], joined(share_cross[1:3]), share_cross[3]
        out_qkv, out_self_out = joined(share_self[:3]), share_self[3]
        share_made = block_share(jnp.concatenate(blocks, axis=1))
        sizes = (0, tasks * down_span, 2 * tasks * down_span, share_made.shape[0])
        own_down, own_up, own_norm = (share_made[a:b] for a, b in zip(sizes, sizes[1:]))
        own_down = jnp.transpose(own_down.reshape(down_rows, bottleneck, tasks), (2, 0, 1))
        own_down, own_up = own_down.reshape(tasks, down_span), own_up.reshape(tasks, down_span)
        own_norm = own_norm.reshape(tasks, norm_span)
        sums = jnp.concatenate([hidden_of(own_down, own_up, own_norm), lax.psum(grad_gains, "dp").reshape(-1, 128)])
        sums = lax.psum(sums, "fsdp")
    grad_hidden = sums[:tasks]
    out_gains = lax.dynamic_slice_in_dim(
        sums[tasks:].reshape(3, width), place * gain_width, gain_width, 1
    )
    _, silu_pull = jax.vjp(jax.nn.silu, pre_hidden)
    grad_pre_hidden = silu_pull(grad_hidden)[0]
    own_hyper = lax.dynamic_slice_in_dim(whole_hyper, place * table_width, table_width, 0)
    out_table = exact_cols(grad_pre_hidden, own_hyper.astype(jnp.float32))
    own_pre = lax.dynamic_slice_in_dim(grad_pre_hidden, place * hyper_width, hyper_width, 1)
    out_hyper = exact_rows(whole_table.astype(jnp.float32), own_pre)
    out_down, out_up, out_norm = (
        dot_tn(hidden, own.astype(jnp.bfloat16)) for own in (own_down, own_up, own_norm)
    )
    return (
        result.astype(jnp.bfloat16),
        grad_tokens,
        grad_memory,
        out_gains,
        out_qkv,
        out_self_out,
        out_query,
        out_keyval,
        out_cross_out,
        out_feed_in,
        out_feed_out,
        out_table,
        out_hyper,
        out_down,
        out_up,
        out_norm,
    )


def solution(mesh):
    placed = (
        P(("fsdp", "dp"), None),
        P(("fsdp", "dp"), None),
        P(("fsdp", "dp"), None),
        P(("fsdp", "dp"), None),
        P(("fsdp", "dp"), None),
        P(("fsdp", "dp"), None),
        P(None, "fsdp"),
        P("fsdp", None),
        P("fsdp", None),
        P("fsdp", None),
        P("fsdp", None),
        P("fsdp", None),
        P("fsdp", None),
        P("fsdp", None),
        P(None, "fsdp"),
        P(None, "fsdp"),
        P(None, "fsdp"),
        P(None, "fsdp"),
        P(None, "fsdp"),
    )
    devices = mesh.shape["fsdp"]
    ring = devices == 16 and mesh.shape["dp"] == 2
    return jax.shard_map(
        functools.partial(per_device, devices, ring),
        mesh=mesh,
        in_specs=placed,
        out_specs=(
            P(("fsdp", "dp"), None),
            P(("fsdp", "dp"), None),
            P(("fsdp", "dp"), None),
            P(None, "fsdp"),
            P("fsdp", None),
            P("fsdp", None),
            P("fsdp", None),
            P("fsdp", None),
            P("fsdp", None),
            P("fsdp", None),
            P("fsdp", None),
            P(None, "fsdp"),
            P(None, "fsdp"),
            P(None, "fsdp"),
            P(None, "fsdp"),
            P(None, "fsdp"),
        ),
        check_vma=False,
    )
```

```python
import functools
import math

import jax
import jax.numpy as jnp
from jax import lax
from jax.experimental import pallas as pl
from jax.experimental.pallas import tpu as pltpu
from jax.sharding import PartitionSpec as P

norm_epsilon = 1e-06
masked_score = -1000000000.0
highest = lax.Precision.HIGHEST


def matmul(left, right):
    return jnp.dot(left, right, preferred_element_type=jnp.float32)


def exact_rows(left, right):
    return lax.dot_general(
        left, right, (((0,), (0,)), ((), ())), precision=highest, preferred_element_type=jnp.float32
    )


def exact_cols(left, right):
    return lax.dot_general(
        left, right, (((1,), (1,)), ((), ())), precision=highest, preferred_element_type=jnp.float32
    )


def segment_rows(lengths, count):
    ends = jnp.cumsum(lengths)
    places = jnp.arange(count, dtype=jnp.int32)
    return jnp.sum((places[:, None] >= ends[None, :]).astype(jnp.int32), axis=1)


def dot(left, right):
    return jnp.dot(left, right, preferred_element_type=jnp.float32)


def dot_nt(left, right):
    return lax.dot_general(
        left, right, (((1,), (1,)), ((), ())), preferred_element_type=jnp.float32
    )


def dot_tn(left, right):
    return lax.dot_general(
        left, right, (((0,), (0,)), ((), ())), preferred_element_type=jnp.float32
    )


def rms_rate(values):
    return lax.rsqrt(jnp.mean(values * values, axis=-1, keepdims=True) + norm_epsilon)


def rms_back(values, rate, gain, grad):
    scaled = grad * gain
    inner = jnp.mean(scaled * values, axis=-1, keepdims=True)
    return rate * (scaled - values * (rate * rate * inner)), grad * values * rate


gelu_slope = math.sqrt(2.0 / math.pi)
gelu_cube = 0.044715


def gelu(values):
    inner = gelu_slope * values * (1.0 + gelu_cube * values * values)
    return 0.5 * values * (1.0 + jnp.tanh(inner))


def gelu_back(values):
    square = values * values
    bent = jnp.tanh(gelu_slope * values * (1.0 + gelu_cube * square))
    slope = gelu_slope * (1.0 + 3.0 * gelu_cube * square)
    return 0.5 * (1.0 + bent) + 0.5 * values * (1.0 - bent * bent) * slope


def halves(dtype):
    lane = lax.broadcasted_iota(jnp.int32, (1, 128), 1)
    first = (lane < 64).astype(jnp.float32)
    return first.astype(dtype), (1.0 - first).astype(dtype)


def lanes(start):
    return pl.ds(pl.multiple_of(start, 128), 128)


class Fetched:
    def __init__(self, source, held, sems, count):
        self.source, self.held, self.sems, self.count = source, held, sems, count
        self.waiting, self.shape, self.started = count == 1, held.shape, False

    def start(self):
        if not self.started:
            for k in range(self.count):
                self.part(k).start()
        self.started = True

    def part(self, k):
        if self.count == 1:
            return pltpu.make_async_copy(self.source, self.held, self.sems.at[0])
        size = self.shape[0] // self.count
        at = pl.ds(k * size, size)
        return pltpu.make_async_copy(self.source.at[at], self.held.at[at], self.sems.at[k])

    def ready(self):
        self.start()
        if self.waiting:
            self.part(0).wait()
            self.waiting = False
        return self.held

    def __getitem__(self, at):
        return self.ready()[at]

    @property
    def at(self):
        return self.ready().at


class Shipped:
    def __init__(self, target, held, sems):
        self.target, self.held, self.sems = target, held, sems
        self.shape, self.parts = held.shape, None

    def __getitem__(self, at):
        return self.held[at]

    def __setitem__(self, at, values):
        self.held[at] = values

    @property
    def at(self):
        return self.held.at

    def copy(self, k, part):
        return pltpu.make_async_copy(part(self.held, k), part(self.target, k), self.sems.at[k])

    def ship(self):
        self.leave(0, lambda ref, k: ref)

    def leave(self, k, part):
        self.parts = part
        self.copy(k, part).start()

    def settle(self):
        if self.parts is None:
            self.ship()
        if self.sems.shape[0] == 1:
            self.copy(0, self.parts).wait()
        else:
            lax.fori_loop(0, self.sems.shape[0], lambda k, _: self.copy(k, self.parts).wait() or 0, 0)


def ready(*refs):
    return [ref.ready() if isinstance(ref, Fetched) else ref for ref in refs]


def sides(turned):
    none = jnp.zeros_like(turned[:64])
    return jnp.concatenate(
        [jnp.concatenate([turned[:64], none], axis=0), jnp.concatenate([none, turned[64:]], axis=0)], axis=1
    )


def own_sides(both):
    half = both.shape[1] // 2
    return jnp.concatenate([both[:64, :half], both[64:, half:]], axis=0)


def attend_forward(queries, keys, values, starts, cap, weights, scales, mixed):
    factor = math.log2(math.e) / 8.0
    queries, keys, values, cap = ready(queries, keys, values, cap)

    def pair(p, _):
        query, key, value = (
            ref[:, lanes(start + p * 128)] for ref, start in zip((queries, keys, values), starts)
        )
        limit = cap[...]
        scores = dot(key, sides(query.T)) * factor
        scores = jnp.minimum(scores, jnp.concatenate([limit, limit], axis=1))
        powers = jnp.exp2(scores - jnp.max(scores, axis=0, keepdims=True))
        scale = 1.0 / jnp.sum(powers, axis=0, keepdims=True)
        powers = powers.astype(jnp.bfloat16)
        weights[p] = powers
        weights.leave(p, one_pair)
        scales[p] = scale
        found = own_sides(dot(value.T, powers) * scale)
        mixed[:, lanes(p * 128)] = found.T.astype(jnp.bfloat16)
        return 0

    lax.fori_loop(0, mixed.shape[1] // 128, pair, 0, unroll=3)
    mixed.ship()
    scales.ship()


def one_pair(ref, k):
    return ref.at[k]


def attend_backward(queries, keys, values, starts, weights, scales, grad_mixed, grads, places, beside):
    marks = halves(jnp.bfloat16)
    pairs = grad_mixed.shape[1] // 128
    weights.started = True
    for p in (0, 1):
        weights.part(p).start()
    for p in range(pairs):
        query, key, value = (
            ref[:, start + p * 128 : start + p * 128 + 128]
            for ref, start in zip((queries, keys, values), starts)
        )
        scale = scales[p]
        grad = sides(grad_mixed[:, p * 128 : p * 128 + 128].T)
        grad = (grad.astype(jnp.float32) * scale).astype(jnp.bfloat16)
        if p == 1:
            beside()
        if p + 2 < pairs:
            weights.part(p + 2).start()
        weights.part(p).wait()
        powers = weights.held[p]
        wide = powers.astype(jnp.float32)
        product = wide * dot(value, grad)
        total = jnp.sum(product, axis=0, keepdims=True) * scale
        product = (product - wide * total).astype(jnp.bfloat16)
        query = jnp.concatenate([query * marks[0], query * marks[1]], axis=0)
        columns = [slice(place + p * 128, place + p * 128 + 128) for place in places]
        grads[2][:, columns[2]] = dot(powers, grad.T).astype(jnp.bfloat16)
        grads[1][:, columns[1]] = (dot(product, query) * 0.125).astype(jnp.bfloat16)
        grads[0][:, columns[0]] = (own_sides(dot(key.T, product)).T * 0.125).astype(jnp.bfloat16)


def adapter_forward(branch, index, tasks, cond, down, up, mask):
    gain = 1.0 + dot(tasks[...], cond[index])
    normed = (branch * rms_rate(branch) * gain).astype(jnp.bfloat16)
    squeezed = dot(normed, down[index]) * mask[...].astype(jnp.float32)
    return branch + dot(gelu(squeezed).astype(jnp.bfloat16), up[index]), squeezed


def adapter_backward(branch, squeezed, index, tasks, cond, down, up, mask, grad, outs):
    low = grad.astype(jnp.bfloat16)
    outs[1][...] = dot_tn(gelu(squeezed).astype(jnp.bfloat16), low)
    grad_squeezed = (gelu_back(squeezed) * dot_nt(low, up[index])).astype(jnp.bfloat16) * mask[...]
    gain = 1.0 + dot(tasks[...], cond[index])
    rate = rms_rate(branch)
    normed = (branch * rate * gain).astype(jnp.bfloat16)
    outs[0][...] = dot_tn(normed, grad_squeezed).astype(jnp.bfloat16)
    grad_branch, grad_gain = rms_back(branch, rate, gain, dot_nt(grad_squeezed, down[index]))
    outs[2][...] = dot_tn(tasks[...], grad_gain.astype(jnp.bfloat16))[: outs[2].shape[0]]
    return grad + grad_branch


def whole_unit(weight):
    return weight.reshape(-1, weight.shape[-1])


def unit_copy(packed, first, held, sems, u):
    return pltpu.make_async_copy(packed.at[:, first + u], held.at[u], sems.at[u])


def load_units(packed, first, held, sems):
    copies = [unit_copy(packed, first, held, sems, u) for u in range(held.shape[0])]
    for copy in copies:
        copy.start()
    return copies


def rows_copy(packed, held, sems, u):
    units = held.shape[1]
    if held.shape[0] == 1:
        return pltpu.make_async_copy(packed.at[:, 8 + units + u], held.at[:, u], sems.at[units + u])
    share = held.shape[0] // units
    at = pl.ds(u * share, share)
    return pltpu.make_async_copy(packed.at[at, 8 + units :], held.at[at], sems.at[units + u])


def out_rows(held, u):
    units = held.shape[1]
    if held.shape[0] == 1:
        return whole_unit(held[0, u])
    share = held.shape[0] // units
    return whole_unit(held[pl.ds(u * share, share)])


def emit(place, outs, unit, grad):
    if len(outs) == 1:
        outs[0][0, 0, unit] = grad.astype(jnp.bfloat16)
    else:
        rows = outs[0].shape[-2]
        grad = grad.astype(jnp.bfloat16)
        for j in range(8):
            even = grad[2 * j * rows : (2 * j + 1) * rows]
            odd = grad[(2 * j + 1) * rows : (2 * j + 2) * rows]
            emit_block(place, outs, unit, j, even, odd)
    for out in outs:
        out.leave(unit, functools.partial(unit_part, place))


def unit_part(place, ref, unit):
    return ref.at[:, :, :, unit] if len(ref.shape) == 6 else ref.at[:, :, unit]


def emit_block(place, outs, unit, j, even, odd):
    at = ((j & 1) ^ place[1], (j // 2 - place[0]) & 3, unit)
    for out, block in zip(outs, (jnp.where(place[2] == 0, odd, even), jnp.where(place[2] == 0, even, odd))):
        if len(out.shape) == 6:
            half = out.shape[5]
            for x in (0, 1):
                out[(x ^ place[3],) + at] = block[:, x * half : (x + 1) * half]
        else:
            out[at] = block


def attention_kernel(
    tokens, gains, packed, self_cap, tasks, cond, down, up, mask, memory, cross_cap,
    first_normed, projected, first_weights, first_scales, first_mixed, first_branch, first_squeezed, stream,
    normed, query, keyval, weights, scales, mixed, branch, squeezed, result,
    held, sems,
):
    made = (tasks, cond, down, up, mask)
    copies = [unit_copy(packed, 0, held, sems, u) for u in range(8)]
    copies[0].start()
    wide = tokens[...].astype(jnp.float32)
    first_normed[...] = (wide * rms_rate(wide) * gains[0:1]).astype(jnp.bfloat16)
    first_normed.ship()
    width = wide.shape[1]
    copies[1].start()
    for u in range(3):
        copies[u + 2].start()
        copies[u].wait()
        projected[:, u * width : (u + 1) * width] = dot(first_normed[...], whole_unit(held[u])).astype(
            jnp.bfloat16
        )
    projected.ship()
    for operand in (*made, memory, cross_cap):
        operand.start()
    for copy in copies[5:]:
        copy.start()
    attend_forward(
        projected, projected, projected, (0, width, 2 * width), self_cap, first_weights, first_scales, first_mixed
    )
    copies[3].wait()
    first_branch[...] = dot(first_mixed[...], whole_unit(held[3]))
    first_branch.ship()
    adapted, first_squeezed[...] = adapter_forward(first_branch[...], 0, *made)
    first_squeezed.ship()
    wide = tokens[...].astype(jnp.float32) + adapted
    stream[...] = wide
    stream.ship()
    normed[...] = (wide * rms_rate(wide) * gains[1:2]).astype(jnp.bfloat16)
    normed.ship()
    copies[4].wait()
    query[...] = dot(normed[...], whole_unit(held[4])).astype(jnp.bfloat16)
    query.ship()
    for u in range(2):
        copies[5 + u].wait()
        keyval[:, u * width : (u + 1) * width] = dot(memory[...], whole_unit(held[5 + u])).astype(
            jnp.bfloat16
        )
    keyval.ship()
    attend_forward(query, keyval, keyval, (0, 0, width), cross_cap, weights, scales, mixed)
    copies[7].wait()
    branch[...] = dot(mixed[...], whole_unit(held[7]))
    branch.ship()
    adapted, squeezed[...] = adapter_forward(branch[...], 1, *made)
    result[...] = stream[...] + adapted


def feed_kernel(
    place, stream, gains, packed, tasks, cond, down, up, mask, out_grad,
    result, grad_stream, grad_down, grad_up, grad_cond, grad_gain, *rest,
):
    made = (tasks, cond, down, up, mask)
    outs, (held_in, held_out, normed, before, active, grad_branch, total, sems) = rest[:-8], rest[-8:]
    ahead, outs = outs[: len(outs) // 2], outs[len(outs) // 2 :]
    units = active.shape[0]

    def start(u):
        unit_copy(packed, 8, held_in, sems, u).start()
        rows_copy(packed, held_out, sems, u).start()

    start(0)
    wide = stream[...]
    normed[...] = (wide * rms_rate(wide) * gains[2:3]).astype(jnp.bfloat16)
    total[...] = jnp.zeros_like(total)
    for u in range(units):
        if u + 1 < units:
            start(u + 1)
        else:
            for operand in (*made, out_grad):
                operand.start()
        unit_copy(packed, 8, held_in, sems, u).wait()
        value = dot(normed[...], whole_unit(held_in[u]))
        before[u] = value
        active[u] = gelu(value).astype(jnp.bfloat16)
        rows_copy(packed, held_out, sems, u).wait()
        total[...] += dot(active[u], out_rows(held_out, u))
    branch = total[...]
    adapted, squeezed = adapter_forward(branch, 0, *made)
    result[...] = (stream[...] + adapted).astype(jnp.bfloat16)
    result.ship()
    grad_branch[...] = adapter_backward(
        branch, squeezed, 0, *made, out_grad[...].astype(jnp.float32), (grad_down, grad_up, grad_cond)
    ).astype(jnp.bfloat16)
    for out in (grad_down, grad_up, grad_cond):
        out.ship()
    half = active.shape[2] // 2

    def row_part(ref, j):
        if len(outs) == 1:
            return ref.at[0, 0, j // 2, pl.ds((j & 1) * half, half)]
        return ref.at[:, (j & 1) ^ place[1], (j // 2 - place[0]) & 3]

    for j in range(2 * units):
        columns = slice((j & 1) * half, (j & 1) * half + half)
        grad = dot_tn(active[j // 2, :, columns], grad_branch[...]).astype(jnp.bfloat16)
        if len(outs) == 1:
            ahead[0][0, 0, j // 2, columns] = grad
        else:
            rows = outs[0].shape[-2]
            for u in range(4):
                emit_block(
                    place, ahead, u, j,
                    grad[u * rows : (u + 1) * rows], grad[(4 + u) * rows : (5 + u) * rows],
                )
        for out in ahead:
            out.leave(j, row_part)
    total[...] = jnp.zeros_like(total)
    for u in range(units):
        grad = dot_nt(grad_branch[...], out_rows(held_out, u))
        grad = (grad * gelu_back(before[u])).astype(jnp.bfloat16)
        emit(place, outs, u, dot_tn(normed[...], grad))
        total[...] += dot_nt(grad, whole_unit(held_in[u]))
    wide = stream[...]
    grad, gain_rows = rms_back(wide, rms_rate(wide), gains[2:3], total[...])
    grad_stream[...] = out_grad[...].astype(jnp.float32) + grad
    grad_gain[...] = jnp.sum(gain_rows, axis=0, keepdims=True)


def branch_kernel(unit, place, grad_result, packed, squeezed, branch, tasks, cond, down, up, mask, *rest):
    *rest, held, sems = rest
    (copy,) = load_units(packed, unit, held, sems)
    others = 12 if len(rest) > 5 else 0
    others, (grad_branch, grad_mixed, *found) = rest[:others], rest[others:]
    low = grad_result[...]
    for operand in others[6:]:
        operand.start()
    grad_branch[...] = adapter_backward(
        branch[...], squeezed[...], 0, tasks, cond, down, up, mask, low, found[:3]
    ).astype(jnp.bfloat16)
    for out in (grad_branch, *found[:3]):
        out.ship()
    copy.wait()
    grad_mixed[...] = dot_nt(grad_branch[...], whole_unit(held[0])).astype(jnp.bfloat16)
    grad_mixed.ship()
    if others:
        emit_made(place, [found[:3], others[:3], others[3:6]], found[3:5], found[-1])
        own, sent, *parts = found[5:-1]
        half = others[6].shape[-1]
        pairs = [(z, u, (z, u // 2, slice(None), slice((u & 1) * half, (u & 1) * half + half)))
                 for z in range(4) for u in range(others[6].shape[2])]
        for z, u, at in pairs:
            sent[at] = low_sum(*(part[1, z, u] for part in others[6:9]))
        sent.ship()
        for z in range(4):
            parts[z][...] = low_sum(*(part[z] for part in others[9:]))
            parts[z].ship()
        for z, u, at in pairs:
            own[at] = low_sum(*(part[0, z, u] for part in others[6:9]))


def low_sum(*parts):
    total = parts[0].astype(jnp.float32)
    for part in parts[1:]:
        total = total + part.astype(jnp.float32)
    return total.astype(jnp.bfloat16)


def first_sums(kept_cross, got_cross, other_cross, kept_made, got_made, own_out, other_y, sent_cross, *parts):
    units = own_out.shape[1]
    for z in range(4):
        parts[z][:2] = low_sum(kept_made[z], got_made[z], other_y[z, units:])
        parts[z][2:] = low_sum(own_out[z], other_y[z, :units])
        parts[z].ship()
    for z in range(4):
        sent_cross[z] = low_sum(kept_cross[z], got_cross[z], other_cross[z])


def kept_sums(kept, got, other, *rest):
    for z in range(4):
        rest[-1][z] = low_sum(kept[z], got[z], other[z])
    if len(rest) > 1:
        rest[-2][...] = low_sum(*(ref[...] for ref in rest[:4]))


def second_sums(*refs):
    total_in, kept_self, got_self, other_self, own_cross, other_cross = refs[4:10]
    gains, totals, made, sent_self, *parts = refs[10:]
    for z in range(4):
        sent_self[z] = low_sum(kept_self[z], got_self[z], other_self[z])
    sent_self.ship()
    made[:2] = low_sum(*(ref[:2] for ref in refs[:4]))
    rows = gains.shape[0]
    below = jnp.zeros((made.shape[1] - rows, made.shape[2]), jnp.float32)
    made[2] = jnp.concatenate([gains[...], below], axis=0).astype(jnp.bfloat16)
    made.ship()
    for z in range(4):
        parts[z][...] = low_sum(own_cross[z], other_cross[z])
        parts[z].ship()
    units = total_in.shape[0]
    totals[units:] = low_sum(*(ref[2:] for ref in refs[:4]))
    totals[:units] = total_in[...]


def join(place, own, other, out, rows, column):
    own, other = own.astype(jnp.float32), other.astype(jnp.float32)
    half = own.shape[-1]
    out[rows, column : column + half] = jnp.where(place[3] == 0, own, other)
    out[rows, column + half : column + 2 * half] = jnp.where(place[3] == 0, other, own)


def out_kernel(
    place, total, other, total_self, other_self,
    out_in, out_out, *outs,
):
    wide = total.shape[-1]
    units, rows, half = out_in.shape[1] // wide, out_in.shape[0], wide // 2
    for u in range(units):
        out_in[:, u * wide : (u + 1) * wide] = total[u].astype(jnp.float32) + other[u].astype(jnp.float32)
    out_in.ship()

    def pair(ref, first, u):
        return ref[first + u // 2, :, (u & 1) * half : (u & 1) * half + half]

    for u in range(units):
        join(place, pair(total, units, u), pair(other, units, u), out_out, slice(u * rows, (u + 1) * rows), 0)
    out_out.ship()
    first = units + units // 2
    columns = [(pair(total, first, u), pair(other, first, u)) for u in range(4)]
    columns += [(total_self[u], other_self[u]) for u in range(4)]
    for out in outs:
        for column in range(0, out.shape[1], wide):
            join(place, *columns.pop(0), out, slice(None), column)
        out.ship()


def third_sums(*refs):
    own_self, other_self, totals, both, *parts = refs[4:]
    for z in range(4):
        parts[z][...] = low_sum(own_self[z], other_self[z])
        parts[z].ship()
    count, half = totals.shape[0], own_self.shape[-1]
    for u in range(4):
        at = (count + u // 2, slice(None), slice((u & 1) * half, (u & 1) * half + half))
        both[at] = low_sum(*(ref[u] for ref in refs[:4]))
    both[:count] = totals[...]


def emit_made(place, made, outs, block):
    rows, wide = outs[0].shape[3], block.shape[2]
    piece, span = wide // 2, wide // 3
    block[...] = jnp.zeros_like(block)
    cond = jnp.concatenate([part[2][...] for part in made], axis=1)
    columns = cond.shape[1] // 16
    for j in range(8):
        for core in (0, 1):
            for slot in range(3):
                at = 3 * (2 * j + core) + slot
                part = made[at // 16][0][(at % 16) * rows : (at % 16 + 1) * rows]
                block[core, :, slot * span : slot * span + part.shape[1]] = part.astype(jnp.float32)
        emit_block(place, outs, 0, j, *(block[core].astype(jnp.bfloat16) for core in (0, 1)))
    for out in outs:
        out.leave(0, functools.partial(unit_part, place))
    block[...] = jnp.zeros_like(block)
    for j in range(8):
        for core in (0, 1):
            owner = 2 * j + core
            for slot in range(9):
                at = 9 * owner + slot
                row, half = (at % 48) // 2, at % 2
                part = made[at // 48][1][row * 8 : row * 8 + 8, half * piece : (half + 1) * piece]
                block[core, slot // 2 * 8 : slot // 2 * 8 + 8, slot % 2 * piece : (slot % 2 + 1) * piece] = part
            turned = pltpu.roll(cond, (cond.shape[1] - owner * columns) % cond.shape[1], 1)
            block[core, 40:48, :span] = turned[:, :span]
        emit_block(place, outs, 1, j, *(block[core].astype(jnp.bfloat16) for core in (0, 1)))
    for out in outs:
        out.leave(1, functools.partial(unit_part, place))


def cross_kernel(
    place, grad_mixed, packed, query, keyval, weights, scales, mixed, grad_branch, normed, memory, stream, gains, grad_result,
    grad_stream, grad_memory, grad_gain, *rest,
):
    outs, (held, grad_query, grad_keyval, sems) = rest[:-4], rest[-4:]
    copies = [unit_copy(packed, 4, held, sems, u) for u in range(3)]
    width = stream.shape[1]

    def beside():
        for copy in (mixed, grad_branch, normed, memory, *copies, stream, gains, grad_result):
            copy.start()

    attend_backward(
        query, keyval, keyval, (0, 0, width), weights, scales, grad_mixed,
        (grad_query, grad_keyval, grad_keyval), (0, 0, width), beside,
    )
    emit(place, outs, 3, dot_tn(mixed[...], grad_branch[...]))
    emit(place, outs, 0, dot_tn(normed[...], grad_query[...]))
    for copy in copies:
        copy.wait()
    for u in range(2):
        grad = grad_keyval[:, u * width : (u + 1) * width]
        emit(place, outs, 1 + u, dot_tn(memory[...], grad))
        if u == 0:
            grad_memory[...] = dot_nt(grad, whole_unit(held[1 + u]))
        else:
            grad_memory[...] += dot_nt(grad, whole_unit(held[1 + u]))
    grad_memory.ship()
    wide = stream[...]
    grad, gain_rows = rms_back(
        wide, rms_rate(wide), gains[1:2], dot_nt(grad_query[...], whole_unit(held[0]))
    )
    grad_stream[...] = grad_result[...] + grad
    grad_gain[...] = jnp.sum(gain_rows, axis=0, keepdims=True)


def self_kernel(
    place, grad_mixed, packed, projected, weights, scales, mixed, grad_branch, normed, tokens, gains, grad_stream,
    grad_tokens, grad_gain, *rest,
):
    outs, (held, grad_projected, total, sems) = rest[:-4], rest[-4:]
    copies = [unit_copy(packed, 0, held, sems, u) for u in range(3)]
    width = tokens.shape[1]

    def beside():
        for copy in (mixed, grad_branch, normed, *copies, tokens, gains, grad_stream):
            copy.start()

    attend_backward(
        projected, projected, projected, (0, width, 2 * width), weights, scales, grad_mixed,
        (grad_projected,) * 3, (0, width, 2 * width), beside,
    )
    emit(place, outs, 3, dot_tn(mixed[...], grad_branch[...]))
    for u in range(3):
        copies[u].wait()
        grad = grad_projected[:, u * width : (u + 1) * width]
        emit(place, outs, u, dot_tn(normed[...], grad))
        if u == 0:
            total[...] = dot_nt(grad, whole_unit(held[u]))
        else:
            total[...] += dot_nt(grad, whole_unit(held[u]))
    wide = tokens[...].astype(jnp.float32)
    grad, gain_rows = rms_back(wide, rms_rate(wide), gains[0:1], total[...])
    grad_tokens[...] = grad_stream[...] + grad
    grad_gain[...] = jnp.sum(gain_rows, axis=0, keepdims=True)


def pack_kernel(*refs):
    shards, packed = refs[:-1], refs[-1]
    rows, width = packed.shape[1:]
    unit = 0
    for shard in shards:
        for row in range(0, shard.shape[0], rows):
            for column in range(0, shard.shape[1], width):
                packed[unit] = shard[row : row + rows, column : column + width]
                unit += 1


def sum_kernel(*refs):
    refs[-1][...] = low_sum(*(ref[...] for ref in refs[:-1]))


def swap(values, axis, count, mate):
    return lax.ppermute(values, axis, [(i, mate(i)) for i in range(count)])


def place_parts():
    place = lax.axis_index("fsdp")
    return place // 4, (place // 2) % 2, place % 2


def ring_gather(block):
    z, y, core = place_parts()
    shifted = [swap(block, "fsdp", 16, lambda i, d=d: (i + 4 * d) % 16) for d in (3, 2, 1)]
    line = jnp.stack(shifted[:1] + shifted[1:] + [block])
    line = lax.dynamic_slice_in_dim(jnp.concatenate([line, line]), 3 - z, 4, 0)
    other = swap(line, "fsdp", 16, lambda i: i ^ 2)
    both = jnp.stack([jnp.where(y == 0, line, other), jnp.where(y == 0, other, line)], axis=1)
    other = swap(both, "fsdp", 16, lambda i: i ^ 1)
    whole = jnp.stack([jnp.where(core == 0, both, other), jnp.where(core == 0, other, both)], axis=2)
    return whole.reshape((16,) + block.shape)


def add_low(left, right):
    return (left.astype(jnp.float32) + right.astype(jnp.float32)).astype(jnp.bfloat16)


def core_swap(sent):
    return swap(sent, "fsdp", 16, lambda i: i ^ 1)


def y_swap(sent):
    return swap(sent, "fsdp", 16, lambda i: i ^ 2)


def x_swap(sent):
    return swap(sent, "dp", 2, lambda i: i ^ 1)


def z_swaps(parts):
    return [swap(parts[d], "fsdp", 16, lambda i, d=d: (i + 4 * d) % 16) for d in (1, 2, 3)]


def both_halves(own, other, first_x):
    return jnp.concatenate([jnp.where(first_x, own, other), jnp.where(first_x, other, own)], axis=-1)


def after(values, *others):
    return lax.optimization_barrier((values, others))[0]


def ring_step(values, bit):
    return values + swap(values, "fsdp", 16, lambda i: i ^ bit)


def gather_shards(block, ring):
    return ring_gather(block) if ring else lax.all_gather(block, "fsdp", axis=0)


def block_share(blocks):
    part = lax.psum_scatter(blocks, "fsdp", scatter_dimension=0, tiled=False)
    return lax.psum(part.astype(jnp.float32), "dp")


def share_of(grads, devices, by_rows):
    whole = grads[0][0, 0]
    count, width = whole.shape[0], whole.shape[-1]
    if by_rows:
        return block_share(whole.reshape(devices, count, -1, width))
    blocks = jnp.transpose(whole.reshape(count, devices, -1, width), (1, 0, 2, 3))
    return block_share(blocks)


def sum_shards(values, ring):
    return ring_sum(values) if ring else lax.psum(values, "fsdp")


def units_of(shard, width):
    rows, columns = shard.shape
    return jnp.transpose(shard.reshape(rows, columns // width, width), (1, 0, 2))


def joined(units):
    return jnp.transpose(units, (1, 0, 2)).reshape(units.shape[1], -1)


def view_shape(shape, view):
    return tuple(at.size for at in view if not isinstance(at, int)) + tuple(shape[len(view) :])


def call(kernel, operands, shapes, scratch, flops, raw=(), split=None, parts=None, later=(), views=None):
    split, parts, views = split or {}, parts or {}, views or {}
    scalars = operands[0].ndim == 1
    moved_in = [i for i in range(int(scalars), len(operands)) if i not in raw]
    specs = [pl.BlockSpec(memory_space=pl.ANY) for _ in operands]
    if scalars:
        specs[0] = pl.BlockSpec(memory_space=pltpu.SMEM)
    outs = [jax.ShapeDtypeStruct(shape, dtype) for shape, dtype in shapes]
    room = 20 if kernel in (kept_sums, sum_kernel, out_kernel) else 60
    buffers = [pltpu.VMEM(view_shape(operands[i].shape, views.get(i, ())), operands[i].dtype) for i in moved_in]
    buffers += [pltpu.VMEM(shape, dtype) for shape, dtype in shapes]
    buffers += [pltpu.SemaphoreType.DMA((split.get(i, 1),)) for i in moved_in]
    buffers += [pltpu.SemaphoreType.DMA((parts.get(k, 1),)) for k in range(len(outs))]

    def body(*refs):
        ins, results = list(refs[: len(operands)]), refs[len(operands) : len(operands) + len(outs)]
        own = refs[len(operands) + len(outs) : len(refs) - len(buffers)]
        held = refs[len(refs) - len(buffers) :]
        held, sems = held[: len(buffers) // 2], held[len(buffers) // 2 :]
        for k, i in enumerate(moved_in):
            source = ins[i].at[views[i]] if i in views else ins[i]
            ins[i] = Fetched(source, held[k], sems[k], split.get(i, 1))
            if i not in later:
                ins[i].start()
        results = [
            Shipped(target, *rest) for target, *rest in zip(results, held[len(moved_in) :], sems[len(moved_in) :])
        ]
        kernel(*ins, *results, *own)
        for operand in ins:
            ready(operand)
        for result in results:
            result.settle()

    moved = sum(math.prod(shape) * jnp.dtype(dtype).itemsize for shape, dtype in shapes)
    moved += sum(operand.size * operand.dtype.itemsize for operand in operands)
    return pl.pallas_call(
        body,
        out_shape=outs,
        in_specs=specs,
        out_specs=[pl.BlockSpec(memory_space=pl.ANY) for _ in outs],
        scratch_shapes=list(scratch) + buffers,
        compiler_params=pltpu.CompilerParams(vmem_limit_bytes=room * 1024 * 1024),
        cost_estimate=pl.CostEstimate(flops=flops, bytes_accessed=moved, transcendentals=0),
    )(*operands)


def per_device(
    devices,
    ring,
    tokens,
    memory,
    out_grad,
    target_len,
    source_len,
    task_ids,
    norm_gains,
    self_qkv,
    self_out,
    cross_query,
    cross_keyval,
    cross_out,
    feed_in,
    feed_out,
    task_table,
    hyper_in,
    maker_down,
    maker_up,
    maker_norm,
):
    width = tokens.shape[1]
    tasks = task_table.shape[0]
    embed = hyper_in.shape[0]
    table_width = task_table.shape[1]
    hyper_width = hyper_in.shape[1]
    gain_width = norm_gains.shape[1]
    down_span = maker_down.shape[1]
    norm_span = maker_norm.shape[1]
    bottleneck = down_span * devices // (3 * width)
    down_rows = 3 * width // devices
    unit = width // devices
    ff_units = feed_in.shape[1] // width
    small = jnp.concatenate(
        [
            jnp.pad(task_table.T, ((0, 0), (0, 128 - tasks))),
            jnp.pad(hyper_in.T, ((0, 0), (0, 128 - embed))),
            jnp.pad(norm_gains, ((0, 0), (0, 128 - gain_width))),
            jnp.zeros((-(table_width + hyper_width + 3) % 16, 128), jnp.bfloat16),
        ]
    )
    small = gather_shards(small, ring)
    whole_table = small[:, :table_width, :tasks].reshape(-1, tasks).T
    whole_hyper = small[:, table_width : table_width + hyper_width, :embed].reshape(-1, embed).T
    first = table_width + hyper_width
    whole_gains = jnp.transpose(small[:, first : first + 3, :gain_width], (1, 0, 2)).reshape(3, width)
    layer = [self_qkv, self_out, cross_query, cross_keyval, cross_out, feed_in]
    if ring:
        shape = ((8 + 2 * ff_units, unit, width), jnp.bfloat16)
        (packed,) = call(pack_kernel, (*layer, feed_out), [shape], [], 1)
        packed = packed.reshape(-1, width)
    else:
        layer = [units_of(w, width) for w in layer] + [feed_out.reshape(ff_units, unit, width)]
        packed = jnp.concatenate([w.reshape(-1, width) for w in layer])
    packed = lax.all_gather(packed, "fsdp", axis=0).reshape(devices, -1, unit, width)
    if not ring:
        first = jnp.transpose(packed[:, : 8 + ff_units], (1, 0, 2, 3)).reshape(-1, width, width)
        last = packed[:, 8 + ff_units :].reshape(-1, width, width)
        packed = jnp.concatenate([first, last])[None]
    pre_hidden = matmul(whole_table, whole_hyper)
    hidden = jax.nn.silu(pre_hidden).astype(jnp.bfloat16)
    own_down = matmul(hidden, maker_down).astype(jnp.bfloat16)
    own_up = matmul(hidden, maker_up).astype(jnp.bfloat16)
    own_norm = matmul(hidden, maker_norm).astype(jnp.bfloat16)
    span = tasks * bottleneck
    own_down = jnp.transpose(own_down.reshape(tasks, down_rows, bottleneck), (1, 2, 0)).reshape(-1, span)
    if ring:
        third, piece = width // 3, width // 2
        own_down = jnp.pad(own_down.reshape(3, unit, span), ((0, 0), (0, 0), (0, third - span)))
        own_down = jnp.transpose(own_down, (1, 0, 2)).reshape(unit, width)
        own_up = jnp.pad(own_up, ((0, 0), (0, 10 * piece - down_span))).reshape(tasks, 5, width)
        own_up = jnp.transpose(own_up, (1, 0, 2)).reshape(5 * tasks, width)
        own_norm = jnp.pad(own_norm, ((0, 0), (0, width - norm_span)))
        made = jnp.concatenate([own_down, own_up, own_norm])
        first_x = lax.axis_index("dp") == 0
        made = ring_gather(jnp.where(first_x, made[:, : width // 2], made[:, width // 2 :]))
        made = both_halves(made, x_swap(made), first_x)
        made_down = made[:, :unit].reshape(devices, unit, 3, third)[..., :span]
        made_down = jnp.transpose(made_down, (0, 2, 1, 3)).reshape(3, width, span)
        made_up = made[:, unit : unit + 5 * tasks].reshape(devices, 5, tasks, 2, piece)
        made_up = jnp.transpose(made_up, (0, 1, 3, 2, 4)).reshape(devices, 10, tasks, piece)[:, :9]
        made_up = jnp.transpose(made_up.reshape(3, bottleneck, 2, tasks, piece), (0, 1, 3, 2, 4))
        made_up = made_up.reshape(3, span, width)
        made_cond = made[:, unit + 5 * tasks :, :norm_span]
    else:
        made_down = lax.all_gather(own_down, "fsdp", axis=0, tiled=True).reshape(3, width, span)
        made_up = lax.all_gather(own_up, "fsdp", axis=1, tiled=True).reshape(tasks, 3, bottleneck, width)
        made_up = jnp.transpose(made_up, (1, 2, 0, 3)).reshape(3, span, width)
        made_cond = lax.all_gather(own_norm, "fsdp", axis=0)
    made_cond = jnp.transpose(made_cond, (1, 0, 2)).reshape(tasks, 3, width)
    made_cond = jnp.pad(jnp.transpose(made_cond, (1, 0, 2)), ((0, 0), (0, 128 - tasks), (0, 0)))
    tok_seg = segment_rows(target_len[0], tokens.shape[0])
    mem_seg = segment_rows(source_len[0], memory.shape[0])
    sequences = jnp.arange(target_len.shape[1], dtype=jnp.int32)
    row_task = jnp.sum(
        jnp.where(tok_seg[:, None] == sequences[None, :], task_ids[0][None, :], 0), axis=1
    )
    onehot = (row_task[:, None] == jnp.arange(128, dtype=jnp.int32)[None, :]).astype(jnp.bfloat16)
    mask = jnp.tile(onehot[:, :tasks], (1, bottleneck))
    places = jnp.arange(tokens.shape[0], dtype=jnp.int32)
    self_allowed = (tok_seg[:, None] == tok_seg[None, :]) & (places[:, None] <= places[None, :])
    cross_allowed = mem_seg[:, None] == tok_seg[None, :]
    self_cap = jnp.where(self_allowed, -masked_score * 1e20, masked_score).astype(jnp.float32)
    cross_cap = jnp.where(cross_allowed, -masked_score * 1e20, masked_score).astype(jnp.float32)
    gains = jnp.pad(whole_gains.astype(jnp.float32), ((0, 5), (0, 0)))
    place = lax.axis_index("fsdp")
    here = jnp.stack([place // 4, (place // 2) % 2, place % 2, lax.axis_index("dp")]).astype(jnp.int32)
    adapters = (onehot, made_cond, made_down, made_up, mask)
    rows, memory_rows = tokens.shape[0], memory.shape[0]
    pairs = width // 128
    low, full = jnp.bfloat16, jnp.float32
    held_unit = packed.shape[:1] + packed.shape[2:]

    def held(count):
        return pltpu.VMEM((count,) + held_unit, low)

    def grad_shapes(count, by_x=False):
        if ring and by_x:
            return [((2, 2, 4, count, unit, width // 2), low)] * 2
        if ring:
            return [((2, 4, count, unit, width), low)] * 2
        return [((1, 1, count, width, width), low)]

    made_shapes = [((width, span), low), ((span, width), full), ((tasks, width), full)]
    gain_shape = [((1, width), full)]
    busy = 1700000000
    scale_shape = ((pairs, 1, 2 * rows), full)
    float_rows, low_rows = ((rows, width), full), ((rows, width), low)
    found = call(
        attention_kernel,
        (tokens, gains, packed, self_cap) + adapters + (memory, cross_cap),
        [low_rows, ((rows, 3 * width), low), ((pairs, rows, 2 * rows), low), scale_shape, low_rows, float_rows]
        + [((rows, span), full), float_rows, low_rows, low_rows, ((memory_rows, 2 * width), low)]
        + [((pairs, memory_rows, 2 * rows), low), scale_shape, low_rows, float_rows]
        + [((rows, span), full), float_rows],
        [held(8), pltpu.SemaphoreType.DMA((8,))],
        37 * busy,
        raw=(2,),
        parts={2: pairs, 11: pairs},
        later=(4, 5, 6, 7, 8, 9, 10),
    )
    normed1, projected, weights1, scales1, mixed1, branch1, squeezed1, stream1, *found = found
    normed2, query2, keyval2, weights2, scales2, mixed2, branch2, squeezed2, stream2 = found
    held_out = (packed.shape[0], ff_units) + packed.shape[2:]
    sets = 2 if ring else 1
    result, grad_stream, *found = call(
        feed_kernel,
        (here, stream2, gains, packed) + adapters + (out_grad,),
        [low_rows, float_rows] + made_shapes + gain_shape + grad_shapes(ff_units, True) + grad_shapes(ff_units),
        [
            held(ff_units),
            pltpu.VMEM(held_out, low),
            pltpu.VMEM((rows, width), low),
            pltpu.VMEM((ff_units, rows, width), full),
            pltpu.VMEM((ff_units, rows, width), low),
            pltpu.VMEM((rows, width), low),
            pltpu.VMEM((rows, width), full),
            pltpu.SemaphoreType.DMA((2 * ff_units,)),
        ],
        36 * busy,
        raw=(3,),
        parts={6 + k: (2 if k < sets else 1) * ff_units for k in range(2 * sets)},
        later=(4, 5, 6, 7, 8, 9),
        views=dict.fromkeys((5, 6, 7), (pl.ds(2, 1),)),
    )
    made_three, grad_gain_three, grads_out, grads_in = found[:3], found[3], found[4 : 4 + sets], found[4 + sets :]

    def branch_back(index, unit_at, grad_result, branch, squeezed, others, shapes):
        return call(
            functools.partial(branch_kernel, unit_at),
            (here, grad_result, packed, squeezed, branch) + adapters + others,
            [low_rows] * 2 + made_shapes + shapes,
            [pltpu.VMEM((2, unit, width), full)] * int(bool(others)) + [held(1), pltpu.SemaphoreType.DMA((1,))],
            30 * busy,
            raw=(2,),
            parts={5: 2, 6: 2} if others else {},
            later=tuple(range(16, 22)) if others else (),
            views=dict.fromkeys((6, 7, 8), (pl.ds(index, 1),))
            | (dict.fromkeys((16, 17, 19, 20), (0,)) if others else {}),
        )

    if ring:
        got_out, got_in = core_swap(grads_out[0]), core_swap(grads_in[0])
    grad_branch, grad_mixed, *made_two = branch_back(1, 7, grad_stream, branch2, squeezed2, (), [])
    if ring:
        got_out, got_in = after((got_out, got_in), grad_mixed)
        sent_out, sent_in = (add_low(kept[1], got[1]) for (_, kept), got in ((grads_out, got_out), (grads_in, got_in)))
        other_out, other_in = x_swap(sent_out), y_swap(sent_in)
        grad_mixed = after(grad_mixed, sent_out, sent_in)
    grad_stream, grad_memory, grad_gain_two, *grads_cross = call(
        cross_kernel,
        (here, grad_mixed, packed, query2, keyval2, weights2, scales2, mixed2, grad_branch, normed2)
        + (memory, stream1, gains, grad_stream),
        [float_rows, ((memory_rows, width), full)] + gain_shape + grad_shapes(4, True),
        [
            held(3),
            pltpu.VMEM((rows, width), low),
            pltpu.VMEM((memory_rows, 2 * width), low),
            pltpu.SemaphoreType.DMA((3,)),
        ],
        24 * busy,
        raw=(2,),
        split={5: pairs},
        parts={3: 4, 4: 4},
        later=(5,) + tuple(range(7, 14)),
    )
    others, shapes = (), []
    if ring:
        got_cross = core_swap(grads_cross[0])
        others = (*made_two, *made_three, grads_out[1], got_out, other_out, grads_in[1], got_in, other_in)
        shapes = [((2, 4, 2, unit, width), low)] * 2
        shapes += [((4, ff_units // 2, unit, width), low)] * 2 + [((ff_units, unit, width), low)] * 4
    grad_branch, grad_mixed, *made_one = branch_back(0, 3, grad_stream, branch1, squeezed1, others, shapes)
    if ring:
        sent_made, kept_made, own_out, sent_out, *parts_in = made_one[3:]
        got_made = core_swap(sent_made)
        got_cross = after(got_cross, grad_mixed)
        sent_cross = add_low(grads_cross[1][1], got_cross[1])
        other_cross = x_swap(sent_cross)
        far_in = z_swaps(after(parts_in, sent_cross))
        sent_made = add_low(kept_made[1], after(got_made, sent_cross)[1])
        other_y = y_swap(jnp.concatenate([sent_out, sent_made], axis=1))
        grad_mixed = after(grad_mixed, sent_made)
    grad_tokens, grad_gain_one, *grads_self = call(
        self_kernel,
        (here, grad_mixed, packed, projected, weights1, scales1, mixed1, grad_branch, normed1, tokens, gains)
        + (grad_stream,),
        [float_rows] + gain_shape + grad_shapes(4, True),
        [
            held(3),
            pltpu.VMEM((rows, 3 * width), low),
            pltpu.VMEM((rows, width), full),
            pltpu.SemaphoreType.DMA((3,)),
        ],
        busy,
        raw=(2,),
        split={4: pairs},
        parts={2: 4, 3: 4},
        later=(4,) + tuple(range(6, 12)),
    )

    def own_made(share):
        own_down = share[0].reshape(unit, 3, third)[:, :, :span]
        own_down = jnp.transpose(own_down, (1, 0, 2)).reshape(down_rows, bottleneck, tasks)
        own_down = jnp.transpose(own_down, (2, 0, 1)).reshape(tasks, down_span)
        own_up = share[1, : 5 * tasks].reshape(5, tasks, width)
        own_up = jnp.transpose(own_up, (1, 0, 2)).reshape(tasks, 5 * width)[:, :down_span]
        return own_down, own_up, share[1, 5 * tasks :, :norm_span]

    def hidden_of(own_down, own_up, own_norm):
        return (
            dot_nt(own_down.astype(jnp.bfloat16), maker_down)
            + dot_nt(own_up.astype(jnp.bfloat16), maker_up)
            + dot_nt(own_norm.astype(jnp.bfloat16), maker_norm)
        )

    def hidden_outs(*made):
        return [dot_tn(hidden, own.astype(jnp.bfloat16)) for own in made]

    grad_gains = jnp.concatenate([grad_gain_one, grad_gain_two, grad_gain_three])
    if ring:
        got_self = core_swap(grads_self[0])
        flight = (far_in, other_cross, other_y)
        far_in, other_cross, other_y = after(flight, grad_gain_one)
        halves_y, column_half = ((4, 4, unit, width // 2), low), ((4, unit, width // 2), low)
        whole_part = ((4, unit, width), low)
        sent_cross, *parts = call(
            first_sums,
            (grads_cross[1], got_cross, other_cross, kept_made, got_made, own_out, other_y),
            [halves_y] + [whole_part] * 4,
            [],
            100 * busy,
            views={0: (0, 1), 1: (0, 1), 2: (1,), 3: (0,), 4: (0,)},
        )
        sent_self = add_low(grads_self[1][1], after(got_self, sent_cross)[1])
        other_self = x_swap(sent_self)
        parts, sent_cross = after((parts, sent_cross), sent_self)
        far = z_swaps(parts)
        kept_cross, far_in = after((grads_cross[1], far_in), sent_self)
        total_in, own_cross = call(
            kept_sums,
            (kept_cross, got_cross, other_cross, parts_in[0], *far_in),
            [whole_part, halves_y],
            [],
            100 * busy,
            views={0: (0, 0), 1: (0, 0), 2: (0,)},
        )
        other_cross = y_swap(sent_cross)
        totals, total_made, sent_self, *parts = call(
            second_sums,
            (parts[0], *far, total_in, grads_self[1], got_self, other_self, own_cross, other_cross)
            + (grad_gains,),
            [((6, unit, width), low), ((3, unit, width), low), halves_y] + [column_half] * 4,
            [],
            5 * busy,
            views={5: (0, 1), 6: (0, 1), 7: (1,)},
        )
        other_made, far = x_swap(total_made), z_swaps(parts)
        (own_self,) = call(
            kept_sums,
            (after(grads_self[1], other_made), got_self, other_self),
            [halves_y],
            [],
            100 * busy,
            views={0: (0, 0), 1: (0, 0), 2: (0,)},
        )
        other_self = y_swap(sent_self)
        share_made = total_made.astype(jnp.float32) + other_made.astype(jnp.float32)
        own_down, own_up, own_norm = own_made(share_made[:2])
        sums = jnp.concatenate(
            [hidden_of(own_down, own_up, own_norm), share_made[2, :3].reshape(-1, 128)]
        )
        sums = ring_step(sums, 1)
        made_outs = hidden_outs(own_down, own_up, own_norm)
        totals, *parts = call(
            third_sums,
            (parts[0], *far, own_self, other_self, after(totals, made_outs)),
            [((8, unit, width), low)] + [column_half] * 4,
            [],
            5 * busy,
        )
        other_totals, far = x_swap(totals), z_swaps(parts)
        sums = ring_step(after(sums, totals), 2)
        for part in z_swaps([sums] * 4):
            sums = sums + part
        far = after(far, sums)
        total_self = call(sum_kernel, (parts[0], *far), [column_half], [], 5 * busy)[0]
        other_self = x_swap(total_self)
        sums = after(sums, total_self)
        shapes = [((unit, ff_units * width), full), ((ff_units * unit, width), full)]
        shapes += [((unit, count * width), full) for count in (1, 2, 1, 3, 1)]
        out_feed_in, out_feed_out, out_query, out_keyval, out_cross_out, out_qkv, out_self_out = call(
            out_kernel, (here, totals, other_totals, total_self, other_self), shapes, [], busy
        )
    else:
        share_in, share_out, share_cross, share_self = (
            share_of(grads, devices, grads is grads_out)
            for grads in (grads_in, grads_out, grads_cross, grads_self)
        )
        made = (made_one, made_two, made_three)
        grad_down = jnp.concatenate([part[0] for part in made]).reshape(devices, -1)
        grad_up = jnp.stack([part[1] for part in made]).reshape(3, bottleneck, tasks, width)
        grad_up = jnp.transpose(grad_up, (2, 0, 1, 3)).reshape(tasks, devices, down_span)
        grad_norm = jnp.concatenate([part[2] for part in made], axis=1)
        grad_norm = grad_norm.reshape(tasks, devices, norm_span)
        blocks = [grad_down.astype(jnp.bfloat16)] + [
            jnp.transpose(part.astype(jnp.bfloat16), (1, 0, 2)).reshape(devices, -1)
            for part in (grad_up, grad_norm)
        ]
        out_feed_in, out_feed_out = joined(share_in), share_out.reshape(-1, width)
        out_query, out_keyval, out_cross_out = share_cross[0], joined(share_cross[1:3]), share_cross[3]
        out_qkv, out_self_out = joined(share_self[:3]), share_self[3]
        share_made = block_share(jnp.concatenate(blocks, axis=1))
        sizes = (0, tasks * down_span, 2 * tasks * down_span, share_made.shape[0])
        own_down, own_up, own_norm = (share_made[a:b] for a, b in zip(sizes, sizes[1:]))
        own_down = jnp.transpose(own_down.reshape(down_rows, bottleneck, tasks), (2, 0, 1))
        own_down, own_up = own_down.reshape(tasks, down_span), own_up.reshape(tasks, down_span)
        own_norm = own_norm.reshape(tasks, norm_span)
        sums = jnp.concatenate([hidden_of(own_down, own_up, own_norm), lax.psum(grad_gains, "dp").reshape(-1, 128)])
        sums = lax.psum(sums, "fsdp")
        made_outs = hidden_outs(own_down, own_up, own_norm)
    grad_hidden = sums[:tasks]
    out_gains = lax.dynamic_slice_in_dim(
        sums[tasks:].reshape(3, width), place * gain_width, gain_width, 1
    )
    _, silu_pull = jax.vjp(jax.nn.silu, pre_hidden)
    grad_pre_hidden = silu_pull(grad_hidden)[0]
    own_hyper = lax.dynamic_slice_in_dim(whole_hyper, place * table_width, table_width, 0)
    out_table = exact_cols(grad_pre_hidden, own_hyper.astype(jnp.float32))
    own_pre = lax.dynamic_slice_in_dim(grad_pre_hidden, place * hyper_width, hyper_width, 1)
    out_hyper = exact_rows(whole_table.astype(jnp.float32), own_pre)
    out_down, out_up, out_norm = made_outs
    return (
        result.astype(jnp.bfloat16),
        grad_tokens,
        grad_memory,
        out_gains,
        out_qkv,
        out_self_out,
        out_query,
        out_keyval,
        out_cross_out,
        out_feed_in,
        out_feed_out,
        out_table,
        out_hyper,
        out_down,
        out_up,
        out_norm,
    )


def solution(mesh):
    placed = (
        P(("fsdp", "dp"), None),
        P(("fsdp", "dp"), None),
        P(("fsdp", "dp"), None),
        P(("fsdp", "dp"), None),
        P(("fsdp", "dp"), None),
        P(("fsdp", "dp"), None),
        P(None, "fsdp"),
        P("fsdp", None),
        P("fsdp", None),
        P("fsdp", None),
        P("fsdp", None),
        P("fsdp", None),
        P("fsdp", None),
        P("fsdp", None),
        P(None, "fsdp"),
        P(None, "fsdp"),
        P(None, "fsdp"),
        P(None, "fsdp"),
        P(None, "fsdp"),
    )
    devices = mesh.shape["fsdp"]
    ring = devices == 16 and mesh.shape["dp"] == 2
    return jax.shard_map(
        functools.partial(per_device, devices, ring),
        mesh=mesh,
        in_specs=placed,
        out_specs=(
            P(("fsdp", "dp"), None),
            P(("fsdp", "dp"), None),
            P(("fsdp", "dp"), None),
            P(None, "fsdp"),
            P("fsdp", None),
            P("fsdp", None),
            P("fsdp", None),
            P("fsdp", None),
            P("fsdp", None),
            P("fsdp", None),
            P("fsdp", None),
            P(None, "fsdp"),
            P(None, "fsdp"),
            P(None, "fsdp"),
            P(None, "fsdp"),
            P(None, "fsdp"),
        ),
        check_vma=False,
    )
```

```python
import functools
import math

import jax
import jax.numpy as jnp
from jax import lax
from jax.experimental import pallas as pl
from jax.experimental.pallas import tpu as pltpu
from jax.sharding import PartitionSpec as P

norm_epsilon = 1e-06
masked_score = -1000000000.0
highest = lax.Precision.HIGHEST


def matmul(left, right):
    return jnp.dot(left, right, preferred_element_type=jnp.float32)


def exact_rows(left, right):
    return lax.dot_general(
        left, right, (((0,), (0,)), ((), ())), precision=highest, preferred_element_type=jnp.float32
    )


def exact_cols(left, right):
    return lax.dot_general(
        left, right, (((1,), (1,)), ((), ())), precision=highest, preferred_element_type=jnp.float32
    )


def segment_rows(lengths, count):
    ends = jnp.cumsum(lengths)
    places = jnp.arange(count, dtype=jnp.int32)
    return jnp.sum((places[:, None] >= ends[None, :]).astype(jnp.int32), axis=1)


def dot(left, right):
    return jnp.dot(left, right, preferred_element_type=jnp.float32)


def dot_nt(left, right):
    return lax.dot_general(
        left, right, (((1,), (1,)), ((), ())), preferred_element_type=jnp.float32
    )


def dot_tn(left, right):
    return lax.dot_general(
        left, right, (((0,), (0,)), ((), ())), preferred_element_type=jnp.float32
    )


def rms_rate(values):
    return lax.rsqrt(jnp.mean(values * values, axis=-1, keepdims=True) + norm_epsilon)


def rms_back(values, rate, gain, grad):
    scaled = grad * gain
    inner = jnp.mean(scaled * values, axis=-1, keepdims=True)
    return rate * (scaled - values * (rate * rate * inner)), grad * values * rate


gelu_slope = math.sqrt(2.0 / math.pi)
gelu_cube = 0.044715


def gelu(values):
    inner = gelu_slope * values * (1.0 + gelu_cube * values * values)
    return 0.5 * values * (1.0 + jnp.tanh(inner))


def gelu_back(values):
    square = values * values
    bent = jnp.tanh(gelu_slope * values * (1.0 + gelu_cube * square))
    slope = gelu_slope * (1.0 + 3.0 * gelu_cube * square)
    return 0.5 * (1.0 + bent) + 0.5 * values * (1.0 - bent * bent) * slope


def halves(dtype):
    lane = lax.broadcasted_iota(jnp.int32, (1, 128), 1)
    first = (lane < 64).astype(jnp.float32)
    return first.astype(dtype), (1.0 - first).astype(dtype)


def lanes(start):
    return pl.ds(pl.multiple_of(start, 128), 128)


class Fetched:
    def __init__(self, source, held, sems, count):
        self.source, self.held, self.sems, self.count = source, held, sems, count
        self.waiting, self.shape, self.started = count == 1, held.shape, False

    def start(self):
        if not self.started:
            for k in range(self.count):
                self.part(k).start()
        self.started = True

    def part(self, k):
        if self.count == 1:
            return pltpu.make_async_copy(self.source, self.held, self.sems.at[0])
        size = self.shape[0] // self.count
        at = pl.ds(k * size, size)
        return pltpu.make_async_copy(self.source.at[at], self.held.at[at], self.sems.at[k])

    def ready(self):
        self.start()
        if self.waiting:
            self.part(0).wait()
            self.waiting = False
        return self.held

    def __getitem__(self, at):
        return self.ready()[at]

    @property
    def at(self):
        return self.ready().at


class Shipped:
    def __init__(self, target, held, sems):
        self.target, self.held, self.sems = target, held, sems
        self.shape, self.parts = held.shape, None

    def __getitem__(self, at):
        return self.held[at]

    def __setitem__(self, at, values):
        self.held[at] = values

    @property
    def at(self):
        return self.held.at

    def copy(self, k, part):
        return pltpu.make_async_copy(part(self.held, k), part(self.target, k), self.sems.at[k])

    def ship(self):
        self.leave(0, lambda ref, k: ref)

    def leave(self, k, part):
        self.parts = part
        self.copy(k, part).start()

    def settle(self):
        if self.parts is None:
            self.ship()
        if self.sems.shape[0] == 1:
            self.copy(0, self.parts).wait()
        else:
            lax.fori_loop(0, self.sems.shape[0], lambda k, _: self.copy(k, self.parts).wait() or 0, 0)


def ready(*refs):
    return [ref.ready() if isinstance(ref, Fetched) else ref for ref in refs]


def sides(turned):
    none = jnp.zeros_like(turned[:64])
    return jnp.concatenate(
        [jnp.concatenate([turned[:64], none], axis=0), jnp.concatenate([none, turned[64:]], axis=0)], axis=1
    )


def own_sides(both):
    half = both.shape[1] // 2
    return jnp.concatenate([both[:64, :half], both[64:, half:]], axis=0)


def attend_forward(queries, keys, values, starts, cap, weights, scales, mixed):
    factor = math.log2(math.e) / 8.0
    queries, keys, values, cap = ready(queries, keys, values, cap)

    def pair(p, _):
        query, key, value = (
            ref[:, lanes(start + p * 128)] for ref, start in zip((queries, keys, values), starts)
        )
        limit = cap[...]
        scores = dot(key, sides(query.T)) * factor
        scores = jnp.minimum(scores, jnp.concatenate([limit, limit], axis=1))
        powers = jnp.exp2(scores - jnp.max(scores, axis=0, keepdims=True))
        scale = 1.0 / jnp.sum(powers, axis=0, keepdims=True)
        powers = powers.astype(jnp.bfloat16)
        weights[p] = powers
        weights.leave(p, one_pair)
        scales[p] = scale
        found = own_sides(dot(value.T, powers) * scale)
        mixed[:, lanes(p * 128)] = found.T.astype(jnp.bfloat16)
        return 0

    lax.fori_loop(0, mixed.shape[1] // 128, pair, 0, unroll=3)
    mixed.ship()
    scales.ship()


def one_pair(ref, k):
    return ref.at[k]


def attend_backward(queries, keys, values, starts, weights, scales, grad_mixed, grads, places, beside):
    marks = halves(jnp.bfloat16)
    pairs = grad_mixed.shape[1] // 128
    weights.started = True
    for p in (0, 1):
        weights.part(p).start()
    for p in range(pairs):
        query, key, value = (
            ref[:, start + p * 128 : start + p * 128 + 128]
            for ref, start in zip((queries, keys, values), starts)
        )
        scale = scales[p]
        grad = sides(grad_mixed[:, p * 128 : p * 128 + 128].T)
        grad = (grad.astype(jnp.float32) * scale).astype(jnp.bfloat16)
        if p == 1:
            beside()
        if p + 2 < pairs:
            weights.part(p + 2).start()
        weights.part(p).wait()
        powers = weights.held[p]
        wide = powers.astype(jnp.float32)
        product = wide * dot(value, grad)
        total = jnp.sum(product, axis=0, keepdims=True) * scale
        product = (product - wide * total).astype(jnp.bfloat16)
        query = jnp.concatenate([query * marks[0], query * marks[1]], axis=0)
        columns = [slice(place + p * 128, place + p * 128 + 128) for place in places]
        grads[2][:, columns[2]] = dot(powers, grad.T).astype(jnp.bfloat16)
        grads[1][:, columns[1]] = (dot(product, query) * 0.125).astype(jnp.bfloat16)
        grads[0][:, columns[0]] = (own_sides(dot(key.T, product)).T * 0.125).astype(jnp.bfloat16)


def adapter_forward(branch, index, tasks, cond, down, up, mask):
    gain = 1.0 + dot(tasks[...], cond[index])
    normed = (branch * rms_rate(branch) * gain).astype(jnp.bfloat16)
    squeezed = dot(normed, down[index]) * mask[...].astype(jnp.float32)
    return branch + dot(gelu(squeezed).astype(jnp.bfloat16), up[index]), squeezed


def adapter_backward(branch, squeezed, index, tasks, cond, down, up, mask, grad, outs):
    low = grad.astype(jnp.bfloat16)
    outs[1][...] = dot_tn(gelu(squeezed).astype(jnp.bfloat16), low)
    grad_squeezed = (gelu_back(squeezed) * dot_nt(low, up[index])).astype(jnp.bfloat16) * mask[...]
    gain = 1.0 + dot(tasks[...], cond[index])
    rate = rms_rate(branch)
    normed = (branch * rate * gain).astype(jnp.bfloat16)
    outs[0][...] = dot_tn(normed, grad_squeezed).astype(jnp.bfloat16)
    grad_branch, grad_gain = rms_back(branch, rate, gain, dot_nt(grad_squeezed, down[index]))
    outs[2][...] = dot_tn(tasks[...], grad_gain.astype(jnp.bfloat16))[: outs[2].shape[0]]
    return grad + grad_branch


def whole_unit(weight):
    return weight.reshape(-1, weight.shape[-1])


def unit_copy(packed, first, held, sems, u):
    return pltpu.make_async_copy(packed.at[:, first + u], held.at[u], sems.at[u])


def load_units(packed, first, held, sems):
    copies = [unit_copy(packed, first, held, sems, u) for u in range(held.shape[0])]
    for copy in copies:
        copy.start()
    return copies


def rows_copy(packed, held, sems, u):
    units = held.shape[1]
    if held.shape[0] == 1:
        return pltpu.make_async_copy(packed.at[:, 8 + units + u], held.at[:, u], sems.at[units + u])
    share = held.shape[0] // units
    at = pl.ds(u * share, share)
    return pltpu.make_async_copy(packed.at[at, 8 + units :], held.at[at], sems.at[units + u])


def out_rows(held, u):
    units = held.shape[1]
    if held.shape[0] == 1:
        return whole_unit(held[0, u])
    share = held.shape[0] // units
    return whole_unit(held[pl.ds(u * share, share)])


def emit(place, outs, unit, grad):
    if len(outs) == 1:
        outs[0][0, 0, unit] = grad.astype(jnp.bfloat16)
    else:
        rows = outs[0].shape[-2]
        grad = grad.astype(jnp.bfloat16)
        for j in range(8):
            even = grad[2 * j * rows : (2 * j + 1) * rows]
            odd = grad[(2 * j + 1) * rows : (2 * j + 2) * rows]
            emit_block(place, outs, unit, j, even, odd)
    for out in outs:
        out.leave(unit, functools.partial(unit_part, place))


def unit_part(place, ref, unit):
    return ref.at[:, :, :, unit] if len(ref.shape) == 6 else ref.at[:, :, unit]


def emit_block(place, outs, unit, j, even, odd):
    at = ((j & 1) ^ place[1], (j // 2 - place[0]) & 3, unit)
    for out, block in zip(outs, (jnp.where(place[2] == 0, odd, even), jnp.where(place[2] == 0, even, odd))):
        if len(out.shape) == 6:
            half = out.shape[5]
            for x in (0, 1):
                out[(x ^ place[3],) + at] = block[:, x * half : (x + 1) * half]
        else:
            out[at] = block


def attention_kernel(
    tokens, gains, packed, self_cap, tasks, cond, down, up, mask, memory, cross_cap,
    first_normed, projected, first_weights, first_scales, first_mixed, first_branch, first_squeezed, stream,
    normed, query, keyval, weights, scales, mixed, branch, squeezed, result,
    held, sems,
):
    made = (tasks, cond, down, up, mask)
    copies = [unit_copy(packed, 0, held, sems, u) for u in range(8)]
    copies[0].start()
    wide = tokens[...].astype(jnp.float32)
    first_normed[...] = (wide * rms_rate(wide) * gains[0:1]).astype(jnp.bfloat16)
    first_normed.ship()
    width = wide.shape[1]
    copies[1].start()
    for u in range(3):
        copies[u + 2].start()
        copies[u].wait()
        projected[:, u * width : (u + 1) * width] = dot(first_normed[...], whole_unit(held[u])).astype(
            jnp.bfloat16
        )
    projected.ship()
    for operand in (*made, memory, cross_cap):
        operand.start()
    for copy in copies[5:]:
        copy.start()
    attend_forward(
        projected, projected, projected, (0, width, 2 * width), self_cap, first_weights, first_scales, first_mixed
    )
    copies[3].wait()
    first_branch[...] = dot(first_mixed[...], whole_unit(held[3]))
    first_branch.ship()
    adapted, first_squeezed[...] = adapter_forward(first_branch[...], 0, *made)
    first_squeezed.ship()
    wide = tokens[...].astype(jnp.float32) + adapted
    stream[...] = wide
    stream.ship()
    normed[...] = (wide * rms_rate(wide) * gains[1:2]).astype(jnp.bfloat16)
    normed.ship()
    copies[4].wait()
    query[...] = dot(normed[...], whole_unit(held[4])).astype(jnp.bfloat16)
    query.ship()
    for u in range(2):
        copies[5 + u].wait()
        keyval[:, u * width : (u + 1) * width] = dot(memory[...], whole_unit(held[5 + u])).astype(
            jnp.bfloat16
        )
    keyval.ship()
    attend_forward(query, keyval, keyval, (0, 0, width), cross_cap, weights, scales, mixed)
    copies[7].wait()
    branch[...] = dot(mixed[...], whole_unit(held[7]))
    branch.ship()
    adapted, squeezed[...] = adapter_forward(branch[...], 1, *made)
    result[...] = stream[...] + adapted


def feed_kernel(
    place, stream, gains, packed, tasks, cond, down, up, mask, out_grad,
    result, grad_stream, grad_down, grad_up, grad_cond, grad_gain, *rest,
):
    made = (tasks, cond, down, up, mask)
    outs, (held_in, held_out, normed, before, active, grad_branch, total, sems) = rest[:-8], rest[-8:]
    ahead, outs = outs[: len(outs) // 2], outs[len(outs) // 2 :]
    units = active.shape[0]

    def start(u):
        unit_copy(packed, 8, held_in, sems, u).start()
        rows_copy(packed, held_out, sems, u).start()

    start(0)
    wide = stream[...]
    normed[...] = (wide * rms_rate(wide) * gains[2:3]).astype(jnp.bfloat16)
    total[...] = jnp.zeros_like(total)
    for u in range(units):
        if u + 1 < units:
            start(u + 1)
        else:
            for operand in (*made, out_grad):
                operand.start()
        unit_copy(packed, 8, held_in, sems, u).wait()
        value = dot(normed[...], whole_unit(held_in[u]))
        before[u] = value
        active[u] = gelu(value).astype(jnp.bfloat16)
        rows_copy(packed, held_out, sems, u).wait()
        total[...] += dot(active[u], out_rows(held_out, u))
    branch = total[...]
    adapted, squeezed = adapter_forward(branch, 0, *made)
    result[...] = (stream[...] + adapted).astype(jnp.bfloat16)
    result.ship()
    grad_branch[...] = adapter_backward(
        branch, squeezed, 0, *made, out_grad[...].astype(jnp.float32), (grad_down, grad_up, grad_cond)
    ).astype(jnp.bfloat16)
    for out in (grad_down, grad_up, grad_cond):
        out.ship()
    half = active.shape[2] // 2

    def row_part(ref, j):
        if len(outs) == 1:
            return ref.at[0, 0, j // 2, pl.ds((j & 1) * half, half)]
        return ref.at[:, (j & 1) ^ place[1], (j // 2 - place[0]) & 3]

    for j in range(2 * units):
        columns = slice((j & 1) * half, (j & 1) * half + half)
        grad = dot_tn(active[j // 2, :, columns], grad_branch[...]).astype(jnp.bfloat16)
        if len(outs) == 1:
            ahead[0][0, 0, j // 2, columns] = grad
        else:
            rows = outs[0].shape[-2]
            for u in range(4):
                emit_block(
                    place, ahead, u, j,
                    grad[u * rows : (u + 1) * rows], grad[(4 + u) * rows : (5 + u) * rows],
                )
        for out in ahead:
            out.leave(j, row_part)
    total[...] = jnp.zeros_like(total)
    for u in range(units):
        grad = dot_nt(grad_branch[...], out_rows(held_out, u))
        grad = (grad * gelu_back(before[u])).astype(jnp.bfloat16)
        emit(place, outs, u, dot_tn(normed[...], grad))
        total[...] += dot_nt(grad, whole_unit(held_in[u]))
    wide = stream[...]
    grad, gain_rows = rms_back(wide, rms_rate(wide), gains[2:3], total[...])
    grad_stream[...] = out_grad[...].astype(jnp.float32) + grad
    grad_gain[...] = jnp.sum(gain_rows, axis=0, keepdims=True)


def branch_kernel(unit, place, grad_result, packed, squeezed, branch, tasks, cond, down, up, mask, *rest):
    *rest, held, sems = rest
    (copy,) = load_units(packed, unit, held, sems)
    others = 12 if len(rest) > 5 else 0
    others, (grad_branch, grad_mixed, *found) = rest[:others], rest[others:]
    low = grad_result[...]
    for operand in others[6:]:
        operand.start()
    grad_branch[...] = adapter_backward(
        branch[...], squeezed[...], 0, tasks, cond, down, up, mask, low, found[:3]
    ).astype(jnp.bfloat16)
    for out in (grad_branch, *found[:3]):
        out.ship()
    copy.wait()
    grad_mixed[...] = dot_nt(grad_branch[...], whole_unit(held[0])).astype(jnp.bfloat16)
    grad_mixed.ship()
    if others:
        emit_made(place, [found[:3], others[:3], others[3:6]], found[3:5], found[-1])
        own, sent, *parts = found[5:-1]
        half = others[6].shape[-1]
        pairs = [(z, u, (z, u // 2, slice(None), slice((u & 1) * half, (u & 1) * half + half)))
                 for z in range(4) for u in range(others[6].shape[2])]
        for z, u, at in pairs:
            sent[at] = low_sum(*(part[1, z, u] for part in others[6:9]))
        sent.ship()
        for z in range(4):
            parts[z][...] = low_sum(*(part[z] for part in others[9:]))
            parts[z].ship()
        for z, u, at in pairs:
            own[at] = low_sum(*(part[0, z, u] for part in others[6:9]))


def low_sum(*parts):
    total = parts[0].astype(jnp.float32)
    for part in parts[1:]:
        total = total + part.astype(jnp.float32)
    return total.astype(jnp.bfloat16)


def first_sums(kept_cross, got_cross, other_cross, kept_made, got_made, own_out, other_y, sent_cross, *parts):
    units = own_out.shape[1]
    for z in range(4):
        parts[z][:2] = low_sum(kept_made[z], got_made[z], other_y[z, units:])
        parts[z][2:] = low_sum(own_out[z], other_y[z, :units])
        parts[z].ship()
    for z in range(4):
        sent_cross[z] = low_sum(kept_cross[z], got_cross[z], other_cross[z])


def kept_sums(kept, got, other, *rest):
    for z in range(4):
        rest[-1][z] = low_sum(kept[z], got[z], other[z])
    if len(rest) > 1:
        rest[-2][...] = low_sum(*(ref[...] for ref in rest[:4]))


def second_sums(*refs):
    total_in, kept_self, got_self, other_self, own_cross, other_cross = refs[4:10]
    gains, totals, made, sent_self, *parts = refs[10:]
    for z in range(4):
        sent_self[z] = low_sum(kept_self[z], got_self[z], other_self[z])
    sent_self.ship()
    made[:2] = low_sum(*(ref[:2] for ref in refs[:4]))
    rows = gains.shape[0]
    below = jnp.zeros((made.shape[1] - rows, made.shape[2]), jnp.float32)
    made[2] = jnp.concatenate([gains[...], below], axis=0).astype(jnp.bfloat16)
    made.ship()
    for z in range(4):
        parts[z][...] = low_sum(own_cross[z], other_cross[z])
        parts[z].ship()
    units = total_in.shape[0]
    totals[units:] = low_sum(*(ref[2:] for ref in refs[:4]))
    totals[:units] = total_in[...]


def join(place, own, other, out, rows, column):
    own, other = own.astype(jnp.float32), other.astype(jnp.float32)
    half = own.shape[-1]
    out[rows, column : column + half] = jnp.where(place[3] == 0, own, other)
    out[rows, column + half : column + 2 * half] = jnp.where(place[3] == 0, other, own)


def out_kernel(
    place, total, other, total_self, other_self,
    out_in, out_out, *outs,
):
    wide = total.shape[-1]
    units, rows, half = out_in.shape[1] // wide, out_in.shape[0], wide // 2
    for u in range(units):
        out_in[:, u * wide : (u + 1) * wide] = total[u].astype(jnp.float32) + other[u].astype(jnp.float32)
    out_in.ship()

    def pair(ref, first, u):
        return ref[first + u // 2, :, (u & 1) * half : (u & 1) * half + half]

    for u in range(units):
        join(place, pair(total, units, u), pair(other, units, u), out_out, slice(u * rows, (u + 1) * rows), 0)
    out_out.ship()
    first = units + units // 2
    columns = [(pair(total, first, u), pair(other, first, u)) for u in range(4)]
    columns += [(total_self[u], other_self[u]) for u in range(4)]
    for out in outs:
        for column in range(0, out.shape[1], wide):
            join(place, *columns.pop(0), out, slice(None), column)
        out.ship()


def third_sums(*refs):
    own_self, other_self, totals, both, *parts = refs[4:]
    for z in range(4):
        parts[z][...] = low_sum(own_self[z], other_self[z])
        parts[z].ship()
    count, half = totals.shape[0], own_self.shape[-1]
    for u in range(4):
        at = (count + u // 2, slice(None), slice((u & 1) * half, (u & 1) * half + half))
        both[at] = low_sum(*(ref[u] for ref in refs[:4]))
    both[:count] = totals[...]


def emit_made(place, made, outs, block):
    rows, wide = outs[0].shape[3], block.shape[2]
    piece, span = wide // 2, wide // 3
    block[...] = jnp.zeros_like(block)
    cond = jnp.concatenate([part[2][...] for part in made], axis=1)
    columns = cond.shape[1] // 16
    for j in range(8):
        for core in (0, 1):
            for slot in range(3):
                at = 3 * (2 * j + core) + slot
                part = made[at // 16][0][(at % 16) * rows : (at % 16 + 1) * rows]
                block[core, :, slot * span : slot * span + part.shape[1]] = part.astype(jnp.float32)
        emit_block(place, outs, 0, j, *(block[core].astype(jnp.bfloat16) for core in (0, 1)))
    for out in outs:
        out.leave(0, functools.partial(unit_part, place))
    block[...] = jnp.zeros_like(block)
    for j in range(8):
        for core in (0, 1):
            owner = 2 * j + core
            for slot in range(9):
                at = 9 * owner + slot
                row, half = (at % 48) // 2, at % 2
                part = made[at // 48][1][row * 8 : row * 8 + 8, half * piece : (half + 1) * piece]
                block[core, slot // 2 * 8 : slot // 2 * 8 + 8, slot % 2 * piece : (slot % 2 + 1) * piece] = part
            turned = pltpu.roll(cond, (cond.shape[1] - owner * columns) % cond.shape[1], 1)
            block[core, 40:48, :span] = turned[:, :span]
        emit_block(place, outs, 1, j, *(block[core].astype(jnp.bfloat16) for core in (0, 1)))
    for out in outs:
        out.leave(1, functools.partial(unit_part, place))


def cross_kernel(
    place, grad_mixed, packed, query, keyval, weights, scales, mixed, grad_branch, normed, memory, stream, gains, grad_result,
    grad_stream, grad_memory, grad_gain, *rest,
):
    outs, (held, grad_query, grad_keyval, sems) = rest[:-4], rest[-4:]
    copies = [unit_copy(packed, 4, held, sems, u) for u in range(3)]
    width = stream.shape[1]

    def beside():
        for copy in (mixed, grad_branch, normed, memory, *copies, stream, gains, grad_result):
            copy.start()

    attend_backward(
        query, keyval, keyval, (0, 0, width), weights, scales, grad_mixed,
        (grad_query, grad_keyval, grad_keyval), (0, 0, width), beside,
    )
    emit(place, outs, 3, dot_tn(mixed[...], grad_branch[...]))
    emit(place, outs, 0, dot_tn(normed[...], grad_query[...]))
    for copy in copies:
        copy.wait()
    for u in range(2):
        grad = grad_keyval[:, u * width : (u + 1) * width]
        emit(place, outs, 1 + u, dot_tn(memory[...], grad))
        if u == 0:
            grad_memory[...] = dot_nt(grad, whole_unit(held[1 + u]))
        else:
            grad_memory[...] += dot_nt(grad, whole_unit(held[1 + u]))
    grad_memory.ship()
    wide = stream[...]
    grad, gain_rows = rms_back(
        wide, rms_rate(wide), gains[1:2], dot_nt(grad_query[...], whole_unit(held[0]))
    )
    grad_stream[...] = grad_result[...] + grad
    grad_gain[...] = jnp.sum(gain_rows, axis=0, keepdims=True)


def self_kernel(
    place, grad_mixed, packed, projected, weights, scales, mixed, grad_branch, normed, tokens, gains, grad_stream,
    grad_tokens, grad_gain, *rest,
):
    outs, (held, grad_projected, total, sems) = rest[:-4], rest[-4:]
    copies = [unit_copy(packed, 0, held, sems, u) for u in range(3)]
    width = tokens.shape[1]

    def beside():
        for copy in (mixed, grad_branch, normed, *copies, tokens, gains, grad_stream):
            copy.start()

    attend_backward(
        projected, projected, projected, (0, width, 2 * width), weights, scales, grad_mixed,
        (grad_projected,) * 3, (0, width, 2 * width), beside,
    )
    emit(place, outs, 3, dot_tn(mixed[...], grad_branch[...]))
    for u in range(3):
        copies[u].wait()
        grad = grad_projected[:, u * width : (u + 1) * width]
        emit(place, outs, u, dot_tn(normed[...], grad))
        if u == 0:
            total[...] = dot_nt(grad, whole_unit(held[u]))
        else:
            total[...] += dot_nt(grad, whole_unit(held[u]))
    wide = tokens[...].astype(jnp.float32)
    grad, gain_rows = rms_back(wide, rms_rate(wide), gains[0:1], total[...])
    grad_tokens[...] = grad_stream[...] + grad
    grad_gain[...] = jnp.sum(gain_rows, axis=0, keepdims=True)


def pack_kernel(*refs):
    shards, packed = refs[:-1], refs[-1]
    rows, width = packed.shape[1:]
    unit = 0
    for shard in shards:
        for row in range(0, shard.shape[0], rows):
            for column in range(0, shard.shape[1], width):
                packed[unit] = shard[row : row + rows, column : column + width]
                unit += 1


def sum_kernel(*refs):
    refs[-1][...] = low_sum(*(ref[...] for ref in refs[:-1]))


def swap(values, axis, count, mate):
    return lax.ppermute(values, axis, [(i, mate(i)) for i in range(count)])


def place_parts():
    place = lax.axis_index("fsdp")
    return place // 4, (place // 2) % 2, place % 2


def ring_gather(block):
    z, y, core = place_parts()
    shifted = [swap(block, "fsdp", 16, lambda i, d=d: (i + 4 * d) % 16) for d in (3, 2, 1)]
    line = jnp.stack(shifted[:1] + shifted[1:] + [block])
    line = lax.dynamic_slice_in_dim(jnp.concatenate([line, line]), 3 - z, 4, 0)
    other = swap(line, "fsdp", 16, lambda i: i ^ 2)
    both = jnp.stack([jnp.where(y == 0, line, other), jnp.where(y == 0, other, line)], axis=1)
    other = swap(both, "fsdp", 16, lambda i: i ^ 1)
    whole = jnp.stack([jnp.where(core == 0, both, other), jnp.where(core == 0, other, both)], axis=2)
    return whole.reshape((16,) + block.shape)


def add_low(left, right):
    return (left.astype(jnp.float32) + right.astype(jnp.float32)).astype(jnp.bfloat16)


def core_swap(sent):
    return swap(sent, "fsdp", 16, lambda i: i ^ 1)


def y_swap(sent):
    return swap(sent, "fsdp", 16, lambda i: i ^ 2)


def x_swap(sent):
    return swap(sent, "dp", 2, lambda i: i ^ 1)


def z_swaps(parts):
    return [swap(parts[d], "fsdp", 16, lambda i, d=d: (i + 4 * d) % 16) for d in (1, 2, 3)]


def both_halves(own, other, first_x):
    return jnp.concatenate([jnp.where(first_x, own, other), jnp.where(first_x, other, own)], axis=-1)


def after(values, *others):
    return lax.optimization_barrier((values, others))[0]


def ring_step(values, bit):
    return values + swap(values, "fsdp", 16, lambda i: i ^ bit)


def gather_shards(block, ring):
    return ring_gather(block) if ring else lax.all_gather(block, "fsdp", axis=0)


def block_share(blocks):
    part = lax.psum_scatter(blocks, "fsdp", scatter_dimension=0, tiled=False)
    return lax.psum(part.astype(jnp.float32), "dp")


def share_of(grads, devices, by_rows):
    whole = grads[0][0, 0]
    count, width = whole.shape[0], whole.shape[-1]
    if by_rows:
        return block_share(whole.reshape(devices, count, -1, width))
    blocks = jnp.transpose(whole.reshape(count, devices, -1, width), (1, 0, 2, 3))
    return block_share(blocks)


def sum_shards(values, ring):
    return ring_sum(values) if ring else lax.psum(values, "fsdp")


def units_of(shard, width):
    rows, columns = shard.shape
    return jnp.transpose(shard.reshape(rows, columns // width, width), (1, 0, 2))


def joined(units):
    return jnp.transpose(units, (1, 0, 2)).reshape(units.shape[1], -1)


def view_shape(shape, view):
    return tuple(at.size for at in view if not isinstance(at, int)) + tuple(shape[len(view) :])


def call(kernel, operands, shapes, scratch, flops, raw=(), split=None, parts=None, later=(), views=None):
    split, parts, views = split or {}, parts or {}, views or {}
    scalars = operands[0].ndim == 1
    moved_in = [i for i in range(int(scalars), len(operands)) if i not in raw]
    specs = [pl.BlockSpec(memory_space=pl.ANY) for _ in operands]
    if scalars:
        specs[0] = pl.BlockSpec(memory_space=pltpu.SMEM)
    outs = [jax.ShapeDtypeStruct(shape, dtype) for shape, dtype in shapes]
    room = 20 if kernel in (sum_kernel, out_kernel) else 60
    buffers = [pltpu.VMEM(view_shape(operands[i].shape, views.get(i, ())), operands[i].dtype) for i in moved_in]
    buffers += [pltpu.VMEM(shape, dtype) for shape, dtype in shapes]
    buffers += [pltpu.SemaphoreType.DMA((split.get(i, 1),)) for i in moved_in]
    buffers += [pltpu.SemaphoreType.DMA((parts.get(k, 1),)) for k in range(len(outs))]

    def body(*refs):
        ins, results = list(refs[: len(operands)]), refs[len(operands) : len(operands) + len(outs)]
        own = refs[len(operands) + len(outs) : len(refs) - len(buffers)]
        held = refs[len(refs) - len(buffers) :]
        held, sems = held[: len(buffers) // 2], held[len(buffers) // 2 :]
        for k, i in enumerate(moved_in):
            source = ins[i].at[views[i]] if i in views else ins[i]
            ins[i] = Fetched(source, held[k], sems[k], split.get(i, 1))
            if i not in later:
                ins[i].start()
        results = [
            Shipped(target, *rest) for target, *rest in zip(results, held[len(moved_in) :], sems[len(moved_in) :])
        ]
        kernel(*ins, *results, *own)
        for operand in ins:
            ready(operand)
        for result in results:
            result.settle()

    moved = sum(math.prod(shape) * jnp.dtype(dtype).itemsize for shape, dtype in shapes)
    moved += sum(operand.size * operand.dtype.itemsize for operand in operands)
    return pl.pallas_call(
        body,
        out_shape=outs,
        in_specs=specs,
        out_specs=[pl.BlockSpec(memory_space=pl.ANY) for _ in outs],
        scratch_shapes=list(scratch) + buffers,
        compiler_params=pltpu.CompilerParams(vmem_limit_bytes=room * 1024 * 1024),
        cost_estimate=pl.CostEstimate(flops=flops, bytes_accessed=moved, transcendentals=0),
    )(*operands)


def per_device(
    devices,
    ring,
    tokens,
    memory,
    out_grad,
    target_len,
    source_len,
    task_ids,
    norm_gains,
    self_qkv,
    self_out,
    cross_query,
    cross_keyval,
    cross_out,
    feed_in,
    feed_out,
    task_table,
    hyper_in,
    maker_down,
    maker_up,
    maker_norm,
):
    width = tokens.shape[1]
    tasks = task_table.shape[0]
    embed = hyper_in.shape[0]
    table_width = task_table.shape[1]
    hyper_width = hyper_in.shape[1]
    gain_width = norm_gains.shape[1]
    down_span = maker_down.shape[1]
    norm_span = maker_norm.shape[1]
    bottleneck = down_span * devices // (3 * width)
    down_rows = 3 * width // devices
    unit = width // devices
    ff_units = feed_in.shape[1] // width
    small = jnp.concatenate(
        [
            jnp.pad(task_table.T, ((0, 0), (0, 128 - tasks))),
            jnp.pad(hyper_in.T, ((0, 0), (0, 128 - embed))),
            jnp.pad(norm_gains, ((0, 0), (0, 128 - gain_width))),
            jnp.zeros((-(table_width + hyper_width + 3) % 16, 128), jnp.bfloat16),
        ]
    )
    small = gather_shards(small, ring)
    whole_table = small[:, :table_width, :tasks].reshape(-1, tasks).T
    whole_hyper = small[:, table_width : table_width + hyper_width, :embed].reshape(-1, embed).T
    first = table_width + hyper_width
    whole_gains = jnp.transpose(small[:, first : first + 3, :gain_width], (1, 0, 2)).reshape(3, width)
    layer = [self_qkv, self_out, cross_query, cross_keyval, cross_out, feed_in]
    if ring:
        shape = ((8 + 2 * ff_units, unit, width), jnp.bfloat16)
        (packed,) = call(pack_kernel, (*layer, feed_out), [shape], [], 1)
        packed = packed.reshape(-1, width)
    else:
        layer = [units_of(w, width) for w in layer] + [feed_out.reshape(ff_units, unit, width)]
        packed = jnp.concatenate([w.reshape(-1, width) for w in layer])
    packed = lax.all_gather(packed, "fsdp", axis=0).reshape(devices, -1, unit, width)
    if not ring:
        first = jnp.transpose(packed[:, : 8 + ff_units], (1, 0, 2, 3)).reshape(-1, width, width)
        last = packed[:, 8 + ff_units :].reshape(-1, width, width)
        packed = jnp.concatenate([first, last])[None]
    pre_hidden = matmul(whole_table, whole_hyper)
    hidden = jax.nn.silu(pre_hidden).astype(jnp.bfloat16)
    own_down = matmul(hidden, maker_down).astype(jnp.bfloat16)
    own_up = matmul(hidden, maker_up).astype(jnp.bfloat16)
    own_norm = matmul(hidden, maker_norm).astype(jnp.bfloat16)
    span = tasks * bottleneck
    own_down = jnp.transpose(own_down.reshape(tasks, down_rows, bottleneck), (1, 2, 0)).reshape(-1, span)
    if ring:
        third, piece = width // 3, width // 2
        own_down = jnp.pad(own_down.reshape(3, unit, span), ((0, 0), (0, 0), (0, third - span)))
        own_down = jnp.transpose(own_down, (1, 0, 2)).reshape(unit, width)
        own_up = jnp.pad(own_up, ((0, 0), (0, 10 * piece - down_span))).reshape(tasks, 5, width)
        own_up = jnp.transpose(own_up, (1, 0, 2)).reshape(5 * tasks, width)
        own_norm = jnp.pad(own_norm, ((0, 0), (0, width - norm_span)))
        made = jnp.concatenate([own_down, own_up, own_norm])
        first_x = lax.axis_index("dp") == 0
        made = ring_gather(jnp.where(first_x, made[:, : width // 2], made[:, width // 2 :]))
        made = both_halves(made, x_swap(made), first_x)
        made_down = made[:, :unit].reshape(devices, unit, 3, third)[..., :span]
        made_down = jnp.transpose(made_down, (0, 2, 1, 3)).reshape(3, width, span)
        made_up = made[:, unit : unit + 5 * tasks].reshape(devices, 5, tasks, 2, piece)
        made_up = jnp.transpose(made_up, (0, 1, 3, 2, 4)).reshape(devices, 10, tasks, piece)[:, :9]
        made_up = jnp.transpose(made_up.reshape(3, bottleneck, 2, tasks, piece), (0, 1, 3, 2, 4))
        made_up = made_up.reshape(3, span, width)
        made_cond = made[:, unit + 5 * tasks :, :norm_span]
    else:
        made_down = lax.all_gather(own_down, "fsdp", axis=0, tiled=True).reshape(3, width, span)
        made_up = lax.all_gather(own_up, "fsdp", axis=1, tiled=True).reshape(tasks, 3, bottleneck, width)
        made_up = jnp.transpose(made_up, (1, 2, 0, 3)).reshape(3, span, width)
        made_cond = lax.all_gather(own_norm, "fsdp", axis=0)
    made_cond = jnp.transpose(made_cond, (1, 0, 2)).reshape(tasks, 3, width)
    made_cond = jnp.pad(jnp.transpose(made_cond, (1, 0, 2)), ((0, 0), (0, 128 - tasks), (0, 0)))
    tok_seg = segment_rows(target_len[0], tokens.shape[0])
    mem_seg = segment_rows(source_len[0], memory.shape[0])
    sequences = jnp.arange(target_len.shape[1], dtype=jnp.int32)
    row_task = jnp.sum(
        jnp.where(tok_seg[:, None] == sequences[None, :], task_ids[0][None, :], 0), axis=1
    )
    onehot = (row_task[:, None] == jnp.arange(128, dtype=jnp.int32)[None, :]).astype(jnp.bfloat16)
    mask = jnp.tile(onehot[:, :tasks], (1, bottleneck))
    places = jnp.arange(tokens.shape[0], dtype=jnp.int32)
    self_allowed = (tok_seg[:, None] == tok_seg[None, :]) & (places[:, None] <= places[None, :])
    cross_allowed = mem_seg[:, None] == tok_seg[None, :]
    self_cap = jnp.where(self_allowed, -masked_score * 1e20, masked_score).astype(jnp.float32)
    cross_cap = jnp.where(cross_allowed, -masked_score * 1e20, masked_score).astype(jnp.float32)
    gains = jnp.pad(whole_gains.astype(jnp.float32), ((0, 5), (0, 0)))
    place = lax.axis_index("fsdp")
    here = jnp.stack([place // 4, (place // 2) % 2, place % 2, lax.axis_index("dp")]).astype(jnp.int32)
    adapters = (onehot, made_cond, made_down, made_up, mask)
    rows, memory_rows = tokens.shape[0], memory.shape[0]
    pairs = width // 128
    low, full = jnp.bfloat16, jnp.float32
    held_unit = packed.shape[:1] + packed.shape[2:]

    def held(count):
        return pltpu.VMEM((count,) + held_unit, low)

    def grad_shapes(count, by_x=False):
        if ring and by_x:
            return [((2, 2, 4, count, unit, width // 2), low)] * 2
        if ring:
            return [((2, 4, count, unit, width), low)] * 2
        return [((1, 1, count, width, width), low)]

    made_shapes = [((width, span), low), ((span, width), full), ((tasks, width), full)]
    gain_shape = [((1, width), full)]
    busy = 1700000000
    scale_shape = ((pairs, 1, 2 * rows), full)
    float_rows, low_rows = ((rows, width), full), ((rows, width), low)
    found = call(
        attention_kernel,
        (tokens, gains, packed, self_cap) + adapters + (memory, cross_cap),
        [low_rows, ((rows, 3 * width), low), ((pairs, rows, 2 * rows), low), scale_shape, low_rows, float_rows]
        + [((rows, span), full), float_rows, low_rows, low_rows, ((memory_rows, 2 * width), low)]
        + [((pairs, memory_rows, 2 * rows), low), scale_shape, low_rows, float_rows]
        + [((rows, span), full), float_rows],
        [held(8), pltpu.SemaphoreType.DMA((8,))],
        37 * busy,
        raw=(2,),
        parts={2: pairs, 11: pairs},
        later=(4, 5, 6, 7, 8, 9, 10),
    )
    normed1, projected, weights1, scales1, mixed1, branch1, squeezed1, stream1, *found = found
    normed2, query2, keyval2, weights2, scales2, mixed2, branch2, squeezed2, stream2 = found
    held_out = (packed.shape[0], ff_units) + packed.shape[2:]
    sets = 2 if ring else 1
    result, grad_stream, *found = call(
        feed_kernel,
        (here, stream2, gains, packed) + adapters + (out_grad,),
        [low_rows, float_rows] + made_shapes + gain_shape + grad_shapes(ff_units, True) + grad_shapes(ff_units),
        [
            held(ff_units),
            pltpu.VMEM(held_out, low),
            pltpu.VMEM((rows, width), low),
            pltpu.VMEM((ff_units, rows, width), full),
            pltpu.VMEM((ff_units, rows, width), low),
            pltpu.VMEM((rows, width), low),
            pltpu.VMEM((rows, width), full),
            pltpu.SemaphoreType.DMA((2 * ff_units,)),
        ],
        36 * busy,
        raw=(3,),
        parts={6 + k: (2 if k < sets else 1) * ff_units for k in range(2 * sets)},
        later=(4, 5, 6, 7, 8, 9),
        views=dict.fromkeys((5, 6, 7), (pl.ds(2, 1),)),
    )
    made_three, grad_gain_three, grads_out, grads_in = found[:3], found[3], found[4 : 4 + sets], found[4 + sets :]

    def branch_back(index, unit_at, grad_result, branch, squeezed, others, shapes):
        return call(
            functools.partial(branch_kernel, unit_at),
            (here, grad_result, packed, squeezed, branch) + adapters + others,
            [low_rows] * 2 + made_shapes + shapes,
            [pltpu.VMEM((2, unit, width), full)] * int(bool(others)) + [held(1), pltpu.SemaphoreType.DMA((1,))],
            30 * busy,
            raw=(2,),
            parts={5: 2, 6: 2} if others else {},
            later=tuple(range(16, 22)) if others else (),
            views=dict.fromkeys((6, 7, 8), (pl.ds(index, 1),))
            | (dict.fromkeys((16, 17, 19, 20), (0,)) if others else {}),
        )

    if ring:
        got_out, got_in = core_swap(grads_out[0]), core_swap(grads_in[0])
    grad_branch, grad_mixed, *made_two = branch_back(1, 7, grad_stream, branch2, squeezed2, (), [])
    if ring:
        got_out, got_in = after((got_out, got_in), grad_mixed)
        sent_out, sent_in = (add_low(kept[1], got[1]) for (_, kept), got in ((grads_out, got_out), (grads_in, got_in)))
        other_out, other_in = x_swap(sent_out), y_swap(sent_in)
        grad_mixed = after(grad_mixed, sent_out, sent_in)
    grad_stream, grad_memory, grad_gain_two, *grads_cross = call(
        cross_kernel,
        (here, grad_mixed, packed, query2, keyval2, weights2, scales2, mixed2, grad_branch, normed2)
        + (memory, stream1, gains, grad_stream),
        [float_rows, ((memory_rows, width), full)] + gain_shape + grad_shapes(4, True),
        [
            held(3),
            pltpu.VMEM((rows, width), low),
            pltpu.VMEM((memory_rows, 2 * width), low),
            pltpu.SemaphoreType.DMA((3,)),
        ],
        24 * busy,
        raw=(2,),
        split={5: pairs},
        parts={3: 4, 4: 4},
        later=(5,) + tuple(range(7, 14)),
    )
    others, shapes = (), []
    if ring:
        got_cross = core_swap(grads_cross[0])
        others = (*made_two, *made_three, grads_out[1], got_out, other_out, grads_in[1], got_in, other_in)
        shapes = [((2, 4, 2, unit, width), low)] * 2
        shapes += [((4, ff_units // 2, unit, width), low)] * 2 + [((ff_units, unit, width), low)] * 4
    grad_branch, grad_mixed, *made_one = branch_back(0, 3, grad_stream, branch1, squeezed1, others, shapes)
    if ring:
        sent_made, kept_made, own_out, sent_out, *parts_in = made_one[3:]
        got_made = core_swap(sent_made)
        got_cross = after(got_cross, grad_mixed)
        sent_cross = add_low(grads_cross[1][1], got_cross[1])
        other_cross = x_swap(sent_cross)
        far_in = z_swaps(after(parts_in, sent_cross))
        sent_made = add_low(kept_made[1], after(got_made, sent_cross)[1])
        other_y = y_swap(jnp.concatenate([sent_out, sent_made], axis=1))
        grad_mixed = after(grad_mixed, sent_made)
    grad_tokens, grad_gain_one, *grads_self = call(
        self_kernel,
        (here, grad_mixed, packed, projected, weights1, scales1, mixed1, grad_branch, normed1, tokens, gains)
        + (grad_stream,),
        [float_rows] + gain_shape + grad_shapes(4, True),
        [
            held(3),
            pltpu.VMEM((rows, 3 * width), low),
            pltpu.VMEM((rows, width), full),
            pltpu.SemaphoreType.DMA((3,)),
        ],
        busy,
        raw=(2,),
        split={4: pairs},
        parts={2: 4, 3: 4},
        later=(4,) + tuple(range(6, 12)),
    )

    def own_made(share):
        own_down = share[0].reshape(unit, 3, third)[:, :, :span]
        own_down = jnp.transpose(own_down, (1, 0, 2)).reshape(down_rows, bottleneck, tasks)
        own_down = jnp.transpose(own_down, (2, 0, 1)).reshape(tasks, down_span)
        own_up = share[1, : 5 * tasks].reshape(5, tasks, width)
        own_up = jnp.transpose(own_up, (1, 0, 2)).reshape(tasks, 5 * width)[:, :down_span]
        return own_down, own_up, share[1, 5 * tasks :, :norm_span]

    def hidden_of(own_down, own_up, own_norm):
        return (
            dot_nt(own_down.astype(jnp.bfloat16), maker_down)
            + dot_nt(own_up.astype(jnp.bfloat16), maker_up)
            + dot_nt(own_norm.astype(jnp.bfloat16), maker_norm)
        )

    def hidden_outs(*made):
        return [dot_tn(hidden, own.astype(jnp.bfloat16)) for own in made]

    grad_gains = jnp.concatenate([grad_gain_one, grad_gain_two, grad_gain_three])
    if ring:
        got_self = core_swap(grads_self[0])
        flight = (far_in, other_cross, other_y)
        far_in, other_cross, other_y = after(flight, grad_gain_one)
        halves_y, column_half = ((4, 4, unit, width // 2), low), ((4, unit, width // 2), low)
        whole_part = ((4, unit, width), low)
        sent_cross, *parts = call(
            first_sums,
            (grads_cross[1], got_cross, other_cross, kept_made, got_made, own_out, other_y),
            [halves_y] + [whole_part] * 4,
            [],
            100 * busy,
            views={0: (0, 1), 1: (0, 1), 2: (1,), 3: (0,), 4: (0,)},
        )
        sent_self = add_low(grads_self[1][1], after(got_self, sent_cross)[1])
        other_self = x_swap(sent_self)
        parts, sent_cross = after((parts, sent_cross), sent_self)
        far = z_swaps(parts)
        kept_cross, far_in = after((grads_cross[1], far_in), sent_self)
        total_in, own_cross = call(
            kept_sums,
            (kept_cross, got_cross, other_cross, parts_in[0], *far_in),
            [whole_part, halves_y],
            [],
            100 * busy,
            views={0: (0, 0), 1: (0, 0), 2: (0,)},
        )
        other_cross = y_swap(sent_cross)
        totals, total_made, sent_self, *parts = call(
            second_sums,
            (parts[0], *far, total_in, grads_self[1], got_self, other_self, own_cross, other_cross)
            + (grad_gains,),
            [((6, unit, width), low), ((3, unit, width), low), halves_y] + [column_half] * 4,
            [],
            5 * busy,
            views={5: (0, 1), 6: (0, 1), 7: (1,)},
        )
        other_made, far = x_swap(total_made), z_swaps(parts)
        (own_self,) = call(
            kept_sums,
            (after(grads_self[1], other_made), got_self, other_self),
            [halves_y],
            [],
            100 * busy,
            views={0: (0, 0), 1: (0, 0), 2: (0,)},
        )
        other_self = y_swap(sent_self)
        share_made = total_made.astype(jnp.float32) + other_made.astype(jnp.float32)
        own_down, own_up, own_norm = own_made(share_made[:2])
        sums = jnp.concatenate(
            [hidden_of(own_down, own_up, own_norm), share_made[2, :3].reshape(-1, 128)]
        )
        sums = ring_step(sums, 1)
        made_outs = hidden_outs(own_down, own_up, own_norm)
        totals, *parts = call(
            third_sums,
            (parts[0], *far, own_self, other_self, after(totals, made_outs)),
            [((8, unit, width), low)] + [column_half] * 4,
            [],
            5 * busy,
        )
        other_totals, far = x_swap(totals), z_swaps(parts)
        sums = ring_step(after(sums, totals), 2)
        for part in z_swaps([sums] * 4):
            sums = sums + part
        far = after(far, sums)
        total_self = call(sum_kernel, (parts[0], *far), [column_half], [], 5 * busy)[0]
        other_self = x_swap(total_self)
        sums = after(sums, total_self)
        shapes = [((unit, ff_units * width), full), ((ff_units * unit, width), full)]
        shapes += [((unit, count * width), full) for count in (1, 2, 1, 3, 1)]
        out_feed_in, out_feed_out, out_query, out_keyval, out_cross_out, out_qkv, out_self_out = call(
            out_kernel, (here, totals, other_totals, total_self, other_self), shapes, [], busy
        )
    else:
        share_in, share_out, share_cross, share_self = (
            share_of(grads, devices, grads is grads_out)
            for grads in (grads_in, grads_out, grads_cross, grads_self)
        )
        made = (made_one, made_two, made_three)
        grad_down = jnp.concatenate([part[0] for part in made]).reshape(devices, -1)
        grad_up = jnp.stack([part[1] for part in made]).reshape(3, bottleneck, tasks, width)
        grad_up = jnp.transpose(grad_up, (2, 0, 1, 3)).reshape(tasks, devices, down_span)
        grad_norm = jnp.concatenate([part[2] for part in made], axis=1)
        grad_norm = grad_norm.reshape(tasks, devices, norm_span)
        blocks = [grad_down.astype(jnp.bfloat16)] + [
            jnp.transpose(part.astype(jnp.bfloat16), (1, 0, 2)).reshape(devices, -1)
            for part in (grad_up, grad_norm)
        ]
        out_feed_in, out_feed_out = joined(share_in), share_out.reshape(-1, width)
        out_query, out_keyval, out_cross_out = share_cross[0], joined(share_cross[1:3]), share_cross[3]
        out_qkv, out_self_out = joined(share_self[:3]), share_self[3]
        share_made = block_share(jnp.concatenate(blocks, axis=1))
        sizes = (0, tasks * down_span, 2 * tasks * down_span, share_made.shape[0])
        own_down, own_up, own_norm = (share_made[a:b] for a, b in zip(sizes, sizes[1:]))
        own_down = jnp.transpose(own_down.reshape(down_rows, bottleneck, tasks), (2, 0, 1))
        own_down, own_up = own_down.reshape(tasks, down_span), own_up.reshape(tasks, down_span)
        own_norm = own_norm.reshape(tasks, norm_span)
        sums = jnp.concatenate([hidden_of(own_down, own_up, own_norm), lax.psum(grad_gains, "dp").reshape(-1, 128)])
        sums = lax.psum(sums, "fsdp")
        made_outs = hidden_outs(own_down, own_up, own_norm)
    grad_hidden = sums[:tasks]
    out_gains = lax.dynamic_slice_in_dim(
        sums[tasks:].reshape(3, width), place * gain_width, gain_width, 1
    )
    _, silu_pull = jax.vjp(jax.nn.silu, pre_hidden)
    grad_pre_hidden = silu_pull(grad_hidden)[0]
    own_hyper = lax.dynamic_slice_in_dim(whole_hyper, place * table_width, table_width, 0)
    out_table = exact_cols(grad_pre_hidden, own_hyper.astype(jnp.float32))
    own_pre = lax.dynamic_slice_in_dim(grad_pre_hidden, place * hyper_width, hyper_width, 1)
    out_hyper = exact_rows(whole_table.astype(jnp.float32), own_pre)
    out_down, out_up, out_norm = made_outs
    return (
        result.astype(jnp.bfloat16),
        grad_tokens,
        grad_memory,
        out_gains,
        out_qkv,
        out_self_out,
        out_query,
        out_keyval,
        out_cross_out,
        out_feed_in,
        out_feed_out,
        out_table,
        out_hyper,
        out_down,
        out_up,
        out_norm,
    )


def solution(mesh):
    placed = (
        P(("fsdp", "dp"), None),
        P(("fsdp", "dp"), None),
        P(("fsdp", "dp"), None),
        P(("fsdp", "dp"), None),
        P(("fsdp", "dp"), None),
        P(("fsdp", "dp"), None),
        P(None, "fsdp"),
        P("fsdp", None),
        P("fsdp", None),
        P("fsdp", None),
        P("fsdp", None),
        P("fsdp", None),
        P("fsdp", None),
        P("fsdp", None),
        P(None, "fsdp"),
        P(None, "fsdp"),
        P(None, "fsdp"),
        P(None, "fsdp"),
        P(None, "fsdp"),
    )
    devices = mesh.shape["fsdp"]
    ring = devices == 16 and mesh.shape["dp"] == 2
    return jax.shard_map(
        functools.partial(per_device, devices, ring),
        mesh=mesh,
        in_specs=placed,
        out_specs=(
            P(("fsdp", "dp"), None),
            P(("fsdp", "dp"), None),
            P(("fsdp", "dp"), None),
            P(None, "fsdp"),
            P("fsdp", None),
            P("fsdp", None),
            P("fsdp", None),
            P("fsdp", None),
            P("fsdp", None),
            P("fsdp", None),
            P("fsdp", None),
            P(None, "fsdp"),
            P(None, "fsdp"),
            P(None, "fsdp"),
            P(None, "fsdp"),
            P(None, "fsdp"),
        ),
        check_vma=False,
    )
```
